32 devices in a mesh: dp: 8 (over y, x, core), expert: 4 (over z).
Axes of the slice: x: 2, y: 2, z: 4, core: 2. Of those that a mesh axis runs over, the one named last changes fastest.
Arguments:
- context: bfloat16 [4096, 4096], P('dp'), may hold values from -6 to 6
- out_weight: bfloat16 [4096, 4096], P('dp', 'expert'), may hold values from -0.09375 to 0.09375
- residual: bfloat16 [4096, 4096], P('dp', 'expert'), may hold values from -6 to 6
- gate_weight: bfloat16 [4, 4096, 8192], P('expert', None, 'dp'), may hold values from -0.09375 to 0.09375
- up_weight: bfloat16 [4, 4096, 8192], P('expert', None, 'dp'), may hold values from -0.09375 to 0.09375
- down_weight: bfloat16 [4, 8192, 4096], P('expert', 'dp'), may hold values from -0.0625 to 0.0625
- gate_values: float32 [4, 512], P('expert'), may hold values from 0.2 to 1
- chosen_blocks: int32 [4, 4], replicated, may hold values from 0 to 31, as said below
- block_counts: int32 [4], replicated, may hold values from 1 to 4, as said below
Outputs:
- mixed: bfloat16 [4096, 4096], P('dp', 'expert')
The draws below stay inside these ranges and needn't reach their ends.
Inputs may be any that keep to these rules, and one draw needn't show every extreme that they name: `chosen_blocks`: within one expert the 4 block numbers are distinct; slots from block_counts on are unused but hold valid block numbers. `block_counts`: some expert uses all 4 slots.
All inputs are finite; a program needn't handle non-finite values.
Results may differ from the reference program's by a relative error of at most 0.008.
Values may be sent and summed in bfloat16 or wider, within the bound.
No kernel may reach another device: no remote copies, remote signals or barrier semaphores. Data moves between devices by JAX's collectives and lax.ppermute only.
A program may use at most 128 MiB of HBM per device.

```python
import jax
import jax.numpy as jnp
from jax import lax

D = 4096
FF = 8192
BLK = 128
CAP = 4
EXPERTS = 4
NBLK = 32
TOKENS = 4096
N_DP = 8


def draw_chosen_blocks(key, part):
    first, second, third = jax.random.split(key, 3)
    keys = jax.random.split(first, EXPERTS)
    orders = jax.vmap(lambda single: jax.random.permutation(single, NBLK))(keys)[:, :CAP]
    middle = 1 + jax.random.permutation(second, NBLK - 2)[:CAP - 2]
    ends = jnp.concatenate([jnp.array([0, NBLK - 1], jnp.int32), middle.astype(jnp.int32)])
    target = jax.random.randint(third, (), 0, EXPERTS)
    rows = jnp.where(jnp.arange(EXPERTS)[:, None] == target, ends[None, :], orders)
    return rows.astype(jnp.int32)


def draw_block_counts(key, part):
    first, second, third = jax.random.split(key, 3)
    heavy = jax.random.randint(first, (EXPERTS,), 0, 4) == 0
    light = jnp.minimum(jax.random.randint(second, (EXPERTS,), 1, 3), CAP)
    counts = jnp.where(heavy, CAP, light)
    target = jax.random.randint(third, (), 0, EXPERTS)
    counts = jnp.where(jnp.arange(EXPERTS) == target, CAP, counts)
    counts = jnp.where(jnp.arange(EXPERTS) == (target + 1) % EXPERTS, 1, counts)
    return counts.astype(jnp.int32)


def shard_levels(own_key, extent, cuts, low, top_value):
    def one(position, blocks):
        draws = jax.random.uniform(jax.random.fold_in(jax.random.fold_in(own_key, 6), position), (blocks,), jnp.float32, low / len(cuts), top_value / len(cuts))
        return jnp.repeat(jnp.exp(draws), extent[position] // blocks).reshape((-1,) + (1,) * (len(extent) - position - 1))

    level = one(*cuts[0])
    for cut in cuts[1:]:
        level = level * one(*cut)
    return level


def noise(own_key, extent, spread, reach, cuts=(), kind=jnp.bfloat16):
    drawn = jax.random.normal(own_key, extent, jnp.float32) * spread
    if len(cuts) > 0:
        drawn = shard_levels(own_key, extent, cuts, -0.22, 0.18) * drawn
    return jnp.clip(drawn, min=-reach, max=reach).astype(kind)


def setup_inputs(seed: int = 0) -> dict:
    seeds = jax.random.split(jax.random.key(seed), 10)
    return {
        "context": noise(seeds[0], (TOKENS, D), 1.0, 6.0, ((0, 8),)),
        "out_weight": noise(seeds[1], (D, D), D ** -0.5, 0.09375, ((0, 8), (1, 4))),
        "residual": noise(seeds[2], (TOKENS, D), 1.0, 6.0, ((0, 8), (1, 4))),
        "gate_weight": noise(seeds[3], (EXPERTS, D, FF), D ** -0.5, 0.09375, ((0, 4), (2, 8))),
        "up_weight": noise(seeds[4], (EXPERTS, D, FF), D ** -0.5, 0.09375, ((0, 4), (2, 8))),
        "down_weight": noise(seeds[5], (EXPERTS, FF, D), FF ** -0.5, 0.0625, ((0, 4), (1, 8))),
        "gate_values": jnp.clip(0.2 + 0.8 * jax.random.uniform(seeds[6], (EXPERTS, CAP * BLK), jnp.float32) ** shard_levels(seeds[6], (EXPERTS, CAP * BLK), ((0, 4),), -0.2, 0.2), 0.2, 1.0),
        "chosen_blocks": draw_chosen_blocks(jax.random.fold_in(seeds[9], 71), 0),
        "block_counts": draw_block_counts(jax.random.fold_in(seeds[9], 71), 0),
    }


def reference(context, out_weight, residual, gate_weight, up_weight, down_weight, gate_values, chosen_blocks, block_counts):
    attended = (residual.astype(jnp.float32) + jnp.dot(context, out_weight, preferred_element_type=jnp.float32)).astype(jnp.bfloat16)
    blocks = attended.reshape(NBLK, BLK, D)
    width = FF // N_DP

    def one_expert(inputs):
        w_gate, w_up, w_down, gate_row, block_list, count = inputs
        picked = blocks[block_list].reshape(CAP * BLK, D)
        gate = jnp.dot(picked, w_gate, preferred_element_type=jnp.float32)
        upper = jnp.dot(picked, w_up, preferred_element_type=jnp.float32)
        hidden = (jax.nn.silu(gate) * upper).astype(jnp.bfloat16)
        live = (jnp.arange(CAP * BLK) // BLK) < count
        scale = jnp.where(live, gate_row, jnp.zeros_like(gate_row))[:, None]
        total = jnp.zeros((CAP * BLK, D), jnp.float32)
        for slice_index in range(N_DP):
            part = jnp.dot(hidden[:, slice_index * width:(slice_index + 1) * width], w_down[slice_index * width:(slice_index + 1) * width], preferred_element_type=jnp.float32)
            rounded = lax.optimization_barrier((part * scale).astype(jnp.bfloat16))
            total = total + rounded.astype(jnp.float32)
        return total.astype(jnp.bfloat16)

    outputs = lax.map(one_expert, (gate_weight, up_weight, down_weight, gate_values, chosen_blocks, block_counts))
    summed = attended.astype(jnp.float32).reshape(NBLK, BLK, D)
    summed = summed.at[chosen_blocks.reshape(-1)].add(outputs.reshape(EXPERTS * CAP, BLK, D).astype(jnp.float32))
    return summed.reshape(TOKENS, D).astype(jnp.bfloat16)
```

```python
import jax
import jax.numpy as jnp
from jax import lax
from jax.experimental import pallas as pl
from jax.experimental.pallas import tpu as pltpu
from jax.sharding import PartitionSpec as P

BLK = 128
CAP = 4
GROUPS = 2
VMEM_LIMIT = 48 * 1024 * 1024


def bit_orders(n_bits):
    forward = list(range(1, n_bits + 1))
    return forward, forward[::-1]


def step_pairs(n_dp, step):
    orders = bit_orders(n_dp.bit_length() - 2)
    return [(i, i ^ (1 << orders[i & 1][step])) for i in range(n_dp)]


def pair_pairs(n_dp):
    return [(i, i ^ 1) for i in range(n_dp)]


def masks_of(n_bits, side):
    order = bit_orders(n_bits)[side]
    return [
        sum(1 << (order[t] - 1) for t in range(n_bits) if (r >> t) & 1) for r in range(1 << n_bits)
    ]


def bit_reversed(n_bits):
    return [
        sum(1 << (n_bits - 1 - t) for t in range(n_bits) if (r >> t) & 1)
        for r in range(1 << n_bits)
    ]


def scatter_sum(buf, n_dp, n_bits):
    for step in range(n_bits - 1, -1, -1):
        half = 1 << step
        got = lax.ppermute(buf[half:], "dp", step_pairs(n_dp, step))
        buf = (buf[:half].astype(jnp.float32) + got.astype(jnp.float32)).astype(buf.dtype)
    return buf[0]


def gather_all(piece, n_dp, n_bits):
    buf = piece[None]
    for step in range(n_bits):
        got = lax.ppermute(buf, "dp", step_pairs(n_dp, step))
        buf = jnp.concatenate([buf, got], axis=0)
    return buf


def swap_planes(parts, n_expert):
    out = [parts[0]]
    for k in range(1, n_expert):
        pairs = [(i, (i + k) % n_expert) for i in range(n_expert)]
        out.append(lax.ppermute(parts[k], "expert", pairs))
    return jnp.stack(out)


def pick_kernel(idx_ref, att_ref, out_ref):
    for i in range(out_ref.shape[0]):
        idx = idx_ref[i]
        value = att_ref[jnp.maximum(idx, 0)]
        out_ref[i] = jnp.where(idx >= 0, value, jnp.zeros_like(value))


def pick(idx, attended):
    return pl.pallas_call(
        pick_kernel,
        out_shape=jax.ShapeDtypeStruct((idx.shape[0],) + attended.shape[1:], attended.dtype),
        in_specs=[
            pl.BlockSpec(memory_space=pltpu.SMEM),
            pl.BlockSpec(memory_space=pltpu.VMEM),
        ],
        out_specs=pl.BlockSpec(memory_space=pltpu.VMEM),
        compiler_params=pltpu.CompilerParams(vmem_limit_bytes=VMEM_LIMIT),
        name="pick_blocks",
    )(idx, attended)


def finish_kernel(idx_ref, att_ref, *refs):
    pieces, out_ref, acc = refs[:-2], refs[-2], refs[-1]
    acc[...] = att_ref[...].astype(jnp.float32)
    at = 0
    for piece in pieces:
        for i in range(piece.shape[0]):
            idx = idx_ref[at]
            at += 1

            @pl.when(idx >= 0)
            def _():
                acc[idx] = acc[idx] + piece[i].astype(jnp.float32)

    out_ref[...] = acc[...].astype(out_ref.dtype)


def finish(idx, attended, pieces):
    return pl.pallas_call(
        finish_kernel,
        out_shape=jax.ShapeDtypeStruct(attended.shape, attended.dtype),
        in_specs=[pl.BlockSpec(memory_space=pltpu.SMEM)]
        + [pl.BlockSpec(memory_space=pltpu.VMEM)] * (1 + len(pieces)),
        out_specs=pl.BlockSpec(memory_space=pltpu.VMEM),
        scratch_shapes=[pltpu.VMEM(attended.shape, jnp.float32)],
        compiler_params=pltpu.CompilerParams(vmem_limit_bytes=VMEM_LIMIT),
        name="add_expert_rows",
    )(idx, attended, *pieces)


def mlp_kernel(n_k, kidx, nidx, x_ref, wg_ref, wu_ref, wd_ref, scale_ref, out_ref, gate, up, hidden):
    step = pl.program_id(0)
    rows = gate.shape[0]

    @pl.when(step < n_k)
    def _():
        x = x_ref[...].reshape(rows, x_ref.shape[-1])
        g = jnp.dot(x, wg_ref[...], preferred_element_type=jnp.float32)
        u = jnp.dot(x, wu_ref[...], preferred_element_type=jnp.float32)

        @pl.when(step == 0)
        def _():
            gate[...] = g
            up[...] = u

        @pl.when(step > 0)
        def _():
            gate[...] += g
            up[...] += u

    @pl.when(step == n_k - 1)
    def _():
        v = gate[...]
        hidden[...] = (v / (1.0 + jnp.exp(-v)) * up[...]).astype(jnp.bfloat16)

    @pl.when(step >= n_k)
    def _():
        part = jnp.dot(hidden[...], wd_ref[...], preferred_element_type=jnp.float32)
        out_ref[...] = (part * scale_ref[...]).astype(out_ref.dtype).reshape(out_ref.shape)


def mlp(x, kidx, nidx, w_gate, w_up, w_down, scale):
    n_side, n_rel, n_z, rows, width = x.shape
    n_k = n_side * n_z
    ff = w_gate.shape[1]
    total = n_rel * rows

    def x_map(i, kidx, nidx):
        k = jnp.minimum(i, n_k - 1)
        return k // n_z, 0, k % n_z, 0, 0

    def k_map(i, kidx, nidx):
        return kidx[jnp.minimum(i, n_k - 1)], 0

    def n_map(i, kidx, nidx):
        return 0, nidx[jnp.maximum(i - n_k, 0)]

    def o_map(i, kidx, nidx):
        n = jnp.maximum(i - n_k, 0)
        return n // n_z, 0, n % n_z, 0, 0

    return pl.pallas_call(
        lambda *refs: mlp_kernel(n_k, *refs),
        out_shape=jax.ShapeDtypeStruct(x.shape, jnp.bfloat16),
        grid_spec=pltpu.PrefetchScalarGridSpec(
            num_scalar_prefetch=2,
            grid=(2 * n_k,),
            in_specs=[
                pl.BlockSpec((1, n_rel, 1, rows, width), x_map),
                pl.BlockSpec((width, ff), k_map),
                pl.BlockSpec((width, ff), k_map),
                pl.BlockSpec((ff, width), n_map),
                pl.BlockSpec((total, 1), lambda i, kidx, nidx: (0, 0)),
            ],
            out_specs=pl.BlockSpec((1, n_rel, 1, rows, width), o_map),
            scratch_shapes=[
                pltpu.VMEM((total, ff), jnp.float32),
                pltpu.VMEM((total, ff), jnp.float32),
                pltpu.VMEM((total, ff), jnp.bfloat16),
            ],
        ),
        compiler_params=pltpu.CompilerParams(vmem_limit_bytes=VMEM_LIMIT),
        cost_estimate=pl.CostEstimate(
            flops=6 * total * ff * n_k * width,
            bytes_accessed=6 * ff * n_k * width,
            transcendentals=total * ff,
        ),
        name="expert_mlp",
    )(kidx, nidx, x, w_gate, w_up, w_down, scale)


def body(
    context,
    out_weight,
    residual,
    gate_weight,
    up_weight,
    down_weight,
    gate_values,
    chosen_blocks,
    block_counts,
):
    n_expert = lax.axis_size("expert")
    n_dp = lax.axis_size("dp")
    n_bits = n_dp.bit_length() - 2
    n_chip = 1 << n_bits
    local_tokens, model_width = context.shape
    local_width = residual.shape[1]
    half = local_width // 2
    depth = out_weight.shape[0]
    local_blocks = local_tokens // BLK
    my_expert = lax.axis_index("expert")
    my_data = lax.axis_index("dp")
    chip, side = my_data // 2, my_data % 2
    masks = jnp.where(
        side == 0,
        jnp.array(masks_of(n_bits, 0), jnp.int32),
        jnp.array(masks_of(n_bits, 1), jnp.int32),
    )
    chips = chip ^ masks
    reverse = bit_reversed(n_bits)
    pair = pair_pairs(n_dp)

    def split_sides(value):
        own = lax.dynamic_slice_in_dim(value, side * half, half, axis=1)
        other = lax.dynamic_slice_in_dim(value, (1 - side) * half, half, axis=1)
        return own, lax.ppermute(other, "dp", pair)

    w_piece = jnp.concatenate(split_sides(out_weight), axis=0)
    pieces = [w_piece]
    for step in range(n_bits):
        pieces = pieces + [lax.ppermute(p, "dp", step_pairs(n_dp, step)) for p in pieces]
    context_pair = jnp.concatenate([context, lax.ppermute(context, "dp", pair)], axis=0)
    residual_pair = jnp.concatenate(split_sides(residual), axis=0)
    projected = jnp.zeros((2 * local_tokens, half), jnp.float32)
    for r in range(n_chip):
        columns = jnp.concatenate(
            [
                lax.dynamic_slice_in_dim(context_pair, (chips[r] * 2 + s) * depth, depth, axis=1)
                for s in (side, 1 - side)
            ],
            axis=1,
        )
        projected = projected + jnp.dot(columns, pieces[r], preferred_element_type=jnp.float32)
    attended = (residual_pair.astype(jnp.float32) + projected).astype(jnp.bfloat16)

    group_rows = CAP * BLK // GROUPS
    share = group_rows // n_chip
    grains = attended.reshape(-1, share, half)
    per_block = BLK // share

    def grain_index(group, experts):
        row = group * group_rows + chips * share
        block = chosen_blocks[experts[None, :], (row // BLK)[:, None]]
        owner = block // local_blocks
        mine = owner // 2 == chip
        first = jnp.where(owner % 2 == side, 0, local_blocks) + block % local_blocks
        index = first * per_block + ((row % BLK) // share)[:, None]
        return jnp.where(mine, index, -1).reshape(-1).astype(jnp.int32)

    ahead = (my_expert + jnp.arange(n_expert)) % n_expert
    behind = (my_expert - jnp.arange(n_expert)) % n_expert
    my_count = lax.dynamic_index_in_dim(block_counts, my_expert, 0, keepdims=False)
    live = jnp.arange(CAP * BLK) // BLK < my_count
    scale_all = jnp.where(live, gate_values[0], 0.0).reshape(GROUPS, n_chip, share)
    sides = jnp.stack([side, 1 - side])
    kidx = (behind[None, :] * 2 + sides[:, None]).reshape(-1).astype(jnp.int32)
    nidx = (ahead[None, :] * 2 + sides[:, None]).reshape(-1).astype(jnp.int32)
    w_gate, w_up, w_down = gate_weight[0], up_weight[0], down_weight[0]
    reverse_index = jnp.array(reverse)

    received = []
    for group in range(GROUPS):
        masked = pick(grain_index(group, ahead), grains).reshape(n_chip, n_expert, share, half)
        mine = scatter_sum(masked, n_dp, n_bits)
        crossed = swap_planes(mine, n_expert)
        own_half = gather_all(crossed, n_dp, n_bits)
        to_other = jnp.stack([own_half[r] for r in reverse])
        picked = jnp.stack([own_half, lax.ppermute(to_other, "dp", pair)])
        scale = scale_all[group][chips].reshape(-1, 1)
        part = mlp(picked, kidx, nidx, w_gate, w_up, w_down, scale)
        to_other = jnp.stack([part[1, r] for r in reverse])
        got = lax.ppermute(to_other, "dp", pair)
        both = (part[0].astype(jnp.float32) + got.astype(jnp.float32)).astype(jnp.bfloat16)
        mine = scatter_sum(both, n_dp, n_bits)
        crossed = swap_planes(mine, n_expert)
        received.append(gather_all(crossed, n_dp, n_bits).reshape(-1, share, half))

    index = jnp.concatenate([grain_index(group, behind) for group in range(GROUPS)])
    mixed = finish(index, grains, received).reshape(2, local_tokens, half)
    got = lax.ppermute(mixed[1], "dp", pair)
    return jnp.where(
        side == 0,
        jnp.concatenate([mixed[0], got], axis=1),
        jnp.concatenate([got, mixed[0]], axis=1),
    )


def solution(mesh):
    in_specs = (
        P("dp", None),
        P("dp", "expert"),
        P("dp", "expert"),
        P("expert", None, "dp"),
        P("expert", None, "dp"),
        P("expert", "dp", None),
        P("expert", None),
        P(),
        P(),
    )
    out_specs = P("dp", "expert")
    return jax.shard_map(body, mesh=mesh, in_specs=in_specs, out_specs=out_specs, check_vma=False)
```

```python
import jax
import jax.numpy as jnp
from jax import lax
from jax.experimental import pallas as pl
from jax.experimental.pallas import tpu as pltpu
from jax.sharding import PartitionSpec as P

BLK = 128
CAP = 4
GROUPS = 2


def bit_orders(n_bits):
    forward = list(range(1, n_bits + 1))
    return forward, forward[::-1]


def step_pairs(n_dp, step):
    orders = bit_orders(n_dp.bit_length() - 2)
    return [(i, i ^ (1 << orders[i & 1][step])) for i in range(n_dp)]


def pair_pairs(n_dp):
    return [(i, i ^ 1) for i in range(n_dp)]


def masks_of(n_bits, side):
    order = bit_orders(n_bits)[side]
    return [
        sum(1 << (order[t] - 1) for t in range(n_bits) if (r >> t) & 1) for r in range(1 << n_bits)
    ]


def bit_reversed(n_bits):
    return [
        sum(1 << (n_bits - 1 - t) for t in range(n_bits) if (r >> t) & 1)
        for r in range(1 << n_bits)
    ]


SMEM = pl.BlockSpec(memory_space=pltpu.SMEM)
VMEM = pl.BlockSpec(memory_space=pltpu.VMEM)
ANY = pl.BlockSpec(memory_space=pl.ANY)
MIB = 1024 * 1024


def f32_sum(a, b):
    return (a.astype(jnp.float32) + b.astype(jnp.float32)).astype(jnp.bfloat16)


def exchange(value, n_dp, step):
    return lax.ppermute(value, "dp", step_pairs(n_dp, step))


def scatter_sum(keep, send, n_dp, n_bits):
    for step in range(n_bits - 1, -1, -1):
        got = exchange(send, n_dp, step)
        if step == 0:
            return f32_sum(keep, got)[0]
        half = 1 << (step - 1)
        keep, send = f32_sum(keep[:half], got[:half]), f32_sum(keep[half:], got[half:])


def gather_all(piece, n_dp, n_bits):
    pieces = [piece]
    for step in range(n_bits):
        pieces = pieces + [exchange(p, n_dp, step) for p in pieces]
    return pieces


def swap_planes(parts, n_expert):
    out = [parts[0]]
    for k in range(1, n_expert):
        pairs = [(i, (i + k) % n_expert) for i in range(n_expert)]
        out.append(lax.ppermute(parts[k], "expert", pairs))
    return jnp.stack(out)


def call(kernel, out_shape, in_specs, out_specs, name, limit, flops=0, moved=0, **more):
    return pl.pallas_call(
        kernel,
        out_shape=out_shape,
        in_specs=in_specs,
        out_specs=out_specs,
        compiler_params=pltpu.CompilerParams(vmem_limit_bytes=limit * MIB),
        cost_estimate=pl.CostEstimate(flops=flops, bytes_accessed=moved, transcendentals=0),
        name=name,
        **more,
    )


def load_kernel(src, after, out, sem):
    copy = pltpu.make_async_copy(src, out, sem)
    copy.start()
    copy.wait()


def load(weight, after, name):
    out = call(
        load_kernel,
        pltpu.VMEM(weight.shape, weight.dtype),
        [ANY, ANY],
        VMEM,
        name,
        1,
        moved=2 * weight.size,
        scratch_shapes=[pltpu.SemaphoreType.DMA],
    )(weight, after)
    return pltpu.with_memory_space_constraint(out, pltpu.VMEM)


def order_kernel(cidx, x_ref, after, own_ref, send_ref):
    own_ref[0] = x_ref[...]
    send_ref[0] = x_ref[...]


def order_context(context, chips, side, reverse, depth, after):
    rows, width = context.shape
    n_block = width // depth
    per_half = n_block // 2
    n_chip = n_block // 2
    r, s = jnp.arange(n_block) // 2, jnp.arange(n_block) % 2
    columns = chips[r] * 2 + (side ^ s)
    target = jnp.array(reverse)[r] * 2 + (1 - s)
    cidx = jnp.stack([columns, target]).astype(jnp.int32)
    shape = jax.ShapeDtypeStruct((2, rows, width // 2), context.dtype)
    return pl.pallas_call(
        order_kernel,
        out_shape=[shape, shape],
        grid_spec=pltpu.PrefetchScalarGridSpec(
            num_scalar_prefetch=1,
            grid=(n_block,),
            in_specs=[pl.BlockSpec((rows, depth), lambda i, c: (0, c[0, i])), ANY],
            out_specs=[
                pl.BlockSpec((1, rows, depth), lambda i, c: (i // per_half, 0, i % per_half)),
                pl.BlockSpec(
                    (1, rows, depth), lambda i, c: (c[1, i] // per_half, 0, c[1, i] % per_half)
                ),
            ],
        ),
        compiler_params=pltpu.CompilerParams(vmem_limit_bytes=12 * MIB),
        cost_estimate=pl.CostEstimate(flops=0, bytes_accessed=6 * context.size, transcendentals=0),
        name="order_context",
    )(cidx, context, after)


def project_kernel(n_w, last, *refs):
    if last:
        own, other, acc, res_own, res_other = refs[:5]
        weights, out, w_all, c_own, c_other, sems = refs[5 : 5 + n_w], *refs[5 + n_w :]
    else:
        own, other = refs[:2]
        weights, out, w_all, c_own, c_other, sems = refs[2 : 2 + n_w], *refs[2 + n_w :]
    copies = [
        pltpu.make_async_copy(own.at[int(last)], c_own, sems.at[0]),
        pltpu.make_async_copy(other.at[int(last)], c_other, sems.at[1]),
    ]
    for c in copies:
        c.start()
    depth = weights[0].shape[0]
    for i, w in enumerate(weights):
        w_all[i * depth : (i + 1) * depth, :] = w[...]
    for i, c in enumerate((c_own, c_other)):
        copies[i].wait()
        value = jnp.dot(c[...], w_all[...], preferred_element_type=jnp.float32)
        if last:
            res = (res_own, res_other)[i]
            value = value + acc[i] + res[...].astype(jnp.float32)
        out[i] = value.astype(out.dtype)


def project(own, other, weights, extra):
    last = len(extra) > 0
    rows, k = own.shape[1:]
    half = weights[0].shape[1]
    return call(
        lambda *refs: project_kernel(len(weights), last, *refs),
        jax.ShapeDtypeStruct((2, rows, half), jnp.bfloat16 if last else jnp.float32),
        [ANY, ANY] + [VMEM] * (len(extra) + len(weights)),
        VMEM,
        "project_last" if last else "project_first",
        20,
        flops=4 * rows * k * half,
        moved=6 * rows * k,
        scratch_shapes=[
            pltpu.VMEM((k, half), jnp.bfloat16),
            pltpu.VMEM((rows, k), jnp.bfloat16),
            pltpu.VMEM((rows, k), jnp.bfloat16),
            pltpu.SemaphoreType.DMA((2,)),
        ],
    )(own, other, *extra, *weights)


def pick_kernel(idx_ref, att_ref, after, keep_ref, send_ref):
    n = keep_ref.shape[0]
    for i in range(2 * n):
        idx = idx_ref[i]
        value = att_ref[jnp.maximum(idx, 0)]
        value = jnp.where(idx >= 0, value, jnp.zeros_like(value))
        if i < n:
            keep_ref[i] = value
        else:
            send_ref[i - n] = value


def pick(idx, attended, after):
    shape = jax.ShapeDtypeStruct((idx.shape[0] // 2,) + attended.shape[1:], attended.dtype)
    return call(
        pick_kernel, [shape, shape], [SMEM, VMEM, ANY], [VMEM, VMEM], "pick_blocks", 8, moved=4 * MIB
    )(idx, attended, after)


def finish_kernel(idx_ref, att_ref, *refs):
    pieces, out_ref, acc = refs[:-2], refs[-2], refs[-1]
    acc[...] = att_ref[...].astype(jnp.float32)
    at = 0
    for piece in pieces:
        for i in range(piece.shape[0]):
            idx = idx_ref[at]
            at += 1

            @pl.when(idx >= 0)
            def _():
                acc[idx] = acc[idx] + piece[i].astype(jnp.float32)

    out_ref[...] = acc[...].astype(out_ref.dtype)


def finish(idx, attended, pieces):
    return call(
        finish_kernel,
        jax.ShapeDtypeStruct(attended.shape, attended.dtype),
        [SMEM] + [VMEM] * (1 + len(pieces)),
        VMEM,
        "add_expert_rows",
        12,
        moved=4 * MIB,
        scratch_shapes=[pltpu.VMEM(attended.shape, jnp.float32)],
    )(idx, attended, *pieces)


def hidden_kernel(n, kidx, *refs):
    own, other, wg, wu, hid, xs = refs[:n], refs[n : 2 * n], *refs[2 * n :]
    n_z, rows, width = own[0].shape
    for s, pieces in enumerate((own, other)):
        for z in range(n_z):
            at = pl.ds(pl.multiple_of(kidx[s * n_z + z] * width, width), width)
            for r in range(n):
                xs[r * rows : (r + 1) * rows, at] = pieces[r][z]
    ff = wg.shape[1]
    tile = min(ff, 256)

    def one(i, carry):
        at = pl.ds(pl.multiple_of(i * tile, tile), tile)
        g = jnp.dot(xs[...], wg[:, at], preferred_element_type=jnp.float32)
        u = jnp.dot(xs[...], wu[:, at], preferred_element_type=jnp.float32)
        hid[:, at] = (g / (1.0 + jnp.exp(-g)) * u).astype(jnp.bfloat16)
        return carry

    lax.fori_loop(0, ff // tile, one, 0)


def hidden_units(own, other, kidx, w_gate, w_up):
    n = len(own)
    n_z, rows, width = own[0].shape
    model_width, ff = w_gate.shape
    return call(
        lambda *refs: hidden_kernel(n, *refs),
        jax.ShapeDtypeStruct((n * rows, ff), jnp.bfloat16),
        [SMEM] + [VMEM] * (2 * n + 2),
        VMEM,
        "expert_hidden",
        14,
        flops=4 * n * rows * ff * model_width,
        moved=2 * n * rows * model_width,
        scratch_shapes=[pltpu.VMEM((n * rows, model_width), jnp.bfloat16)],
    )(kidx, *own, *other, w_gate, w_up)


def down_kernel(order, nidx, hid, wd, scale, out):
    n, n_z, rows, width = out.shape
    for z in range(n_z):
        at = pl.ds(pl.multiple_of(nidx[z] * width, width), width)
        part = jnp.dot(hid[...], wd[:, at], preferred_element_type=jnp.float32)
        part = (part * scale[...]).astype(out.dtype)
        for r in range(n):
            out[order[r], z] = part[r * rows : (r + 1) * rows]


def down(hid, nidx, w_down, scale, order, rows, width):
    n, n_z = len(order), nidx.shape[0]
    return call(
        lambda *refs: down_kernel(order, *refs),
        jax.ShapeDtypeStruct((n, n_z, rows, width), jnp.bfloat16),
        [SMEM, VMEM, VMEM, VMEM],
        VMEM,
        "expert_down",
        10,
        flops=2 * hid.size * n_z * width,
        moved=2 * n * rows * n_z * width,
    )(nidx, hid, w_down, scale)


def body(
    context,
    out_weight,
    residual,
    gate_weight,
    up_weight,
    down_weight,
    gate_values,
    chosen_blocks,
    block_counts,
):
    n_expert = lax.axis_size("expert")
    n_dp = lax.axis_size("dp")
    n_bits = n_dp.bit_length() - 2
    n_chip = 1 << n_bits
    local_tokens, model_width = context.shape
    local_width = residual.shape[1]
    half = local_width // 2
    depth = out_weight.shape[0]
    local_blocks = local_tokens // BLK
    my_expert = lax.axis_index("expert")
    my_data = lax.axis_index("dp")
    chip, side = my_data // 2, my_data % 2
    masks = jnp.where(
        side == 0,
        jnp.array(masks_of(n_bits, 0), jnp.int32),
        jnp.array(masks_of(n_bits, 1), jnp.int32),
    )
    chips = chip ^ masks
    reverse = bit_reversed(n_bits)
    pair = pair_pairs(n_dp)

    def to_partner(value):
        return lax.ppermute(value, "dp", pair)

    def split_sides(value):
        own = lax.dynamic_slice_in_dim(value, side * half, half, axis=1)
        other = lax.dynamic_slice_in_dim(value, (1 - side) * half, half, axis=1)
        return own, to_partner(other)

    w_own, w_other = split_sides(out_weight)
    pieces = [(w_own, w_other)]
    for step in range(n_bits):
        pieces = pieces + [tuple(exchange(w, n_dp, step) for w in p) for p in pieces]
    pieces = [w for p in pieces for w in p]
    context_own, context_send = order_context(context, chips, side, reverse, depth, w_other)
    context_other = to_partner(context_send)
    residual_own, residual_other = split_sides(residual)
    first = project(context_own, context_other, pieces[:n_chip], ())
    w_gate = load(gate_weight[0], pieces[2], "load_gate")
    w_up = load(up_weight[0], pieces[2], "load_up")
    w_down = load(down_weight[0], pieces[2], "load_down")
    attended = project(
        context_own, context_other, pieces[n_chip:], (first, residual_own, residual_other)
    )

    group_rows = CAP * BLK // GROUPS
    share = group_rows // n_chip
    grains = attended.reshape(-1, share, half)
    per_block = BLK // share

    def grain_index(group, experts):
        row = group * group_rows + chips * share
        block = chosen_blocks[experts[None, :], (row // BLK)[:, None]]
        owner = block // local_blocks
        mine = owner // 2 == chip
        base = jnp.where(owner % 2 == side, 0, local_blocks) + block % local_blocks
        index = base * per_block + ((row % BLK) // share)[:, None]
        return jnp.where(mine, index, -1).reshape(-1).astype(jnp.int32)

    ahead = (my_expert + jnp.arange(n_expert)) % n_expert
    behind = (my_expert - jnp.arange(n_expert)) % n_expert
    my_count = lax.dynamic_index_in_dim(block_counts, my_expert, 0, keepdims=False)
    live = jnp.arange(CAP * BLK) // BLK < my_count
    scale_all = jnp.where(live, gate_values[0], 0.0).reshape(GROUPS, n_chip, share)
    sides = jnp.stack([side, 1 - side])
    kidx = (behind[None, :] * 2 + sides[:, None]).reshape(-1).astype(jnp.int32)
    nidx = (ahead[None, :] * 2 + sides[:, None]).astype(jnp.int32)
    plain = list(range(n_chip))

    received = []
    after = first
    for group in range(GROUPS):
        keep, send = pick(grain_index(group, ahead), grains, after)
        shape = (n_chip // 2, n_expert, share, half)
        mine = scatter_sum(keep.reshape(shape), send.reshape(shape), n_dp, n_bits)
        after = mine
        crossed = swap_planes(mine, n_expert)
        own_half = gather_all(crossed, n_dp, n_bits)
        got = [to_partner(p) for p in own_half]
        other_half = [got[r] for r in reverse]
        hid = hidden_units(own_half, other_half, kidx, w_gate, w_up)
        scale = scale_all[group][chips].reshape(-1, 1)
        to_other = down(hid, nidx[1], w_down, scale, reverse, share, half)
        got = to_partner(to_other)
        mine = down(hid, nidx[0], w_down, scale, plain, share, half)
        top = n_chip // 2
        mine = scatter_sum(
            f32_sum(mine[:top], got[:top]), f32_sum(mine[top:], got[top:]), n_dp, n_bits
        )
        crossed = swap_planes(mine, n_expert)
        received += gather_all(crossed, n_dp, n_bits)

    index = jnp.concatenate([grain_index(group, behind) for group in range(GROUPS)])
    mixed = finish(index, grains, received).reshape(2, local_tokens, half)
    got = to_partner(mixed[1])
    return jnp.where(
        side == 0,
        jnp.concatenate([mixed[0], got], axis=1),
        jnp.concatenate([got, mixed[0]], axis=1),
    )


def solution(mesh):
    in_specs = (
        P("dp", None),
        P("dp", "expert"),
        P("dp", "expert"),
        P("expert", None, "dp"),
        P("expert", None, "dp"),
        P("expert", "dp", None),
        P("expert", None),
        P(),
        P(),
    )
    out_specs = P("dp", "expert")
    return jax.shard_map(body, mesh=mesh, in_specs=in_specs, out_specs=out_specs, check_vma=False)
```

```python
import jax
import jax.numpy as jnp
from jax import lax
from jax.experimental import pallas as pl
from jax.experimental.pallas import tpu as pltpu
from jax.sharding import PartitionSpec as P

BLK = 128
CAP = 4
GROUPS = 2


def bit_orders(n_bits):
    forward = list(range(1, n_bits + 1))
    return forward, forward[::-1]


def step_pairs(n_dp, step):
    orders = bit_orders(n_dp.bit_length() - 2)
    return [(i, i ^ (1 << orders[i & 1][step])) for i in range(n_dp)]


def pair_pairs(n_dp):
    return [(i, i ^ 1) for i in range(n_dp)]


def masks_of(n_bits, side):
    order = bit_orders(n_bits)[side]
    return [
        sum(1 << (order[t] - 1) for t in range(n_bits) if (r >> t) & 1) for r in range(1 << n_bits)
    ]


def bit_reversed(n_bits):
    return [
        sum(1 << (n_bits - 1 - t) for t in range(n_bits) if (r >> t) & 1)
        for r in range(1 << n_bits)
    ]


SMEM = pl.BlockSpec(memory_space=pltpu.SMEM)
VMEM = pl.BlockSpec(memory_space=pltpu.VMEM)
ANY = pl.BlockSpec(memory_space=pl.ANY)
MIB = 1024 * 1024


def f32_sum(a, b):
    return (a.astype(jnp.float32) + b.astype(jnp.float32)).astype(jnp.bfloat16)


def exchange(value, n_dp, step):
    return lax.ppermute(value, "dp", step_pairs(n_dp, step))


def scatter_sum(keep, send, n_dp, n_bits, afters=()):
    seen = []
    for i, step in enumerate(range(n_bits - 1, -1, -1)):
        got = exchange(send, n_dp, step)
        keep, send = add_split(keep, got, afters[i] if i < len(afters) else None, step > 0)
        seen.append(keep)
    return keep[0], seen


def gather_all(piece, n_dp, n_bits):
    pieces = [piece]
    for step in range(n_bits):
        pieces = pieces + [exchange(p, n_dp, step) for p in pieces]
    return pieces


def swap_planes(parts, n_expert, after=None):
    out = [parts[0]]
    for k in range(1, n_expert):
        pairs = [(i, (i + k) % n_expert) for i in range(n_expert)]
        out.append(lax.ppermute(parts[k], "expert", pairs))
    return stack(out, after)


def call(kernel, out_shape, in_specs, out_specs, name, limit, flops=0, moved=0, **more):
    return pl.pallas_call(
        kernel,
        out_shape=out_shape,
        in_specs=in_specs,
        out_specs=out_specs,
        compiler_params=pltpu.CompilerParams(vmem_limit_bytes=limit * MIB),
        cost_estimate=pl.CostEstimate(flops=flops, bytes_accessed=moved, transcendentals=0),
        name=name,
        **more,
    )


def add_split_kernel(split, keep, got, *refs):
    out = refs[1:] if len(refs) > (2 if split else 1) else refs
    n = out[0].shape[0]
    for i in range(keep.shape[0]):
        value = f32_sum(keep[i], got[i])
        if i < n:
            out[0][i] = value
        else:
            out[1][i - n] = value


def add_split(keep, got, after, split):
    n = keep.shape[0]
    shape = jax.ShapeDtypeStruct((n // 2 if split else n,) + keep.shape[1:], keep.dtype)
    extra = [] if after is None else [after]
    out = call(
        lambda *refs: add_split_kernel(split, *refs),
        [shape] * (2 if split else 1),
        [VMEM, VMEM] + [ANY] * len(extra),
        [VMEM] * (2 if split else 1),
        "add_halves",
        8,
        moved=2 * keep.size,
    )(keep, got, *extra)
    return out if split else (out[0], None)


def stack_kernel(n, *refs):
    for i in range(n):
        refs[-1][i] = refs[i][...]


def stack(parts, after):
    extra = [] if after is None else [after]
    return call(
        lambda *refs: stack_kernel(len(parts), *refs),
        jax.ShapeDtypeStruct((len(parts),) + parts[0].shape, parts[0].dtype),
        [VMEM] * len(parts) + [ANY] * len(extra),
        VMEM,
        "stack_planes",
        8,
        moved=2 * len(parts) * parts[0].size,
    )(*parts, *extra)


class Place:
    def __init__(self, n_bits, n_expert):
        data = lax.axis_index("dp")
        self.chip, self.side = lax.div(data, 2), lax.rem(data, 2)
        self.expert = lax.axis_index("expert")
        self.n_expert = n_expert
        self.n_bits = n_bits

    def chip_at(self, r):
        first, second = (masks_of(self.n_bits, s)[r] for s in (0, 1))
        return self.chip ^ jnp.where(self.side == 0, first, second)

    def ahead(self, k):
        return lax.rem(self.expert + k, self.n_expert)

    def behind(self, k):
        return lax.rem(self.expert + (self.n_expert - k), self.n_expert)


class Layout:
    def __init__(self, group, n_chip, local_blocks):
        self.rows = CAP * BLK // GROUPS
        self.share = self.rows // n_chip
        self.group, self.local_blocks = group, local_blocks

    def first_row(self, place, r):
        return self.group * self.rows + place.chip_at(r) * self.share

    def grain(self, place, chosen, r, expert):
        row = self.first_row(place, r)
        block = chosen[expert, lax.div(row, BLK)]
        owner = lax.div(block, self.local_blocks)
        base = jnp.where(lax.rem(owner, 2) == place.side, 0, self.local_blocks)
        base = base + lax.rem(block, self.local_blocks)
        index = base * (BLK // self.share) + lax.div(lax.rem(row, BLK), self.share)
        return index, lax.div(owner, 2) == place.chip


def load_kernel(src, after, out, sem):
    copy = pltpu.make_async_copy(src, out, sem)
    copy.start()
    copy.wait()


def load(weight, after, name):
    out = call(
        load_kernel,
        pltpu.VMEM(weight.shape, weight.dtype),
        [ANY, ANY],
        VMEM,
        name,
        1,
        moved=2 * weight.size,
        scratch_shapes=[pltpu.SemaphoreType.DMA],
    )(weight, after)
    return pltpu.with_memory_space_constraint(out, pltpu.VMEM)


def project_kernel(make_place, parts, n_w, n_res, *refs):
    context, other = refs[:2]
    weights = refs[2 : 2 + n_w]
    extra = refs[2 + n_w : 2 + n_w + n_res]
    out, w_all, c_own, c_other, sems = refs[-5:]
    depth = weights[0].shape[0]
    place = make_place()
    copies = []
    for i, (src, dst) in enumerate(((context, c_own), (other, c_other))):
        for j, r in enumerate(parts):
            for s in range(2):
                at = (place.chip_at(r) * 2 + (place.side ^ s)) * depth
                at = pl.ds(pl.multiple_of(at, depth), depth)
                n = 2 * j + s
                copies.append(
                    pltpu.make_async_copy(
                        src.at[:, at], dst.at[:, n * depth : (n + 1) * depth], sems.at[i, n]
                    )
                )
    for c in copies:
        c.start()
    for i, w in enumerate(weights):
        w_all[i * depth : (i + 1) * depth, :] = w[...]
    for i, c in enumerate((c_own, c_other)):
        for copy in copies[i * n_w : (i + 1) * n_w]:
            copy.wait()
        value = jnp.dot(c[...], w_all[...], preferred_element_type=jnp.float32)
        if n_res:
            acc, *res = extra
            value = value + acc[i] + res[i][...].astype(jnp.float32)
        out[i] = value.astype(out.dtype)


def project(make_place, parts, own, other, weights, extra, held):
    last = len(extra) > 0
    rows = own.shape[0]
    depth, half = weights[0].shape
    k = depth * len(weights)
    return call(
        lambda *refs: project_kernel(make_place, parts, len(weights), len(extra), *refs),
        jax.ShapeDtypeStruct((2, rows, half), jnp.bfloat16 if last else jnp.float32),
        [ANY, ANY] + [VMEM] * (len(weights) + len(extra) + len(held)),
        VMEM,
        "project_last" if last else "project_first",
        20,
        flops=4 * rows * k * half,
        moved=6 * rows * k,
        scratch_shapes=[
            pltpu.VMEM((k, half), jnp.bfloat16),
            pltpu.VMEM((rows, k), jnp.bfloat16),
            pltpu.VMEM((rows, k), jnp.bfloat16),
            pltpu.SemaphoreType.DMA((2, len(weights))),
        ],
    )(own, other, *weights, *extra, *held)


def pick_kernel(make_place, layout, n_chip, chosen, att_ref, *refs):
    place = make_place()
    keep_ref, send_ref = refs[-2:]
    top = n_chip // 2
    for r in range(n_chip):
        for k in range(place.n_expert):
            index, mine = layout.grain(place, chosen, r, place.ahead(k))
            value = att_ref[jnp.where(mine, index, 0)]
            value = jnp.where(mine, value, jnp.zeros_like(value))
            if r < top:
                keep_ref[r, k] = value
            else:
                send_ref[r - top, k] = value


def pick(make_place, layout, n_chip, n_expert, chosen, grains, after):
    shape = (n_chip // 2, n_expert) + grains.shape[1:]
    shape = jax.ShapeDtypeStruct(shape, grains.dtype)
    extra = [] if after is None else [after]
    return call(
        lambda *refs: pick_kernel(make_place, layout, n_chip, *refs),
        [shape, shape],
        [SMEM, VMEM] + [ANY] * len(extra),
        [VMEM, VMEM],
        "pick_blocks",
        8,
        moved=4 * MIB,
    )(chosen, grains, *extra)


def finish_kernel(make_place, layouts, n_chip, chosen, att_ref, *refs):
    pieces, out_ref, acc = refs[:-2], refs[-2], refs[-1]
    place = make_place()
    acc[...] = att_ref[...].astype(jnp.float32)
    for g, layout in enumerate(layouts):
        for r in range(n_chip):
            piece = pieces[g * n_chip + r]
            for k in range(place.n_expert):
                index, mine = layout.grain(place, chosen, r, place.behind(k))

                @pl.when(mine)
                def _():
                    acc[index] = acc[index] + piece[k].astype(jnp.float32)

    out_ref[...] = acc[...].astype(out_ref.dtype)


def finish(make_place, layouts, n_chip, chosen, grains, pieces):
    return call(
        lambda *refs: finish_kernel(make_place, layouts, n_chip, *refs),
        jax.ShapeDtypeStruct(grains.shape, grains.dtype),
        [SMEM] + [VMEM] * (1 + len(pieces)),
        VMEM,
        "add_expert_rows",
        12,
        moved=4 * MIB,
        scratch_shapes=[pltpu.VMEM(grains.shape, jnp.float32)],
    )(chosen, grains, *pieces)


def hidden_kernel(make_place, n, *refs):
    own, other, wg, wu, hid, xs = refs[:n], refs[n : 2 * n], *refs[2 * n : 2 * n + 2], *refs[-2:]
    n_z, rows, width = own[0].shape
    place = make_place()
    for s, pieces in enumerate((own, other)):
        for z in range(n_z):
            at = (place.behind(z) * 2 + (place.side ^ s)) * width
            at = pl.ds(pl.multiple_of(at, width), width)
            for r in range(n):
                xs[r * rows : (r + 1) * rows, at] = pieces[r][z]
    ff = wg.shape[1]
    tile = min(ff, 256)

    def one(i, carry):
        at = pl.ds(pl.multiple_of(i * tile, tile), tile)
        g = jnp.dot(xs[...], wg[:, at], preferred_element_type=jnp.float32)
        u = jnp.dot(xs[...], wu[:, at], preferred_element_type=jnp.float32)
        hid[:, at] = (g / (1.0 + jnp.exp(-g)) * u).astype(jnp.bfloat16)
        return carry

    lax.fori_loop(0, ff // tile, one, 0)


def hidden_units(make_place, own, other, w_gate, w_up, after):
    n = len(own)
    n_z, rows, width = own[0].shape
    model_width, ff = w_gate.shape
    extra = [] if after is None else [after]
    return call(
        lambda *refs: hidden_kernel(make_place, n, *refs),
        jax.ShapeDtypeStruct((n * rows, ff), jnp.bfloat16),
        [VMEM] * (2 * n + 2) + [ANY] * len(extra),
        VMEM,
        "expert_hidden",
        14,
        flops=4 * n * rows * ff * model_width,
        moved=2 * n * rows * model_width,
        scratch_shapes=[pltpu.VMEM((n * rows, model_width), jnp.bfloat16)],
    )(*own, *other, w_gate, w_up, *extra)


def down_kernel(make_place, layout, order, s, counts, hid, wd, values, *refs):
    out = refs[-1]
    n, n_z, rows, width = out.shape
    place = make_place()
    count = counts[place.expert]
    scale = []
    for r in range(n):
        row = layout.first_row(place, r)
        value = values[pl.ds(pl.multiple_of(row, rows), rows), :]
        scale.append(jnp.where(lax.div(row, BLK) < count, value, jnp.zeros_like(value)))
    for z in range(n_z):
        at = (place.ahead(z) * 2 + (place.side ^ s)) * width
        at = pl.ds(pl.multiple_of(at, width), width)
        part = jnp.dot(hid[...], wd[:, at], preferred_element_type=jnp.float32)
        for r in range(n):
            out[order[r], z] = (part[r * rows : (r + 1) * rows] * scale[r]).astype(out.dtype)


def down(make_place, layout, order, s, n_z, width, counts, hid, w_down, values, after):
    n = len(order)
    extra = [] if after is None else [after]
    return call(
        lambda *refs: down_kernel(make_place, layout, order, s, *refs),
        jax.ShapeDtypeStruct((n, n_z, layout.share, width), jnp.bfloat16),
        [SMEM] + [VMEM] * 3 + [ANY] * len(extra),
        VMEM,
        "expert_down",
        10,
        flops=2 * hid.size * n_z * width,
        moved=2 * n * layout.share * n_z * width,
    )(counts, hid, w_down, values, *extra)


def body(
    context,
    out_weight,
    residual,
    gate_weight,
    up_weight,
    down_weight,
    gate_values,
    chosen_blocks,
    block_counts,
):
    n_expert = lax.axis_size("expert")
    n_dp = lax.axis_size("dp")
    n_bits = n_dp.bit_length() - 2
    n_chip = 1 << n_bits
    local_tokens, model_width = context.shape
    local_width = residual.shape[1]
    half = local_width // 2
    depth = out_weight.shape[0]
    local_blocks = local_tokens // BLK
    place = Place(n_bits, n_expert)
    side = place.side
    reverse = bit_reversed(n_bits)
    pair = pair_pairs(n_dp)

    def to_partner(value):
        return lax.ppermute(value, "dp", pair)

    def split_sides(value):
        own = lax.dynamic_slice_in_dim(value, side * half, half, axis=1)
        other = lax.dynamic_slice_in_dim(value, (1 - side) * half, half, axis=1)
        return own, to_partner(other)

    w_own, w_other = split_sides(out_weight)
    pieces = [(w_own, w_other)]
    for step in range(n_bits):
        pieces = pieces + [tuple(exchange(w, n_dp, step) for w in p) for p in pieces]
    pieces = [w for p in pieces for w in p]
    context_other = to_partner(context)
    residual_own, residual_other = split_sides(residual)
    w_gate = load(gate_weight[0], w_other, "load_gate")
    w_up = load(up_weight[0], w_other, "load_up")
    w_down = load(down_weight[0], w_other, "load_down")
    plain = list(range(n_chip))
    top = n_chip // 2

    def make_place():
        return Place(n_bits, n_expert)

    first = project(
        make_place, plain[:top], context, context_other, pieces[:n_chip], (), (w_gate, w_up, w_down)
    )
    attended = project(
        make_place,
        plain[top:],
        context,
        context_other,
        pieces[n_chip:],
        (first, residual_own, residual_other),
        (),
    )

    layouts = [Layout(group, n_chip, local_blocks) for group in range(GROUPS)]
    share = layouts[0].share
    grains = attended.reshape(-1, share, half)
    values = gate_values.reshape(-1, 1)

    received = []
    after_pick, after_add, after_stack, after_hidden, after_down = None, None, None, None, None
    for layout in layouts:
        keep, send = pick(make_place, layout, n_chip, n_expert, chosen_blocks, grains, after_pick)
        mine, sums = scatter_sum(keep, send, n_dp, n_bits, [after_add])
        after_pick = mine
        crossed = swap_planes(mine, n_expert, after_stack)
        after_add = crossed
        own_half = gather_all(crossed, n_dp, n_bits)
        got = [to_partner(p) for p in own_half]
        other_half = [got[r] for r in reverse]
        hid = hidden_units(make_place, own_half, other_half, w_gate, w_up, after_hidden)
        after_stack = hid

        def downs(order, s, after):
            return down(
                make_place, layout, order, s, n_expert, half, block_counts, hid, w_down, values, after
            )

        got = to_partner(downs(reverse, 1, after_down))
        mine = downs(plain, 0, after_down)
        keep, send = add_split(mine, got, None, True)
        after_hidden = keep
        mine, sums = scatter_sum(keep, send, n_dp, n_bits)
        after_down = sums[0]
        crossed = swap_planes(mine, n_expert)
        received += gather_all(crossed, n_dp, n_bits)

    mixed = finish(make_place, layouts, n_chip, chosen_blocks, grains, received).reshape(2, local_tokens, half)
    got = to_partner(mixed[1])
    return jnp.where(
        side == 0,
        jnp.concatenate([mixed[0], got], axis=1),
        jnp.concatenate([got, mixed[0]], axis=1),
    )


def solution(mesh):
    in_specs = (
        P("dp", None),
        P("dp", "expert"),
        P("dp", "expert"),
        P("expert", None, "dp"),
        P("expert", None, "dp"),
        P("expert", "dp", None),
        P("expert", None),
        P(),
        P(),
    )
    out_specs = P("dp", "expert")
    return jax.shard_map(body, mesh=mesh, in_specs=in_specs, out_specs=out_specs, check_vma=False)
```

```python
import jax
import jax.numpy as jnp
from jax import lax
from jax.experimental import pallas as pl
from jax.experimental.pallas import tpu as pltpu
from jax.sharding import PartitionSpec as P

BLK = 128
CAP = 4
GROUPS = 2


def bit_orders(n_bits):
    forward = list(range(1, n_bits + 1))
    return forward, forward[::-1]


def step_pairs(n_dp, step):
    orders = bit_orders(n_dp.bit_length() - 2)
    return [(i, i ^ (1 << orders[i & 1][step])) for i in range(n_dp)]


def pair_pairs(n_dp):
    return [(i, i ^ 1) for i in range(n_dp)]


def masks_of(n_bits, side):
    order = bit_orders(n_bits)[side]
    return [
        sum(1 << (order[t] - 1) for t in range(n_bits) if (r >> t) & 1) for r in range(1 << n_bits)
    ]


def bit_reversed(n_bits):
    return [
        sum(1 << (n_bits - 1 - t) for t in range(n_bits) if (r >> t) & 1)
        for r in range(1 << n_bits)
    ]


SMEM = pl.BlockSpec(memory_space=pltpu.SMEM)
VMEM = pl.BlockSpec(memory_space=pltpu.VMEM)
ANY = pl.BlockSpec(memory_space=pl.ANY)
HBM = pl.BlockSpec(memory_space=pltpu.HBM)
MIB = 1024 * 1024


def f32_sum(a, b):
    return (a.astype(jnp.float32) + b.astype(jnp.float32)).astype(jnp.bfloat16)


def exchange(value, n_dp, step):
    return lax.ppermute(value, "dp", step_pairs(n_dp, step))


def gather_all(piece, n_dp, n_bits):
    pieces = [piece]
    for step in range(n_bits):
        pieces = pieces + [exchange(p, n_dp, step) for p in pieces]
    return pieces


def swap_planes(parts, n_expert, after=None):
    out = [parts[0]]
    for k in range(1, n_expert):
        pairs = [(i, (i + k) % n_expert) for i in range(n_expert)]
        out.append(lax.ppermute(parts[k], "expert", pairs))
    return stack(out, after)


def call(kernel, out_shape, in_specs, out_specs, name, limit, flops=0, moved=0, **more):
    return pl.pallas_call(
        kernel,
        out_shape=out_shape,
        in_specs=in_specs,
        out_specs=out_specs,
        compiler_params=pltpu.CompilerParams(vmem_limit_bytes=limit * MIB),
        name=name,
        **more,
    )


def add_split_kernel(split, keep, got, *refs):
    out = refs[1:] if len(refs) > (2 if split else 1) else refs
    n = out[0].shape[0]
    for i in range(keep.shape[0]):
        value = f32_sum(keep[i], got[i])
        if i < n:
            out[0][i] = value
        else:
            out[1][i - n] = value


def add_split(keep, got, after, split):
    n = keep.shape[0]
    shape = jax.ShapeDtypeStruct((n // 2 if split else n,) + keep.shape[1:], keep.dtype)
    extra = [] if after is None else [after]
    out = call(
        lambda *refs: add_split_kernel(split, *refs),
        [shape] * (2 if split else 1),
        [VMEM, VMEM] + [ANY] * len(extra),
        [VMEM] * (2 if split else 1),
        "add_halves",
        8,
        moved=2 * keep.size,
    )(keep, got, *extra)
    return out if split else (out[0], None)


def stack_kernel(n, *refs):
    for i in range(n):
        refs[-1][i] = refs[i][...]


def stack(parts, after):
    extra = [] if after is None else [after]
    return call(
        lambda *refs: stack_kernel(len(parts), *refs),
        jax.ShapeDtypeStruct((len(parts),) + parts[0].shape, parts[0].dtype),
        [VMEM] * len(parts) + [ANY] * len(extra),
        VMEM,
        "stack_planes",
        8,
        moved=2 * len(parts) * parts[0].size,
    )(*parts, *extra)


class Place:
    def __init__(self, n_bits, n_expert):
        data = lax.axis_index("dp")
        self.chip, self.side = lax.div(data, 2), lax.rem(data, 2)
        self.expert = lax.axis_index("expert")
        self.n_expert = n_expert
        self.n_bits = n_bits

    def chip_at(self, r):
        first, second = (masks_of(self.n_bits, s)[r] for s in (0, 1))
        return self.chip ^ jnp.where(self.side == 0, first, second)

    def ahead(self, k):
        return lax.rem(self.expert + k, self.n_expert)

    def behind(self, k):
        return lax.rem(self.expert + (self.n_expert - k), self.n_expert)


class Layout:
    def __init__(self, group, n_chip, local_blocks):
        self.rows = CAP * BLK // GROUPS
        self.share = self.rows // n_chip
        self.group, self.local_blocks = group, local_blocks

    def first_row(self, place, r):
        return self.group * self.rows + place.chip_at(r) * self.share

    def grain(self, place, chosen, r, expert):
        row = self.first_row(place, r)
        block = chosen[expert, lax.div(row, BLK)]
        owner = lax.div(block, self.local_blocks)
        base = jnp.where(lax.rem(owner, 2) == place.side, 0, self.local_blocks)
        base = base + lax.rem(block, self.local_blocks)
        index = base * (BLK // self.share) + lax.div(lax.rem(row, BLK), self.share)
        return index, lax.div(owner, 2) == place.chip


def project_kernel(make_place, parts, n_w, n_res, *refs):
    context, other = refs[:2]
    weights = refs[2 : 2 + n_w]
    extra = refs[2 + n_w : 2 + n_w + n_res]
    out, w_all, c_own, c_other, sems = refs[-5:]
    depth = weights[0].shape[0]
    place = make_place()
    copies = []
    for i, (src, dst) in enumerate(((context, c_own), (other, c_other))):
        for j, r in enumerate(parts):
            for s in range(2):
                at = (place.chip_at(r) * 2 + (place.side ^ s)) * depth
                at = pl.ds(pl.multiple_of(at, depth), depth)
                n = 2 * j + s
                copies.append(
                    pltpu.make_async_copy(
                        src.at[:, at], dst.at[:, n * depth : (n + 1) * depth], sems.at[i, n]
                    )
                )
    for c in copies:
        c.start()
    for i, w in enumerate(weights):
        w_all[i * depth : (i + 1) * depth, :] = w[...]
    for i, c in enumerate((c_own, c_other)):
        for copy in copies[i * n_w : (i + 1) * n_w]:
            copy.wait()
        value = jnp.dot(c[...], w_all[...], preferred_element_type=jnp.float32)
        if n_res:
            acc, *res = extra
            value = value + acc[i] + res[i][...].astype(jnp.float32)
        out[i] = value.astype(out.dtype)


def project(make_place, parts, own, other, weights, extra):
    last = len(extra) > 0
    rows = own.shape[0]
    depth, half = weights[0].shape
    k = depth * len(weights)
    return call(
        lambda *refs: project_kernel(make_place, parts, len(weights), len(extra), *refs),
        jax.ShapeDtypeStruct((2, rows, half), jnp.bfloat16 if last else jnp.float32),
        [ANY, ANY] + [VMEM] * (len(weights) + len(extra)),
        VMEM,
        "project_last" if last else "project_first",
        20,
        flops=4 * rows * k * half,
        moved=6 * rows * k,
        scratch_shapes=[
            pltpu.VMEM((k, half), jnp.bfloat16),
            pltpu.VMEM((rows, k), jnp.bfloat16),
            pltpu.VMEM((rows, k), jnp.bfloat16),
            pltpu.SemaphoreType.DMA((2, len(weights))),
        ],
    )(own, other, *weights, *extra)


def pick_kernel(make_place, layout, n_chip, chosen, att_ref, *refs):
    place = make_place()
    keep_ref, send_ref = refs[-2:]
    top = n_chip // 2
    for r in range(n_chip):
        for k in range(place.n_expert):
            index, mine = layout.grain(place, chosen, r, place.ahead(k))
            value = att_ref[jnp.where(mine, index, 0)]
            value = jnp.where(mine, value, jnp.zeros_like(value))
            if r < top:
                keep_ref[r, k] = value
            else:
                send_ref[r - top, k] = value


def pick(make_place, layout, n_chip, n_expert, chosen, grains, after):
    shape = (n_chip // 2, n_expert) + grains.shape[1:]
    shape = jax.ShapeDtypeStruct(shape, grains.dtype)
    extra = [] if after is None else [after]
    return call(
        lambda *refs: pick_kernel(make_place, layout, n_chip, *refs),
        [shape, shape],
        [SMEM, VMEM] + [ANY] * len(extra),
        [VMEM, VMEM],
        "pick_blocks",
        8,
        moved=4 * MIB,
    )(chosen, grains, *extra)


def finish_kernel(make_place, layouts, n_chip, chosen, att_ref, *refs):
    pieces, out_ref, acc = refs[:-2], refs[-2], refs[-1]
    place = make_place()
    acc[...] = att_ref[...].astype(jnp.float32)
    for g, layout in enumerate(layouts):
        for r in range(n_chip):
            piece = pieces[g * n_chip + r]
            for k in range(place.n_expert):
                index, mine = layout.grain(place, chosen, r, place.behind(k))

                @pl.when(mine)
                def _():
                    acc[index] = acc[index] + piece[k].astype(jnp.float32)

    out_ref[...] = acc[...].astype(out_ref.dtype)


def finish(make_place, layouts, n_chip, chosen, grains, pieces):
    return call(
        lambda *refs: finish_kernel(make_place, layouts, n_chip, *refs),
        jax.ShapeDtypeStruct(grains.shape, grains.dtype),
        [SMEM] + [VMEM] * (1 + len(pieces)),
        VMEM,
        "add_expert_rows",
        12,
        moved=4 * MIB,
        scratch_shapes=[pltpu.VMEM(grains.shape, jnp.float32)],
    )(chosen, grains, *pieces)


def hidden_kernel(make_place, n, *refs):
    own, other, wg, wu = refs[:n], refs[n : 2 * n], *refs[2 * n : 2 * n + 2]
    hid, xs, wgs, wus, sems = refs[-5:]
    n_z, rows, width = own[0].shape
    place = make_place()
    n_tile, _, tile = wgs.shape

    def copies(i):
        at = pl.ds(pl.multiple_of(i * tile, tile), tile)
        return (
            pltpu.make_async_copy(wg.at[:, at], wgs.at[i], sems.at[0, i]),
            pltpu.make_async_copy(wu.at[:, at], wus.at[i], sems.at[1, i]),
        )

    def start(i):
        for c in copies(i):
            c.start()

    start(0)
    if n_tile > 1:
        start(1)
    for s, pieces in enumerate((own, other)):
        for z in range(n_z):
            at = (place.behind(z) * 2 + (place.side ^ s)) * width
            at = pl.ds(pl.multiple_of(at, width), width)
            for r in range(n):
                xs[r * rows : (r + 1) * rows, at] = pieces[r][z]

    def one(i, carry):
        for c in copies(i):
            c.wait()

        @pl.when(i + 2 < n_tile)
        def _():
            start(i + 2)

        at = pl.ds(pl.multiple_of(i * tile, tile), tile)
        g = jnp.dot(xs[...], wgs[i], preferred_element_type=jnp.float32)
        u = jnp.dot(xs[...], wus[i], preferred_element_type=jnp.float32)
        hid[:, at] = (g / (1.0 + jnp.exp(-g)) * u).astype(jnp.bfloat16)
        return carry

    lax.fori_loop(0, n_tile, one, 0)


def hidden_units(make_place, own, other, w_gate, w_up, after):
    n = len(own)
    n_z, rows, width = own[0].shape
    model_width, ff = w_gate.shape
    tile = min(ff, 256)
    extra = [] if after is None else [after]
    return call(
        lambda *refs: hidden_kernel(make_place, n, *refs),
        jax.ShapeDtypeStruct((n * rows, ff), jnp.bfloat16),
        [VMEM] * (2 * n) + [HBM] * 2 + [ANY] * len(extra),
        VMEM,
        "expert_hidden",
        28,
        flops=4 * n * rows * ff * model_width,
        moved=4 * model_width * ff,
        scratch_shapes=[
            pltpu.VMEM((n * rows, model_width), jnp.bfloat16),
            pltpu.VMEM((ff // tile, model_width, tile), jnp.bfloat16),
            pltpu.VMEM((ff // tile, model_width, tile), jnp.bfloat16),
            pltpu.SemaphoreType.DMA((2, ff // tile)),
        ],
    )(*own, *other, w_gate, w_up, *extra)


def down_kernel(make_place, layout, order, s, counts, hid, wd, values, *refs):
    out, wds, sems = refs[-3:]
    n, n_z, rows, width = out.shape
    place = make_place()
    copies = []
    for z in range(n_z):
        at = (place.ahead(z) * 2 + (place.side ^ s)) * width
        at = pl.ds(pl.multiple_of(at, width), width)
        copies.append(pltpu.make_async_copy(wd.at[:, at], wds.at[z], sems.at[z]))
    for c in copies:
        c.start()
    count = counts[place.expert]
    scale = []
    for r in range(n):
        row = layout.first_row(place, r)
        value = values[pl.ds(pl.multiple_of(row, rows), rows), :]
        scale.append(jnp.where(lax.div(row, BLK) < count, value, jnp.zeros_like(value)))
    for z in range(n_z):
        copies[z].wait()
        part = jnp.dot(hid[...], wds[z], preferred_element_type=jnp.float32)
        for r in range(n):
            out[order[r], z] = (part[r * rows : (r + 1) * rows] * scale[r]).astype(out.dtype)


def down(make_place, layout, order, s, n_z, width, counts, hid, w_down, values, after):
    n = len(order)
    ff = hid.shape[1]
    extra = [] if after is None else [after]
    return call(
        lambda *refs: down_kernel(make_place, layout, order, s, *refs),
        jax.ShapeDtypeStruct((n, n_z, layout.share, width), jnp.bfloat16),
        [SMEM, VMEM, HBM, VMEM] + [ANY] * len(extra),
        VMEM,
        "expert_down",
        12,
        flops=2 * hid.size * n_z * width,
        moved=2 * ff * n_z * width,
        scratch_shapes=[
            pltpu.VMEM((n_z, ff, width), jnp.bfloat16),
            pltpu.SemaphoreType.DMA((n_z,)),
        ],
    )(counts, hid, w_down, values, *extra)


def group_steps(layout, scope, tables, grains):
    make_place, n_dp, n_bits, n_expert, half, reverse, to_partner = scope
    chosen, counts, values, w_gate, w_up, w_down = tables
    n_chip = 1 << n_bits
    plain = list(range(n_chip))
    after = yield
    keep, send = pick(make_place, layout, n_chip, n_expert, chosen, grains, after)
    after = yield keep, None
    for step in range(n_bits - 1, -1, -1):
        keep, send = add_split(keep, exchange(send, n_dp, step), after, step > 0)
        after = yield keep, None
    crossed = swap_planes(keep[0], n_expert, after)
    own_half = gather_all(crossed, n_dp, n_bits)
    after = yield (own_half[1] if layout.group == GROUPS - 1 else crossed), None
    got = [to_partner(p) for p in own_half]
    other_half = [got[r] for r in reverse]
    hid = hidden_units(make_place, own_half, other_half, w_gate, w_up, after)
    after = yield hid, None

    def downs(order, s):
        return down(
            make_place, layout, order, s, n_expert, half, counts, hid, w_down, values, after
        )

    theirs = downs(reverse, 1)
    after = yield theirs, None
    mine = downs(plain, 0)
    after = yield mine, None
    keep, send = add_split(mine, to_partner(theirs), after, True)
    after = yield keep, None
    for step in range(n_bits - 1, -1, -1):
        keep, send = add_split(keep, exchange(send, n_dp, step), after, step > 0)
        after = yield keep, None
    crossed = swap_planes(keep[0], n_expert, after)
    yield crossed, gather_all(crossed, n_dp, n_bits)


def kernel_order(n_bits):
    order = [0, 0] + [1, 0] * n_bits + [1, 1]
    order += [0] * 4 + [1] * 2 + [0]
    return order + [1, 1] + [0, 1] * n_bits + [1]


def body(
    context,
    out_weight,
    residual,
    gate_weight,
    up_weight,
    down_weight,
    gate_values,
    chosen_blocks,
    block_counts,
):
    n_expert = lax.axis_size("expert")
    n_dp = lax.axis_size("dp")
    n_bits = n_dp.bit_length() - 2
    n_chip = 1 << n_bits
    local_tokens, model_width = context.shape
    local_width = residual.shape[1]
    half = local_width // 2
    depth = out_weight.shape[0]
    local_blocks = local_tokens // BLK
    place = Place(n_bits, n_expert)
    side = place.side
    reverse = bit_reversed(n_bits)
    pair = pair_pairs(n_dp)

    def to_partner(value):
        return lax.ppermute(value, "dp", pair)

    def split_sides(value):
        own = lax.dynamic_slice_in_dim(value, side * half, half, axis=1)
        other = lax.dynamic_slice_in_dim(value, (1 - side) * half, half, axis=1)
        return own, to_partner(other)

    w_own, w_other = split_sides(out_weight)
    pieces = [(w_own, w_other)]
    for step in range(n_bits):
        pieces = pieces + [tuple(exchange(w, n_dp, step) for w in p) for p in pieces]
    pieces = [w for p in pieces for w in p]
    context_other = to_partner(context)
    residual_own, residual_other = split_sides(residual)
    w_gate, w_up, w_down = gate_weight[0], up_weight[0], down_weight[0]
    plain = list(range(n_chip))
    top = n_chip // 2
    share = CAP * BLK // GROUPS // n_chip

    def make_place():
        return Place(n_bits, n_expert)

    first = project(
        make_place, plain[:top], context, context_other, pieces[:n_chip], ()
    )
    attended = project(
        make_place,
        plain[top:],
        context,
        context_other,
        pieces[n_chip:],
        (first, residual_own, residual_other),
    )

    layouts = [Layout(group, n_chip, local_blocks) for group in range(GROUPS)]
    grains = attended.reshape(-1, share, half)
    values = gate_values.reshape(-1, 1)

    scope = (make_place, n_dp, n_bits, n_expert, half, reverse, to_partner)
    tables = (chosen_blocks, block_counts, values, w_gate, w_up, w_down)
    groups = [group_steps(layout, scope, tables, grains) for layout in layouts]
    for group in groups:
        next(group)
    after, received = None, [None] * GROUPS
    for g in kernel_order(n_bits):
        after, done = groups[g].send(after)
        received[g] = done
    received = [piece for pieces in received for piece in pieces]

    mixed = finish(make_place, layouts, n_chip, chosen_blocks, grains, received).reshape(2, local_tokens, half)
    got = to_partner(mixed[1])
    return jnp.where(
        side == 0,
        jnp.concatenate([mixed[0], got], axis=1),
        jnp.concatenate([got, mixed[0]], axis=1),
    )


def solution(mesh):
    in_specs = (
        P("dp", None),
        P("dp", "expert"),
        P("dp", "expert"),
        P("expert", None, "dp"),
        P("expert", None, "dp"),
        P("expert", "dp", None),
        P("expert", None),
        P(),
        P(),
    )
    out_specs = P("dp", "expert")
    return jax.shard_map(body, mesh=mesh, in_specs=in_specs, out_specs=out_specs, check_vma=False)
```

```python
import jax
import jax.numpy as jnp
from jax import lax
from jax.experimental import pallas as pl
from jax.experimental.pallas import tpu as pltpu
from jax.sharding import PartitionSpec as P

BLK = 128
CAP = 4
GROUPS = 2


def bit_orders(n_bits):
    forward = list(range(1, n_bits + 1))
    return forward, forward[::-1]


def step_pairs(n_dp, step):
    orders = bit_orders(n_dp.bit_length() - 2)
    return [(i, i ^ (1 << orders[i & 1][step])) for i in range(n_dp)]


def pair_pairs(n_dp):
    return [(i, i ^ 1) for i in range(n_dp)]


def masks_of(n_bits, side):
    order = bit_orders(n_bits)[side]
    return [
        sum(1 << (order[t] - 1) for t in range(n_bits) if (r >> t) & 1) for r in range(1 << n_bits)
    ]


def bit_reversed(n_bits):
    return [
        sum(1 << (n_bits - 1 - t) for t in range(n_bits) if (r >> t) & 1)
        for r in range(1 << n_bits)
    ]


SMEM = pl.BlockSpec(memory_space=pltpu.SMEM)
VMEM = pl.BlockSpec(memory_space=pltpu.VMEM)
ANY = pl.BlockSpec(memory_space=pl.ANY)
MIB = 1024 * 1024


def exchange(value, n_dp, step):
    return lax.ppermute(value, "dp", step_pairs(n_dp, step))


def gather_all(piece, n_dp, n_bits):
    pieces = [piece]
    for step in range(n_bits):
        pieces = pieces + [exchange(p, n_dp, step) for p in pieces]
    return pieces


def swap_planes(parts, n_expert, after=None):
    out = [parts[0]]
    for k in range(1, n_expert):
        pairs = [(i, (i + k) % n_expert) for i in range(n_expert)]
        out.append(lax.ppermute(parts[k], "expert", pairs))
    return stack(out, after)


def call(kernel, out_shape, in_specs, out_specs, name, limit, **more):
    return pl.pallas_call(
        kernel,
        out_shape=out_shape,
        in_specs=in_specs,
        out_specs=out_specs,
        compiler_params=pltpu.CompilerParams(vmem_limit_bytes=limit * MIB),
        name=name,
        **more,
    )


def add_kernel(counts, *refs):
    at, outs = sum(counts), refs[-len(counts) :]
    terms = iter(refs[:at])
    for n, out in zip(counts, outs):
        total = next(terms)[...].astype(jnp.float32)
        for _ in range(n - 1):
            total = total + next(terms)[...].astype(jnp.float32)
        out[...] = total.astype(out.dtype)


def add_terms(terms, after):
    counts = [len(t) for t in terms]
    shapes = [jax.ShapeDtypeStruct(t[0].shape, t[0].dtype) for t in terms]
    return call(
        lambda *refs: add_kernel(counts, *refs),
        shapes,
        [VMEM] * sum(counts) + [ANY],
        [VMEM] * len(counts),
        "add_terms",
        8,
    )(*[x for t in terms for x in t], after)


def stack_kernel(n, *refs):
    for i in range(n):
        refs[-1][i] = refs[i][...]


def stack(parts, after):
    extra = [] if after is None else [after]
    return call(
        lambda *refs: stack_kernel(len(parts), *refs),
        jax.ShapeDtypeStruct((len(parts),) + parts[0].shape, parts[0].dtype),
        [VMEM] * len(parts) + [ANY] * len(extra),
        VMEM,
        "stack_planes",
        8,
    )(*parts, *extra)


class Place:
    def __init__(self, n_bits, n_expert):
        data = lax.axis_index("dp")
        self.chip, self.side = lax.div(data, 2), lax.rem(data, 2)
        self.expert = lax.axis_index("expert")
        self.n_expert = n_expert
        self.n_bits = n_bits

    def chip_at(self, r):
        first, second = (masks_of(self.n_bits, s)[r] for s in (0, 1))
        return self.chip ^ jnp.where(self.side == 0, first, second)

    def ahead(self, k):
        return lax.rem(self.expert + k, self.n_expert)

    def behind(self, k):
        return lax.rem(self.expert + (self.n_expert - k), self.n_expert)


class Layout:
    def __init__(self, group, n_chip, local_blocks):
        self.rows = CAP * BLK // GROUPS
        self.share = self.rows // n_chip
        self.group, self.local_blocks = group, local_blocks

    def first_row(self, place, r):
        return self.group * self.rows + place.chip_at(r) * self.share

    def grain(self, place, chosen, r, expert):
        row = self.first_row(place, r)
        block = chosen[expert, lax.div(row, BLK)]
        owner = lax.div(block, self.local_blocks)
        base = jnp.where(lax.rem(owner, 2) == place.side, 0, self.local_blocks)
        base = base + lax.rem(block, self.local_blocks)
        index = base * (BLK // self.share) + lax.div(lax.rem(row, BLK), self.share)
        return index, lax.div(owner, 2) == place.chip


def project_kernel(make_place, parts, n_w, n_res, *refs):
    context, other = refs[:2]
    weights = refs[2 : 2 + n_w]
    extra = refs[2 + n_w : 2 + n_w + n_res]
    out, w_all, c_own, c_other, sems = refs[-5:]
    depth = weights[0].shape[0]
    place = make_place()
    copies = []
    for i, (src, dst) in enumerate(((context, c_own), (other, c_other))):
        for j, r in enumerate(parts):
            for s in range(2):
                at = (place.chip_at(r) * 2 + (place.side ^ s)) * depth
                at = pl.ds(pl.multiple_of(at, depth), depth)
                n = 2 * j + s
                copies.append(
                    pltpu.make_async_copy(
                        src.at[:, at], dst.at[:, n * depth : (n + 1) * depth], sems.at[i, n]
                    )
                )
    for c in copies:
        c.start()
    for i, w in enumerate(weights):
        w_all[i * depth : (i + 1) * depth, :] = w[...]
    for i, c in enumerate((c_own, c_other)):
        for copy in copies[i * n_w : (i + 1) * n_w]:
            copy.wait()
        value = jnp.dot(c[...], w_all[...], preferred_element_type=jnp.float32)
        if n_res:
            acc, *res = extra
            value = value + acc[i] + res[i][...].astype(jnp.float32)
        out[i] = value.astype(out.dtype)


def project(make_place, parts, own, other, weights, extra):
    last = len(extra) > 0
    rows = own.shape[0]
    depth, half = weights[0].shape
    k = depth * len(weights)
    return call(
        lambda *refs: project_kernel(make_place, parts, len(weights), len(extra), *refs),
        jax.ShapeDtypeStruct((2, rows, half), jnp.bfloat16 if last else jnp.float32),
        [ANY, ANY] + [VMEM] * (len(weights) + len(extra)),
        VMEM,
        "project_last" if last else "project_first",
        20,
        scratch_shapes=[
            pltpu.VMEM((k, half), jnp.bfloat16),
            pltpu.VMEM((rows, k), jnp.bfloat16),
            pltpu.VMEM((rows, k), jnp.bfloat16),
            pltpu.SemaphoreType.DMA((2, len(weights))),
        ],
    )(own, other, *weights, *extra)


def pick_kernel(make_place, layout, n_chip, chosen, att_ref, *refs):
    place = make_place()
    outs = refs[-n_chip:]
    for r in range(n_chip):
        for k in range(place.n_expert):
            index, mine = layout.grain(place, chosen, r, place.ahead(k))
            value = att_ref[jnp.where(mine, index, 0)]
            outs[r][k] = jnp.where(mine, value, jnp.zeros_like(value))


def pick(make_place, layout, n_chip, n_expert, chosen, grains, after):
    shape = jax.ShapeDtypeStruct((n_expert,) + grains.shape[1:], grains.dtype)
    extra = [] if after is None else [after]
    return call(
        lambda *refs: pick_kernel(make_place, layout, n_chip, *refs),
        [shape] * n_chip,
        [SMEM, VMEM] + [ANY] * len(extra),
        [VMEM] * n_chip,
        "pick_blocks",
        8,
    )(chosen, grains, *extra)


def finish_kernel(make_place, layouts, n_chip, chosen, att_ref, *refs):
    pieces, out_ref, acc = refs[:-2], refs[-2], refs[-1]
    place = make_place()
    acc[...] = att_ref[...].astype(jnp.float32)
    for g, layout in enumerate(layouts):
        for r in range(n_chip):
            piece = pieces[g * n_chip + r]
            for k in range(place.n_expert):
                index, mine = layout.grain(place, chosen, r, place.behind(k))

                @pl.when(mine)
                def _():
                    acc[index] = acc[index] + piece[k].astype(jnp.float32)

    out_ref[...] = acc[...].astype(out_ref.dtype)


def finish(make_place, layouts, n_chip, chosen, grains, pieces):
    return call(
        lambda *refs: finish_kernel(make_place, layouts, n_chip, *refs),
        jax.ShapeDtypeStruct(grains.shape, grains.dtype),
        [SMEM] + [VMEM] * (1 + len(pieces)),
        VMEM,
        "add_expert_rows",
        12,
        scratch_shapes=[pltpu.VMEM(grains.shape, jnp.float32)],
    )(chosen, grains, *pieces)


def hidden_kernel(make_place, n, *refs):
    own, other, wg, wu = refs[:n], refs[n : 2 * n], *refs[2 * n : 2 * n + 2]
    hid, xs, wgs, wus, sems = refs[-5:]
    n_z, rows, width = own[0].shape
    place = make_place()
    n_tile, _, tile = wgs.shape

    def copies(i):
        at = pl.ds(pl.multiple_of(i * tile, tile), tile)
        return (
            pltpu.make_async_copy(wg.at[:, at], wgs.at[i], sems.at[0, i]),
            pltpu.make_async_copy(wu.at[:, at], wus.at[i], sems.at[1, i]),
        )

    def start(i):
        for c in copies(i):
            c.start()

    start(0)
    if n_tile > 1:
        start(1)
    for s, pieces in enumerate((own, other)):
        for z in range(n_z):
            at = (place.behind(z) * 2 + (place.side ^ s)) * width
            at = pl.ds(pl.multiple_of(at, width), width)
            for r in range(n):
                xs[r * rows : (r + 1) * rows, at] = pieces[r][z]

    def one(i, carry):
        for c in copies(i):
            c.wait()

        @pl.when(i + 2 < n_tile)
        def _():
            start(i + 2)

        at = pl.ds(pl.multiple_of(i * tile, tile), tile)
        g = jnp.dot(xs[...], wgs[i], preferred_element_type=jnp.float32)
        u = jnp.dot(xs[...], wus[i], preferred_element_type=jnp.float32)
        hid[:, at] = (g / (1.0 + jnp.exp(-g)) * u).astype(jnp.bfloat16)
        return carry

    lax.fori_loop(0, n_tile, one, 0)


def hidden_units(make_place, own, other, w_gate, w_up, after):
    n = len(own)
    n_z, rows, width = own[0].shape
    model_width, ff = w_gate.shape
    tile = min(ff, 256)
    extra = [] if after is None else [after]
    return call(
        lambda *refs: hidden_kernel(make_place, n, *refs),
        jax.ShapeDtypeStruct((n * rows, ff), jnp.bfloat16),
        [VMEM] * (2 * n) + [ANY] * 2 + [ANY] * len(extra),
        VMEM,
        "expert_hidden",
        28,
        scratch_shapes=[
            pltpu.VMEM((n * rows, model_width), jnp.bfloat16),
            pltpu.VMEM((ff // tile, model_width, tile), jnp.bfloat16),
            pltpu.VMEM((ff // tile, model_width, tile), jnp.bfloat16),
            pltpu.SemaphoreType.DMA((2, ff // tile)),
        ],
    )(*own, *other, w_gate, w_up, *extra)


def down_kernel(make_place, layout, order, s, counts, hid, wd, values, *refs):
    outs, wds, sems = refs[-2 - len(order) : -2], refs[-2], refs[-1]
    n = len(order)
    n_z, rows, width = outs[0].shape
    place = make_place()
    copies = []
    for z in range(n_z):
        at = (place.ahead(z) * 2 + (place.side ^ s)) * width
        at = pl.ds(pl.multiple_of(at, width), width)
        copies.append(pltpu.make_async_copy(wd.at[:, at], wds.at[z], sems.at[z]))
    for c in copies:
        c.start()
    count = counts[place.expert]
    scale = []
    for r in range(n):
        row = layout.first_row(place, r)
        value = values[pl.ds(pl.multiple_of(row, rows), rows), :]
        scale.append(jnp.where(lax.div(row, BLK) < count, value, jnp.zeros_like(value)))
    for z in range(n_z):
        copies[z].wait()
        part = jnp.dot(hid[...], wds[z], preferred_element_type=jnp.float32)
        for r in range(n):
            value = part[r * rows : (r + 1) * rows] * scale[r]
            outs[order[r]][z] = value.astype(jnp.bfloat16)


def down(make_place, layout, order, s, n_z, width, counts, hid, w_down, values, after):
    n = len(order)
    ff = hid.shape[1]
    extra = [] if after is None else [after]
    return call(
        lambda *refs: down_kernel(make_place, layout, order, s, *refs),
        [jax.ShapeDtypeStruct((n_z, layout.share, width), jnp.bfloat16)] * n,
        [SMEM, VMEM, ANY, VMEM] + [ANY] * len(extra),
        [VMEM] * n,
        "expert_down",
        12,
        scratch_shapes=[
            pltpu.VMEM((n_z, ff, width), jnp.bfloat16),
            pltpu.SemaphoreType.DMA((n_z,)),
        ],
    )(counts, hid, w_down, values, *extra)


def group_steps(layout, scope, tables, grains):
    make_place, n_dp, n_bits, n_expert, half, reverse, to_partner = scope
    chosen, counts, values, w_gate, w_up, w_down = tables
    n_chip = 1 << n_bits
    plain = list(range(n_chip))
    after = yield
    terms = [[p] for p in pick(make_place, layout, n_chip, n_expert, chosen, grains, after)]
    after = yield terms[0][0], None
    for step in range(n_bits - 1, -1, -1):
        half_way = 1 << step
        send = [t[0] for t in terms[half_way:]]
        if len(terms[half_way]) > 1:
            send = add_terms(terms[half_way:], after)
            after = yield send[0], None
        terms = [t + [exchange(s, n_dp, step)] for t, s in zip(terms, send)]
    mine = add_terms(terms, after)[0]
    after = yield mine, None
    crossed = swap_planes(mine, n_expert, after)
    own_half = gather_all(crossed, n_dp, n_bits)
    after = yield (own_half[1] if layout.group == GROUPS - 1 else crossed), None
    got = [to_partner(p) for p in own_half]
    other_half = [got[r] for r in reverse]
    hid = hidden_units(make_place, own_half, other_half, w_gate, w_up, after)
    after = yield hid, None

    def downs(order, s):
        return down(
            make_place, layout, order, s, n_expert, half, counts, hid, w_down, values, after
        )

    theirs = downs(reverse, 1)
    after = yield theirs[0], None
    mine = downs(plain, 0)
    after = yield mine[0], None
    terms = [[m, to_partner(t)] for m, t in zip(mine, theirs)]
    for step in range(n_bits - 1, -1, -1):
        send = add_terms(terms[1 << step :], after)
        after = yield send[0], None
        terms = [t + [exchange(s, n_dp, step)] for t, s in zip(terms, send)]
    mine = add_terms(terms, after)[0]
    after = yield mine, None
    crossed = swap_planes(mine, n_expert, after)
    yield crossed, gather_all(crossed, n_dp, n_bits)


def kernel_order(n_bits):
    order = [0, 0] + [1, 0] * n_bits + [1, 1]
    order += [0] * 4 + [1] * 2 + [0]
    return order + [1, 1] + [0, 1] * n_bits + [1]


def body(
    context,
    out_weight,
    residual,
    gate_weight,
    up_weight,
    down_weight,
    gate_values,
    chosen_blocks,
    block_counts,
):
    n_expert = lax.axis_size("expert")
    n_dp = lax.axis_size("dp")
    n_bits = n_dp.bit_length() - 2
    n_chip = 1 << n_bits
    local_tokens, model_width = context.shape
    local_width = residual.shape[1]
    half = local_width // 2
    depth = out_weight.shape[0]
    local_blocks = local_tokens // BLK
    place = Place(n_bits, n_expert)
    side = place.side
    reverse = bit_reversed(n_bits)
    pair = pair_pairs(n_dp)

    def to_partner(value):
        return lax.ppermute(value, "dp", pair)

    def split_sides(value):
        own = lax.dynamic_slice_in_dim(value, side * half, half, axis=1)
        other = lax.dynamic_slice_in_dim(value, (1 - side) * half, half, axis=1)
        return own, to_partner(other)

    w_own, w_other = split_sides(out_weight)
    pieces = [(w_own, w_other)]
    for step in range(n_bits):
        pieces = pieces + [tuple(exchange(w, n_dp, step) for w in p) for p in pieces]
    pieces = [w for p in pieces for w in p]
    context_other = to_partner(context)
    residual_own, residual_other = split_sides(residual)
    w_gate, w_up, w_down = gate_weight[0], up_weight[0], down_weight[0]
    plain = list(range(n_chip))
    top = n_chip // 2
    share = CAP * BLK // GROUPS // n_chip

    def make_place():
        return Place(n_bits, n_expert)

    first = project(
        make_place, plain[:top], context, context_other, pieces[:n_chip], ()
    )
    attended = project(
        make_place,
        plain[top:],
        context,
        context_other,
        pieces[n_chip:],
        (first, residual_own, residual_other),
    )

    layouts = [Layout(group, n_chip, local_blocks) for group in range(GROUPS)]
    grains = attended.reshape(-1, share, half)
    values = gate_values.reshape(-1, 1)

    scope = (make_place, n_dp, n_bits, n_expert, half, reverse, to_partner)
    tables = (chosen_blocks, block_counts, values, w_gate, w_up, w_down)
    groups = [group_steps(layout, scope, tables, grains) for layout in layouts]
    for group in groups:
        next(group)
    after, received = None, [None] * GROUPS
    for g in kernel_order(n_bits):
        after, done = groups[g].send(after)
        received[g] = done
    received = [piece for pieces in received for piece in pieces]

    mixed = finish(make_place, layouts, n_chip, chosen_blocks, grains, received).reshape(2, local_tokens, half)
    got = to_partner(mixed[1])
    return jnp.where(
        side == 0,
        jnp.concatenate([mixed[0], got], axis=1),
        jnp.concatenate([got, mixed[0]], axis=1),
    )


def solution(mesh):
    in_specs = (
        P("dp", None),
        P("dp", "expert"),
        P("dp", "expert"),
        P("expert", None, "dp"),
        P("expert", None, "dp"),
        P("expert", "dp", None),
        P("expert", None),
        P(),
        P(),
    )
    out_specs = P("dp", "expert")
    return jax.shard_map(body, mesh=mesh, in_specs=in_specs, out_specs=out_specs, check_vma=False)
```

```python
import jax
import jax.numpy as jnp
from jax import lax
from jax.experimental import pallas as pl
from jax.experimental.pallas import tpu as pltpu
from jax.sharding import PartitionSpec as P

BLK = 128
CAP = 4
GROUPS = 2


def bit_orders(n_bits):
    forward = list(range(1, n_bits + 1))
    return forward, forward[::-1]


def step_pairs(n_dp, step):
    orders = bit_orders(n_dp.bit_length() - 2)
    return [(i, i ^ (1 << orders[i & 1][step])) for i in range(n_dp)]


def pair_pairs(n_dp):
    return [(i, i ^ 1) for i in range(n_dp)]


def masks_of(n_bits, side):
    order = bit_orders(n_bits)[side]
    return [
        sum(1 << (order[t] - 1) for t in range(n_bits) if (r >> t) & 1) for r in range(1 << n_bits)
    ]


def bit_reversed(n_bits):
    return [
        sum(1 << (n_bits - 1 - t) for t in range(n_bits) if (r >> t) & 1)
        for r in range(1 << n_bits)
    ]


SMEM = pl.BlockSpec(memory_space=pltpu.SMEM)
VMEM = pl.BlockSpec(memory_space=pltpu.VMEM)
ANY = pl.BlockSpec(memory_space=pl.ANY)
MIB = 1024 * 1024


def exchange(value, n_dp, step):
    return lax.ppermute(value, "dp", step_pairs(n_dp, step))


def gather_all(piece, n_dp, n_bits):
    pieces = [piece]
    for step in range(n_bits):
        pieces = pieces + [exchange(p, n_dp, step) for p in pieces]
    return pieces


def swap_planes(parts, n_expert, after=None):
    out = [parts[0]]
    for k in range(1, n_expert):
        pairs = [(i, (i + k) % n_expert) for i in range(n_expert)]
        out.append(lax.ppermute(parts[k], "expert", pairs))
    return stack(out, after)


def call(kernel, out_shape, in_specs, out_specs, name, limit, **more):
    return pl.pallas_call(
        kernel,
        out_shape=out_shape,
        in_specs=in_specs,
        out_specs=out_specs,
        compiler_params=pltpu.CompilerParams(vmem_limit_bytes=limit * MIB),
        name=name,
        **more,
    )


def add_kernel(counts, *refs):
    at, outs = sum(counts), refs[-len(counts) :]
    terms = iter(refs[:at])
    for n, out in zip(counts, outs):
        total = next(terms)[...].astype(jnp.float32)
        for _ in range(n - 1):
            total = total + next(terms)[...].astype(jnp.float32)
        out[...] = total.astype(out.dtype)


def add_terms(terms, after):
    counts = [len(t) for t in terms]
    shapes = [jax.ShapeDtypeStruct(t[0].shape, t[0].dtype) for t in terms]
    return call(
        lambda *refs: add_kernel(counts, *refs),
        shapes,
        [VMEM] * sum(counts) + [ANY],
        [VMEM] * len(counts),
        "add_terms",
        8,
    )(*[x for t in terms for x in t], after)


def stack_kernel(n, *refs):
    for i in range(n):
        refs[-1][i] = refs[i][...]


def stack(parts, after):
    extra = [] if after is None else [after]
    return call(
        lambda *refs: stack_kernel(len(parts), *refs),
        jax.ShapeDtypeStruct((len(parts),) + parts[0].shape, parts[0].dtype),
        [VMEM] * len(parts) + [ANY] * len(extra),
        VMEM,
        "stack_planes",
        8,
    )(*parts, *extra)


class Place:
    def __init__(self, n_bits, n_expert):
        data = lax.axis_index("dp")
        self.chip, self.side = lax.div(data, 2), lax.rem(data, 2)
        self.expert = lax.axis_index("expert")
        self.n_expert = n_expert
        self.n_bits = n_bits

    def chip_at(self, r):
        first, second = (masks_of(self.n_bits, s)[r] for s in (0, 1))
        return self.chip ^ jnp.where(self.side == 0, first, second)

    def ahead(self, k):
        return lax.rem(self.expert + k, self.n_expert)

    def behind(self, k):
        return lax.rem(self.expert + (self.n_expert - k), self.n_expert)


class Layout:
    def __init__(self, group, n_chip, local_blocks):
        self.rows = CAP * BLK // GROUPS
        self.share = self.rows // n_chip
        self.group, self.local_blocks = group, local_blocks

    def first_row(self, place, r):
        return self.group * self.rows + place.chip_at(r) * self.share

    def grain(self, place, chosen, r, expert):
        row = self.first_row(place, r)
        block = chosen[expert, lax.div(row, BLK)]
        owner = lax.div(block, self.local_blocks)
        base = jnp.where(lax.rem(owner, 2) == place.side, 0, self.local_blocks)
        base = base + lax.rem(block, self.local_blocks)
        index = base * (BLK // self.share) + lax.div(lax.rem(row, BLK), self.share)
        return index, lax.div(owner, 2) == place.chip


def project_kernel(make_place, parts, n_w, n_res, *refs):
    context, other = refs[:2]
    weights = refs[2 : 2 + n_w]
    extra = refs[2 + n_w : 2 + n_w + n_res]
    out, w_all, c_own, c_other, sems = refs[-5:]
    depth = weights[0].shape[0]
    place = make_place()
    copies = []
    for i, (src, dst) in enumerate(((context, c_own), (other, c_other))):
        for j, r in enumerate(parts):
            for s in range(2):
                at = (place.chip_at(r) * 2 + (place.side ^ s)) * depth
                at = pl.ds(pl.multiple_of(at, depth), depth)
                n = 2 * j + s
                copies.append(
                    pltpu.make_async_copy(
                        src.at[:, at], dst.at[:, n * depth : (n + 1) * depth], sems.at[i, n]
                    )
                )
    for c in copies:
        c.start()
    for i, w in enumerate(weights):
        w_all[i * depth : (i + 1) * depth, :] = w[...]
    for i, c in enumerate((c_own, c_other)):
        for copy in copies[i * n_w : (i + 1) * n_w]:
            copy.wait()
        value = jnp.dot(c[...], w_all[...], preferred_element_type=jnp.float32)
        if n_res:
            acc, *res = extra
            value = value + acc[i] + res[i][...].astype(jnp.float32)
        out[i] = value.astype(out.dtype)


def project(make_place, parts, own, other, weights, extra, unread):
    last = len(extra) > 0
    rows = own.shape[0]
    depth, half = weights[0].shape
    k = depth * len(weights)
    return call(
        lambda *refs: project_kernel(make_place, parts, len(weights), len(extra), *refs),
        jax.ShapeDtypeStruct((2, rows, half), jnp.bfloat16 if last else jnp.float32),
        [ANY, ANY] + [VMEM] * (len(weights) + len(extra)) + [ANY] * len(unread),
        VMEM,
        "project_last" if last else "project_first",
        12,
        scratch_shapes=[
            pltpu.VMEM((k, half), jnp.bfloat16),
            pltpu.VMEM((rows, k), jnp.bfloat16),
            pltpu.VMEM((rows, k), jnp.bfloat16),
            pltpu.SemaphoreType.DMA((2, len(weights))),
        ],
    )(own, other, *weights, *extra, *unread)


def pick_kernel(make_place, layout, n_chip, chosen, att_ref, *refs):
    place = make_place()
    outs = refs[-n_chip:]
    for r in range(n_chip):
        for k in range(place.n_expert):
            index, mine = layout.grain(place, chosen, r, place.ahead(k))
            value = att_ref[jnp.where(mine, index, 0)]
            outs[r][k] = jnp.where(mine, value, jnp.zeros_like(value))


def pick(make_place, layout, n_chip, n_expert, chosen, grains, after):
    shape = jax.ShapeDtypeStruct((n_expert,) + grains.shape[1:], grains.dtype)
    extra = [] if after is None else [after]
    return call(
        lambda *refs: pick_kernel(make_place, layout, n_chip, *refs),
        [shape] * n_chip,
        [SMEM, VMEM] + [ANY] * len(extra),
        [VMEM] * n_chip,
        "pick_blocks",
        8,
    )(chosen, grains, *extra)


def finish_kernel(make_place, layouts, n_chip, chosen, att_ref, *refs):
    pieces, outs, acc = refs[:-3], refs[-3:-1], refs[-1]
    place = make_place()
    acc[...] = att_ref[...].astype(jnp.float32)
    for g, layout in enumerate(layouts):
        for r in range(n_chip):
            piece = pieces[g * n_chip + r]
            for k in range(place.n_expert):
                index, mine = layout.grain(place, chosen, r, place.behind(k))

                @pl.when(mine)
                def _():
                    acc[index] = acc[index] + piece[k].astype(jnp.float32)

    n = outs[0].shape[0]
    for s, out in enumerate(outs):
        out[...] = acc[s * n : (s + 1) * n].astype(out.dtype)


def finish(make_place, layouts, n_chip, chosen, grains, pieces):
    return call(
        lambda *refs: finish_kernel(make_place, layouts, n_chip, *refs),
        [jax.ShapeDtypeStruct((grains.shape[0] // 2,) + grains.shape[1:], grains.dtype)] * 2,
        [SMEM] + [VMEM] * (1 + len(pieces)),
        [VMEM] * 2,
        "add_expert_rows",
        12,
        scratch_shapes=[pltpu.VMEM(grains.shape, jnp.float32)],
    )(chosen, grains, *pieces)


def join_kernel(make_place, own, other, out):
    side = make_place().side
    rows, half = out.shape[0], out.shape[1] // 2
    for s, value in enumerate((own, other)):
        at = pl.ds(pl.multiple_of((side ^ s) * half, half), half)
        out[:, at] = value[...].reshape(rows, half)


def join(make_place, own, other, rows):
    return call(
        lambda *refs: join_kernel(make_place, *refs),
        jax.ShapeDtypeStruct((rows, 2 * own.shape[-1]), own.dtype),
        [VMEM, VMEM],
        VMEM,
        "join_halves",
        8,
    )(own, other)


def hidden_kernel(make_place, n, *refs):
    own, other, wg, wu = refs[:n], refs[n : 2 * n], *refs[2 * n : 2 * n + 2]
    hid, xs = refs[-2:]
    n_z, rows, width = own[0].shape
    place = make_place()
    for s, pieces in enumerate((own, other)):
        for z in range(n_z):
            at = (place.behind(z) * 2 + (place.side ^ s)) * width
            at = pl.ds(pl.multiple_of(at, width), width)
            for r in range(n):
                xs[r * rows : (r + 1) * rows, at] = pieces[r][z]
    ff = wg.shape[1]
    tile = min(ff, 256)

    def one(i, carry):
        at = pl.ds(pl.multiple_of(i * tile, tile), tile)
        g = jnp.dot(xs[...], wg[:, at], preferred_element_type=jnp.float32)
        u = jnp.dot(xs[...], wu[:, at], preferred_element_type=jnp.float32)
        hid[:, at] = (g / (1.0 + jnp.exp(-g)) * u).astype(jnp.bfloat16)
        return carry

    lax.fori_loop(0, ff // tile, one, 0)


def hidden_units(make_place, own, other, w_gate, w_up, after):
    n = len(own)
    n_z, rows, width = own[0].shape
    model_width, ff = w_gate.shape
    return call(
        lambda *refs: hidden_kernel(make_place, n, *refs),
        jax.ShapeDtypeStruct((n * rows, ff), jnp.bfloat16),
        [VMEM] * (2 * n + 2) + [ANY],
        VMEM,
        "expert_hidden",
        12,
        scratch_shapes=[pltpu.VMEM((n * rows, model_width), jnp.bfloat16)],
    )(*own, *other, w_gate, w_up, after)


def down_kernel(make_place, layout, order, s, counts, hid, wd, values, after, *outs):
    n = len(order)
    n_z, rows, width = outs[0].shape
    place = make_place()
    count = counts[place.expert]
    n_row = values.shape[1]
    row_of = lax.broadcasted_iota(jnp.int32, (rows, n_row), 0)
    at_of = lax.broadcasted_iota(jnp.int32, (rows, n_row), 1)
    scale = []
    for r in range(n):
        row = layout.first_row(place, r)
        chosen = (at_of == row_of + row) & (lax.div(row, BLK) < count)
        scale.append(jnp.sum(jnp.where(chosen, values[...], 0.0), axis=1, keepdims=True))
    for z in range(n_z):
        at = (place.ahead(z) * 2 + (place.side ^ s)) * width
        at = pl.ds(pl.multiple_of(at, width), width)
        part = jnp.dot(hid[...], wd[:, at], preferred_element_type=jnp.float32)
        for r in range(n):
            value = part[r * rows : (r + 1) * rows] * scale[r]
            outs[order[r]][z] = value.astype(jnp.bfloat16)


def down(make_place, layout, order, s, n_z, width, counts, hid, w_down, values, after):
    n = len(order)
    return call(
        lambda *refs: down_kernel(make_place, layout, order, s, *refs),
        [jax.ShapeDtypeStruct((n_z, layout.share, width), jnp.bfloat16)] * n,
        [SMEM] + [VMEM] * 3 + [ANY],
        [VMEM] * n,
        "expert_down",
        8,
    )(counts, hid, w_down, values, after)


def group_steps(layout, scope, tables, grains):
    make_place, n_dp, n_bits, n_expert, half, reverse, to_partner = scope
    chosen, counts, values, w_gate, w_up, w_down = tables
    n_chip = 1 << n_bits
    plain = list(range(n_chip))
    after = yield
    terms = [[p] for p in pick(make_place, layout, n_chip, n_expert, chosen, grains, after)]
    after = yield terms[0][0], None
    for step in range(n_bits - 1, -1, -1):
        half_way = 1 << step
        send = [t[0] for t in terms[half_way:]]
        if len(terms[half_way]) > 1:
            send = add_terms(terms[half_way:], after)
            after = yield send[0], None
        terms = [t + [exchange(s, n_dp, step)] for t, s in zip(terms, send)]
    mine = add_terms(terms, after)[0]
    after = yield mine, None
    crossed = swap_planes(mine, n_expert, after)
    own_half = gather_all(crossed, n_dp, n_bits)
    after = yield (own_half[1] if layout.group == GROUPS - 1 else crossed), None
    got = [to_partner(p) for p in own_half]
    other_half = [got[r] for r in reverse]
    hid = hidden_units(make_place, own_half, other_half, w_gate, w_up, after)
    after = yield hid, None

    def downs(order, s):
        return down(
            make_place, layout, order, s, n_expert, half, counts, hid, w_down, values, after
        )

    theirs = downs(reverse, 1)
    after = yield theirs[0], None
    mine = downs(plain, 0)
    after = yield mine[0], None
    terms = [[m, to_partner(t)] for m, t in zip(mine, theirs)]
    for step in range(n_bits - 1, -1, -1):
        send = add_terms(terms[1 << step :], after)
        after = yield send[0], None
        terms = [t + [exchange(s, n_dp, step)] for t, s in zip(terms, send)]
    mine = add_terms(terms, after)[0]
    after = yield mine, None
    crossed = swap_planes(mine, n_expert, after)
    yield crossed, gather_all(crossed, n_dp, n_bits)


def kernel_order(n_bits):
    order = [0, 0] + [1, 0] * n_bits + [1, 1]
    order += [0] * 4 + [1] * 2 + [0]
    return order + [1, 1] + [0, 1] * n_bits + [1]


def body(
    context,
    out_weight,
    residual,
    gate_weight,
    up_weight,
    down_weight,
    gate_values,
    chosen_blocks,
    block_counts,
):
    n_expert = lax.axis_size("expert")
    n_dp = lax.axis_size("dp")
    n_bits = n_dp.bit_length() - 2
    n_chip = 1 << n_bits
    local_tokens, model_width = context.shape
    local_width = residual.shape[1]
    half = local_width // 2
    depth = out_weight.shape[0]
    local_blocks = local_tokens // BLK
    place = Place(n_bits, n_expert)
    side = place.side
    reverse = bit_reversed(n_bits)
    pair = pair_pairs(n_dp)

    def to_partner(value):
        return lax.ppermute(value, "dp", pair)

    def split_sides(value):
        own = lax.dynamic_slice_in_dim(value, side * half, half, axis=1)
        other = lax.dynamic_slice_in_dim(value, (1 - side) * half, half, axis=1)
        return own, to_partner(other)

    w_own, w_other = split_sides(out_weight)
    pieces = [(w_own, w_other)]
    for step in range(n_bits):
        pieces = pieces + [tuple(exchange(w, n_dp, step) for w in p) for p in pieces]
    pieces = [w for p in pieces for w in p]
    context_other = to_partner(context)
    residual_own, residual_other = split_sides(residual)
    w_gate, w_up, w_down = gate_weight[0], up_weight[0], down_weight[0]
    plain = list(range(n_chip))
    top = n_chip // 2
    share = CAP * BLK // GROUPS // n_chip

    def make_place():
        return Place(n_bits, n_expert)

    first = project(
        make_place,
        plain[:top],
        context,
        context_other,
        pieces[:n_chip],
        (),
        (),
    )
    attended = project(
        make_place,
        plain[top:],
        context,
        context_other,
        pieces[n_chip:],
        (first, residual_own, residual_other),
        (),
    )

    layouts = [Layout(group, n_chip, local_blocks) for group in range(GROUPS)]
    grains = attended.reshape(-1, share, half)
    values = gate_values

    scope = (make_place, n_dp, n_bits, n_expert, half, reverse, to_partner)
    tables = (chosen_blocks, block_counts, values, w_gate, w_up, w_down)
    groups = [group_steps(layout, scope, tables, grains) for layout in layouts]
    for group in groups:
        next(group)
    after, received = None, [None] * GROUPS
    for g in kernel_order(n_bits):
        after, done = groups[g].send(after)
        received[g] = done
    received = [piece for pieces in received for piece in pieces]

    own, other = finish(make_place, layouts, n_chip, chosen_blocks, grains, received)
    return join(make_place, own, to_partner(other), local_tokens)


def solution(mesh):
    in_specs = (
        P("dp", None),
        P("dp", "expert"),
        P("dp", "expert"),
        P("expert", None, "dp"),
        P("expert", None, "dp"),
        P("expert", "dp", None),
        P("expert", None),
        P(),
        P(),
    )
    out_specs = P("dp", "expert")
    return jax.shard_map(body, mesh=mesh, in_specs=in_specs, out_specs=out_specs, check_vma=False)
```

```python
import jax
import jax.numpy as jnp
from jax import lax
from jax.experimental import pallas as pl
from jax.experimental.pallas import tpu as pltpu
from jax.sharding import PartitionSpec as P

BLK = 128
CAP = 4
GROUPS = 2
DIRECT = ((0, 0, 0, 0), (0, 1, 1, 0))
PICK_WAIT = (0, 0)
HOP_WAIT = ((0, 1), (0, 0))
ORDER = '001010110010001011101011'


def bit_orders(n_bits):
    forward = list(range(1, n_bits + 1))
    return forward, forward[::-1]


def step_pairs(n_dp, step):
    orders = bit_orders(n_dp.bit_length() - 2)
    return [(i, i ^ (1 << orders[i & 1][step])) for i in range(n_dp)]


def pair_pairs(n_dp):
    return [(i, i ^ 1) for i in range(n_dp)]


def masks_of(n_bits, side):
    order = bit_orders(n_bits)[side]
    return [
        sum(1 << (order[t] - 1) for t in range(n_bits) if (r >> t) & 1) for r in range(1 << n_bits)
    ]


def bit_reversed(n_bits):
    return [
        sum(1 << (n_bits - 1 - t) for t in range(n_bits) if (r >> t) & 1)
        for r in range(1 << n_bits)
    ]


SMEM = pl.BlockSpec(memory_space=pltpu.SMEM)
VMEM = pl.BlockSpec(memory_space=pltpu.VMEM)
ANY = pl.BlockSpec(memory_space=pl.ANY)
MIB = 1024 * 1024


def exchange(value, n_dp, step):
    return lax.ppermute(value, "dp", step_pairs(n_dp, step))


def gather_steps(piece, n_dp, n_bits):
    pieces = [piece]
    for step in range(n_bits):
        pieces = pieces + [exchange(p, n_dp, step) for p in pieces]
    return pieces


def gather(piece, n_dp, n_bits, at_once):
    if at_once:
        return direct([piece] * (1 << n_bits), n_dp, n_bits)
    return gather_steps(piece, n_dp, n_bits)


def scatter(terms, n_dp, n_bits, at_once, hop_wait, wait, after):
    if at_once:
        if len(terms[0]) > 1:
            terms = [[t] for t in add_terms(terms, [after])]
            after = yield terms[0][0], None
        got = direct([t[0] for t in terms], n_dp, n_bits)
        if wait:
            after = yield got[1], None
        mine = add_terms([got], [after])[0]
        after = yield mine, None
        return mine, after
    for step in range(n_bits - 1, -1, -1):
        half_way = 1 << step
        send = [t[0] for t in terms[half_way:]]
        if len(terms[half_way]) > 1:
            others = [t[-1] for t in terms[:half_way]] if hop_wait else []
            send = add_terms(terms[half_way:], [after] + others)
            after = yield send[0], None
        terms = [t + [exchange(s, n_dp, step)] for t, s in zip(terms, send)]
        if wait and step == n_bits - 1:
            after = yield terms[half_way - 1][-1], None
    mine = add_terms(terms, [after])[0]
    after = yield mine, None
    return mine, after


def direct(values, n_dp, n_bits):
    masks = [masks_of(n_bits, side) for side in (0, 1)]
    out = []
    for r, value in enumerate(values):
        pairs = [(i, i ^ (masks[i & 1][r] << 1)) for i in range(n_dp)]
        out.append(lax.ppermute(value, "dp", pairs) if r else value)
    return out


def swap_planes(parts, n_expert, after=None):
    out = [parts[0]]
    for k in range(1, n_expert):
        pairs = [(i, (i + k) % n_expert) for i in range(n_expert)]
        out.append(lax.ppermute(parts[k], "expert", pairs))
    return stack(out, after)


def call(kernel, out_shape, in_specs, out_specs, name, limit, **more):
    return pl.pallas_call(
        kernel,
        out_shape=out_shape,
        in_specs=in_specs,
        out_specs=out_specs,
        compiler_params=pltpu.CompilerParams(vmem_limit_bytes=limit * MIB),
        name=name,
        **more,
    )


def add_kernel(counts, *refs):
    at, outs = sum(counts), refs[-len(counts) :]
    terms = iter(refs[:at])
    for n, out in zip(counts, outs):
        total = next(terms)[...].astype(jnp.float32)
        for _ in range(n - 1):
            total = total + next(terms)[...].astype(jnp.float32)
        out[...] = total.astype(out.dtype)


def add_terms(terms, unread):
    counts = [len(t) for t in terms]
    shapes = [jax.ShapeDtypeStruct(t[0].shape, t[0].dtype) for t in terms]
    return call(
        lambda *refs: add_kernel(counts, *refs),
        shapes,
        [VMEM] * sum(counts) + [ANY] * len(unread),
        [VMEM] * len(counts),
        "add_terms",
        8,
    )(*[x for t in terms for x in t], *unread)


def stack_kernel(n, *refs):
    for i in range(n):
        refs[-1][i] = refs[i][...]


def stack(parts, after):
    extra = [] if after is None else [after]
    return call(
        lambda *refs: stack_kernel(len(parts), *refs),
        jax.ShapeDtypeStruct((len(parts),) + parts[0].shape, parts[0].dtype),
        [VMEM] * len(parts) + [ANY] * len(extra),
        VMEM,
        "stack_planes",
        8,
    )(*parts, *extra)


class Place:
    def __init__(self, n_bits, n_expert):
        data = lax.axis_index("dp")
        self.chip, self.side = lax.div(data, 2), lax.rem(data, 2)
        self.expert = lax.axis_index("expert")
        self.n_expert = n_expert
        self.n_bits = n_bits

    def chip_at(self, r):
        first, second = (masks_of(self.n_bits, s)[r] for s in (0, 1))
        return self.chip ^ jnp.where(self.side == 0, first, second)

    def ahead(self, k):
        return lax.rem(self.expert + k, self.n_expert)

    def behind(self, k):
        return lax.rem(self.expert + (self.n_expert - k), self.n_expert)


class Layout:
    def __init__(self, group, n_chip, local_blocks):
        self.rows = CAP * BLK // GROUPS
        self.share = self.rows // n_chip
        self.group, self.local_blocks = group, local_blocks

    def first_row(self, place, r):
        return self.group * self.rows + place.chip_at(r) * self.share

    def grain(self, place, chosen, r, expert):
        row = self.first_row(place, r)
        block = chosen[expert, lax.div(row, BLK)]
        owner = lax.div(block, self.local_blocks)
        base = jnp.where(lax.rem(owner, 2) == place.side, 0, self.local_blocks)
        base = base + lax.rem(block, self.local_blocks)
        index = base * (BLK // self.share) + lax.div(lax.rem(row, BLK), self.share)
        return index, lax.div(owner, 2) == place.chip


def project_kernel(make_place, parts, n_w, n_res, *refs):
    context, other = refs[:2]
    weights = refs[2 : 2 + n_w]
    extra = refs[2 + n_w : 2 + n_w + n_res]
    out, w_all, c_own, c_other, sems = refs[-5:]
    depth = weights[0].shape[0]
    place = make_place()
    copies = []
    for i, (src, dst) in enumerate(((context, c_own), (other, c_other))):
        for j, r in enumerate(parts):
            for s in range(2):
                at = (place.chip_at(r) * 2 + (place.side ^ s)) * depth
                at = pl.ds(pl.multiple_of(at, depth), depth)
                n = 2 * j + s
                copies.append(
                    pltpu.make_async_copy(
                        src.at[:, at], dst.at[:, n * depth : (n + 1) * depth], sems.at[i, n]
                    )
                )
    for c in copies:
        c.start()
    for i, w in enumerate(weights):
        w_all[i * depth : (i + 1) * depth, :] = w[...]
    for i, c in enumerate((c_own, c_other)):
        for copy in copies[i * n_w : (i + 1) * n_w]:
            copy.wait()
        value = jnp.dot(c[...], w_all[...], preferred_element_type=jnp.float32)
        if n_res > 0:
            value = value + extra[0][i]
        if n_res > 1:
            value = value + extra[1 + i][...].astype(jnp.float32)
        out[i] = value.astype(out.dtype)


def project(make_place, parts, own, other, weights, extra):
    rows = own.shape[0]
    depth, half = weights[0].shape
    k = depth * len(weights)
    return call(
        lambda *refs: project_kernel(make_place, parts, len(weights), len(extra), *refs),
        jax.ShapeDtypeStruct((2, rows, half), jnp.bfloat16 if len(extra) > 1 else jnp.float32),
        [ANY, ANY] + [VMEM] * (len(weights) + len(extra)),
        VMEM,
        "project",
        12,
        scratch_shapes=[
            pltpu.VMEM((k, half), jnp.bfloat16),
            pltpu.VMEM((rows, k), jnp.bfloat16),
            pltpu.VMEM((rows, k), jnp.bfloat16),
            pltpu.SemaphoreType.DMA((2, len(weights))),
        ],
    )(own, other, *weights, *extra)


def pick_kernel(make_place, layout, n_chip, chosen, att_ref, *refs):
    place = make_place()
    outs = refs[-n_chip:]
    for r in range(n_chip):
        for k in range(place.n_expert):
            index, mine = layout.grain(place, chosen, r, place.ahead(k))
            value = att_ref[jnp.where(mine, index, 0)]
            outs[r][k] = jnp.where(mine, value, jnp.zeros_like(value))


def pick(make_place, layout, n_chip, n_expert, chosen, grains, after):
    shape = jax.ShapeDtypeStruct((n_expert,) + grains.shape[1:], grains.dtype)
    extra = [] if after is None else [after]
    return call(
        lambda *refs: pick_kernel(make_place, layout, n_chip, *refs),
        [shape] * n_chip,
        [SMEM, VMEM] + [ANY] * len(extra),
        [VMEM] * n_chip,
        "pick_blocks",
        8,
    )(chosen, grains, *extra)


def finish_kernel(make_place, layout, n_chip, lo, hi, chosen, *refs):
    pieces, old, out = refs[:n_chip], refs[n_chip], refs[n_chip + 1]
    acc = refs[-1]
    place = make_place()
    acc[...] = old[lo:hi].astype(jnp.float32)
    for r in range(n_chip):
        for k in range(place.n_expert):
            index, mine = layout.grain(place, chosen, r, place.behind(k))

            @pl.when(mine & (index >= lo) & (index < hi))
            def _():
                acc[index - lo] = acc[index - lo] + pieces[r][k].astype(jnp.float32)

    if acc is not out:
        out[...] = acc[...].astype(out.dtype)


def finish(make_place, layout, n_chip, chosen, old, pieces, lo, hi, last):
    dtype = jnp.bfloat16 if last else jnp.float32
    shape = (hi - lo,) + old.shape[1:]
    return call(
        lambda *refs: finish_kernel(make_place, layout, n_chip, lo, hi, *refs),
        jax.ShapeDtypeStruct(shape, dtype),
        [SMEM] + [VMEM] * (len(pieces) + 1),
        VMEM,
        "add_expert_rows",
        8,
        scratch_shapes=[pltpu.VMEM(shape, jnp.float32)] if last else (),
    )(chosen, *pieces, old)


def join_kernel(make_place, own, other, out):
    side = make_place().side
    rows, half = out.shape[0], out.shape[1] // 2
    for s, value in enumerate((own, other)):
        at = pl.ds(pl.multiple_of((side ^ s) * half, half), half)
        out[:, at] = value[...].reshape(rows, half)


def join(make_place, own, other, rows):
    return call(
        lambda *refs: join_kernel(make_place, *refs),
        jax.ShapeDtypeStruct((rows, 2 * own.shape[-1]), own.dtype),
        [VMEM, VMEM],
        VMEM,
        "join_halves",
        8,
    )(own, other)


def hidden_kernel(make_place, reverse, own, other, wg, wu, after, hid, xs):
    n_z, rows, width = own.shape[1:]
    place = make_place()
    for s, pieces in enumerate((own, other)):
        for z in range(n_z):
            at = (place.behind(z) * 2 + (place.side ^ s)) * width
            at = pl.ds(pl.multiple_of(at, width), width)
            for r, to in enumerate(reverse):
                to = to if s else r
                xs[to * rows : (to + 1) * rows, at] = pieces[r, z]
    ff = wg.shape[1]
    tile = min(ff, 256)

    def one(i, carry):
        at = pl.ds(pl.multiple_of(i * tile, tile), tile)
        g = jnp.dot(xs[...], wg[:, at], preferred_element_type=jnp.float32)
        u = jnp.dot(xs[...], wu[:, at], preferred_element_type=jnp.float32)
        hid[:, at] = (g / (1.0 + jnp.exp(-g)) * u).astype(jnp.bfloat16)
        return carry

    lax.fori_loop(0, ff // tile, one, 0)


def hidden_units(make_place, reverse, own, other, w_gate, w_up, after):
    n_row = own.shape[0] * own.shape[2]
    model_width, ff = w_gate.shape
    return call(
        lambda *refs: hidden_kernel(make_place, reverse, *refs),
        jax.ShapeDtypeStruct((n_row, ff), jnp.bfloat16),
        [VMEM] * 4 + [ANY],
        VMEM,
        "expert_hidden",
        12,
        scratch_shapes=[pltpu.VMEM((n_row, model_width), jnp.bfloat16)],
    )(own, other, w_gate, w_up, after)


def down_kernel(make_place, layout, order, s, counts, hid, wd, values, after, *outs):
    n = len(order)
    n_z, rows, width = outs[0].shape
    place = make_place()
    count = counts[place.expert]
    n_row = values.shape[1]
    row_of = lax.broadcasted_iota(jnp.int32, (rows, n_row), 0)
    at_of = lax.broadcasted_iota(jnp.int32, (rows, n_row), 1)
    scale = []
    for r in range(n):
        row = layout.first_row(place, r)
        chosen = (at_of == row_of + row) & (lax.div(row, BLK) < count)
        scale.append(jnp.sum(jnp.where(chosen, values[...], 0.0), axis=1, keepdims=True))
    for z in range(n_z):
        at = (place.ahead(z) * 2 + (place.side ^ s)) * width
        at = pl.ds(pl.multiple_of(at, width), width)
        part = jnp.dot(hid[...], wd[:, at], preferred_element_type=jnp.float32)
        for r in range(n):
            value = part[r * rows : (r + 1) * rows] * scale[r]
            outs[order[r]][z] = value.astype(jnp.bfloat16)


def down(make_place, layout, order, s, n_z, width, counts, hid, w_down, values, after):
    n = len(order)
    return call(
        lambda *refs: down_kernel(make_place, layout, order, s, *refs),
        [jax.ShapeDtypeStruct((n_z, layout.share, width), jnp.bfloat16)] * n,
        [SMEM] + [VMEM] * 3 + [ANY],
        [VMEM] * n,
        "expert_down",
        8,
    )(counts, hid, w_down, values, after)


def group_steps(layout, scope, tables, grains):
    make_place, n_dp, n_bits, n_expert, half, reverse, to_partner = scope
    chosen, counts, values, w_gate, w_up, w_down = tables
    n_chip = 1 << n_bits
    plain = list(range(n_chip))
    after = yield
    modes, hop_wait = DIRECT[layout.group], HOP_WAIT[layout.group]
    terms = [[p] for p in pick(make_place, layout, n_chip, n_expert, chosen, grains, after)]
    if not PICK_WAIT[layout.group]:
        after = yield terms[0][0], None
    mine, after = yield from scatter(
        terms, n_dp, n_bits, modes[0], hop_wait[0], PICK_WAIT[layout.group], after
    )
    crossed = swap_planes(mine, n_expert, after)
    own_half = gather(crossed, n_dp, n_bits, modes[1])
    after = yield crossed, None
    own = stack(own_half, after)
    other = to_partner(own)
    after = yield own, None
    hid = hidden_units(make_place, reverse, own, other, w_gate, w_up, after)
    after = yield hid, None

    def downs(order, s):
        return down(
            make_place, layout, order, s, n_expert, half, counts, hid, w_down, values, after
        )

    theirs = downs(reverse, 1)
    after = yield theirs[0], None
    mine = downs(plain, 0)
    after = yield mine[0], None
    terms = [[m, to_partner(t)] for m, t in zip(mine, theirs)]
    mine, after = yield from scatter(terms, n_dp, n_bits, modes[2], hop_wait[1], 0, after)
    crossed = swap_planes(mine, n_expert, after)
    yield crossed, gather(crossed, n_dp, n_bits, modes[3])


def body(
    context,
    out_weight,
    residual,
    gate_weight,
    up_weight,
    down_weight,
    gate_values,
    chosen_blocks,
    block_counts,
):
    n_expert = lax.axis_size("expert")
    n_dp = lax.axis_size("dp")
    n_bits = n_dp.bit_length() - 2
    n_chip = 1 << n_bits
    local_tokens, model_width = context.shape
    local_width = residual.shape[1]
    half = local_width // 2
    depth = out_weight.shape[0]
    local_blocks = local_tokens // BLK
    place = Place(n_bits, n_expert)
    side = place.side
    reverse = bit_reversed(n_bits)
    pair = pair_pairs(n_dp)

    def to_partner(value):
        return lax.ppermute(value, "dp", pair)

    def split_sides(value):
        own = lax.dynamic_slice_in_dim(value, side * half, half, axis=1)
        other = lax.dynamic_slice_in_dim(value, (1 - side) * half, half, axis=1)
        return own, to_partner(other)

    w_own, w_other = split_sides(out_weight)
    pieces = [(w_own, w_other)]
    for step in range(n_bits):
        pieces = pieces + [tuple(exchange(w, n_dp, step) for w in p) for p in pieces]
    pieces = [w for p in pieces for w in p]
    context_other = to_partner(context)
    residual_own, residual_other = split_sides(residual)
    w_gate, w_up, w_down = gate_weight[0], up_weight[0], down_weight[0]
    plain = list(range(n_chip))
    top = n_chip // 2
    share = CAP * BLK // GROUPS // n_chip

    def make_place():
        return Place(n_bits, n_expert)

    bounds = [0, top, n_chip - 1, n_chip]
    total = ()
    for lo, hi in zip(bounds[:-1], bounds[1:]):
        if hi == n_chip:
            total = total + (residual_own, residual_other)
        part = pieces[2 * lo : 2 * hi]
        total = (project(make_place, plain[lo:hi], context, context_other, part, total),)
    attended = total[0]

    layouts = [Layout(group, n_chip, local_blocks) for group in range(GROUPS)]
    grains = attended.reshape(-1, share, half)
    values = gate_values

    scope = (make_place, n_dp, n_bits, n_expert, half, reverse, to_partner)
    tables = (chosen_blocks, block_counts, values, w_gate, w_up, w_down)
    groups = [group_steps(layout, scope, tables, grains) for layout in layouts]
    for group in groups:
        next(group)
    after, received = None, [None] * GROUPS
    turn = 0
    while any(done is None for done in received):
        g = int(ORDER[turn]) if turn < len(ORDER) else turn % GROUPS
        turn += 1
        if received[g] is None:
            after, received[g] = groups[g].send(after)

    total, n = grains, grains.shape[0]
    for layout, got in zip(layouts[:-1], received[:-1]):
        total = finish(make_place, layout, n_chip, chosen_blocks, total, got, 0, n, False)
    last = (make_place, layouts[-1], n_chip, chosen_blocks, total, received[-1])
    other = finish(*last, n // 2, n, True)
    own = finish(*last, 0, n // 2, True)
    return join(make_place, own, to_partner(other), local_tokens)


def solution(mesh):
    in_specs = (
        P("dp", None),
        P("dp", "expert"),
        P("dp", "expert"),
        P("expert", None, "dp"),
        P("expert", None, "dp"),
        P("expert", "dp", None),
        P("expert", None),
        P(),
        P(),
    )
    out_specs = P("dp", "expert")
    return jax.shard_map(body, mesh=mesh, in_specs=in_specs, out_specs=out_specs, check_vma=False)
```

```python
import jax
import jax.numpy as jnp
from jax import lax
from jax.experimental import pallas as pl
from jax.experimental.pallas import tpu as pltpu
from jax.sharding import PartitionSpec as P

BLK = 128
CAP = 4
GROUPS = 2
DIRECT = ((0, 0, 0, 0), (0, 1, 1, 0))
PICK_WAIT = (0, 0)
HOP_WAIT = ((0, 1), (1, 0))
ORDER = '001010110001001101101011'


def bit_orders(n_bits):
    forward = list(range(1, n_bits + 1))
    return forward, forward[::-1]


def step_pairs(n_dp, step):
    orders = bit_orders(n_dp.bit_length() - 2)
    return [(i, i ^ (1 << orders[i & 1][step])) for i in range(n_dp)]


def pair_pairs(n_dp):
    return [(i, i ^ 1) for i in range(n_dp)]


def masks_of(n_bits, side):
    order = bit_orders(n_bits)[side]
    return [
        sum(1 << (order[t] - 1) for t in range(n_bits) if (r >> t) & 1) for r in range(1 << n_bits)
    ]


def bit_reversed(n_bits):
    return [
        sum(1 << (n_bits - 1 - t) for t in range(n_bits) if (r >> t) & 1)
        for r in range(1 << n_bits)
    ]


SMEM = pl.BlockSpec(memory_space=pltpu.SMEM)
VMEM = pl.BlockSpec(memory_space=pltpu.VMEM)
ANY = pl.BlockSpec(memory_space=pl.ANY)
MIB = 1024 * 1024


def exchange(value, n_dp, step):
    return lax.ppermute(value, "dp", step_pairs(n_dp, step))


def gather_steps(piece, n_dp, n_bits):
    pieces = [piece]
    for step in range(n_bits):
        pieces = pieces + [exchange(p, n_dp, step) for p in pieces]
    return pieces


def gather(piece, n_dp, n_bits, at_once):
    if at_once:
        return direct([piece] * (1 << n_bits), n_dp, n_bits)
    return gather_steps(piece, n_dp, n_bits)


def scatter(terms, n_dp, n_bits, at_once, hop_wait, wait, after):
    if at_once:
        if len(terms[0]) > 1:
            terms = [[t] for t in add_terms(terms, [after])]
            after = yield terms[0][0], None
        got = direct([t[0] for t in terms], n_dp, n_bits)
        if wait:
            after = yield got[1], None
        mine = add_terms([got], [after])[0]
        after = yield mine, None
        return mine, after
    for step in range(n_bits - 1, -1, -1):
        half_way = 1 << step
        send = [t[0] for t in terms[half_way:]]
        if len(terms[half_way]) > 1:
            others = [t[-1] for t in terms[:half_way]] if hop_wait else []
            send = add_terms(terms[half_way:], [after] + others)
            after = yield send[0], None
        terms = [t + [exchange(s, n_dp, step)] for t, s in zip(terms, send)]
        if wait and step == n_bits - 1:
            after = yield terms[half_way - 1][-1], None
    mine = add_terms(terms, [after])[0]
    after = yield mine, None
    return mine, after


def direct(values, n_dp, n_bits):
    masks = [masks_of(n_bits, side) for side in (0, 1)]
    out = []
    for r, value in enumerate(values):
        pairs = [(i, i ^ (masks[i & 1][r] << 1)) for i in range(n_dp)]
        out.append(lax.ppermute(value, "dp", pairs) if r else value)
    return out


def swap_planes(parts, n_expert, after=None):
    out = [parts[0]]
    for k in range(1, n_expert):
        pairs = [(i, (i + k) % n_expert) for i in range(n_expert)]
        out.append(lax.ppermute(parts[k], "expert", pairs))
    return stack(out, after)


def call(kernel, out_shape, in_specs, out_specs, name, limit, **more):
    return pl.pallas_call(
        kernel,
        out_shape=out_shape,
        in_specs=in_specs,
        out_specs=out_specs,
        compiler_params=pltpu.CompilerParams(vmem_limit_bytes=limit * MIB),
        name=name,
        **more,
    )


def add_kernel(counts, *refs):
    at, outs = sum(counts), refs[-len(counts) :]
    terms = iter(refs[:at])
    for n, out in zip(counts, outs):
        total = next(terms)[...].astype(jnp.float32)
        for _ in range(n - 1):
            total = total + next(terms)[...].astype(jnp.float32)
        out[...] = total.astype(out.dtype)


def add_terms(terms, unread):
    counts = [len(t) for t in terms]
    shapes = [jax.ShapeDtypeStruct(t[0].shape, t[0].dtype) for t in terms]
    return call(
        lambda *refs: add_kernel(counts, *refs),
        shapes,
        [VMEM] * sum(counts) + [ANY] * len(unread),
        [VMEM] * len(counts),
        "add_terms",
        8,
    )(*[x for t in terms for x in t], *unread)


def stack_kernel(n, *refs):
    for i in range(n):
        refs[-1][i] = refs[i][...]


def stack(parts, after):
    extra = [] if after is None else [after]
    return call(
        lambda *refs: stack_kernel(len(parts), *refs),
        jax.ShapeDtypeStruct((len(parts),) + parts[0].shape, parts[0].dtype),
        [VMEM] * len(parts) + [ANY] * len(extra),
        VMEM,
        "stack_planes",
        8,
    )(*parts, *extra)


class Place:
    def __init__(self, n_bits, n_expert):
        data = lax.axis_index("dp")
        self.chip, self.side = lax.div(data, 2), lax.rem(data, 2)
        self.expert = lax.axis_index("expert")
        self.n_expert = n_expert
        self.n_bits = n_bits

    def chip_at(self, r):
        first, second = (masks_of(self.n_bits, s)[r] for s in (0, 1))
        return self.chip ^ jnp.where(self.side == 0, first, second)

    def ahead(self, k):
        return lax.rem(self.expert + k, self.n_expert)

    def behind(self, k):
        return lax.rem(self.expert + (self.n_expert - k), self.n_expert)


class Layout:
    def __init__(self, group, n_chip, local_blocks):
        self.rows = CAP * BLK // GROUPS
        self.share = self.rows // n_chip
        self.group, self.local_blocks = group, local_blocks

    def first_row(self, place, r):
        return self.group * self.rows + place.chip_at(r) * self.share

    def grain(self, place, chosen, r, expert):
        row = self.first_row(place, r)
        block = chosen[expert, lax.div(row, BLK)]
        owner = lax.div(block, self.local_blocks)
        base = jnp.where(lax.rem(owner, 2) == place.side, 0, self.local_blocks)
        base = base + lax.rem(block, self.local_blocks)
        index = base * (BLK // self.share) + lax.div(lax.rem(row, BLK), self.share)
        return index, lax.div(owner, 2) == place.chip


def project_kernel(make_place, parts, n_w, n_res, *refs):
    context, other = refs[:2]
    weights = refs[2 : 2 + n_w]
    extra = refs[2 + n_w : 2 + n_w + n_res]
    out, w_all, c_own, c_other, sems = refs[-5:]
    depth = weights[0].shape[0]
    place = make_place()
    copies = []
    for i, (src, dst) in enumerate(((context, c_own), (other, c_other))):
        for j, r in enumerate(parts):
            for s in range(2):
                at = (place.chip_at(r) * 2 + (place.side ^ s)) * depth
                at = pl.ds(pl.multiple_of(at, depth), depth)
                n = 2 * j + s
                copies.append(
                    pltpu.make_async_copy(
                        src.at[:, at], dst.at[:, n * depth : (n + 1) * depth], sems.at[i, n]
                    )
                )
    for c in copies:
        c.start()
    for i, w in enumerate(weights):
        w_all[i * depth : (i + 1) * depth, :] = w[...]
    for i, c in enumerate((c_own, c_other)):
        for copy in copies[i * n_w : (i + 1) * n_w]:
            copy.wait()
        value = jnp.dot(c[...], w_all[...], preferred_element_type=jnp.float32)
        if n_res > 0:
            value = value + extra[0][i]
        if n_res > 1:
            value = value + extra[1 + i][...].astype(jnp.float32)
        out[i] = value.astype(out.dtype)


def project(make_place, parts, own, other, weights, extra):
    rows = own.shape[0]
    depth, half = weights[0].shape
    k = depth * len(weights)
    return call(
        lambda *refs: project_kernel(make_place, parts, len(weights), len(extra), *refs),
        jax.ShapeDtypeStruct((2, rows, half), jnp.bfloat16 if len(extra) > 1 else jnp.float32),
        [ANY, ANY] + [VMEM] * (len(weights) + len(extra)),
        VMEM,
        "project",
        12,
        scratch_shapes=[
            pltpu.VMEM((k, half), jnp.bfloat16),
            pltpu.VMEM((rows, k), jnp.bfloat16),
            pltpu.VMEM((rows, k), jnp.bfloat16),
            pltpu.SemaphoreType.DMA((2, len(weights))),
        ],
    )(own, other, *weights, *extra)


def pick_kernel(make_place, layout, n_chip, chosen, att_ref, *refs):
    place = make_place()
    outs = refs[-n_chip:]
    for r in range(n_chip):
        for k in range(place.n_expert):
            index, mine = layout.grain(place, chosen, r, place.ahead(k))
            value = att_ref[jnp.where(mine, index, 0)]
            outs[r][k] = jnp.where(mine, value, jnp.zeros_like(value))


def pick(make_place, layout, n_chip, n_expert, chosen, grains, after):
    shape = jax.ShapeDtypeStruct((n_expert,) + grains.shape[1:], grains.dtype)
    extra = [] if after is None else [after]
    return call(
        lambda *refs: pick_kernel(make_place, layout, n_chip, *refs),
        [shape] * n_chip,
        [SMEM, VMEM] + [ANY] * len(extra),
        [VMEM] * n_chip,
        "pick_blocks",
        8,
    )(chosen, grains, *extra)


def finish_kernel(make_place, layout, n_chip, lo, hi, chosen, *refs):
    pieces, old, out = refs[:n_chip], refs[n_chip], refs[n_chip + 1]
    acc = refs[-1]
    place = make_place()
    acc[...] = old[lo:hi].astype(jnp.float32)
    for r in range(n_chip):
        for k in range(place.n_expert):
            index, mine = layout.grain(place, chosen, r, place.behind(k))

            @pl.when(mine & (index >= lo) & (index < hi))
            def _():
                acc[index - lo] = acc[index - lo] + pieces[r][k].astype(jnp.float32)

    if acc is not out:
        out[...] = acc[...].astype(out.dtype)


def finish(make_place, layout, n_chip, chosen, old, pieces, lo, hi, last):
    dtype = jnp.bfloat16 if last else jnp.float32
    shape = (hi - lo,) + old.shape[1:]
    return call(
        lambda *refs: finish_kernel(make_place, layout, n_chip, lo, hi, *refs),
        jax.ShapeDtypeStruct(shape, dtype),
        [SMEM] + [VMEM] * (len(pieces) + 1),
        VMEM,
        "add_expert_rows",
        8,
        scratch_shapes=[pltpu.VMEM(shape, jnp.float32)] if last else (),
    )(chosen, *pieces, old)


def join_kernel(make_place, own, other, out):
    side = make_place().side
    rows, half = out.shape[0], out.shape[1] // 2
    for s, value in enumerate((own, other)):
        at = pl.ds(pl.multiple_of((side ^ s) * half, half), half)
        out[:, at] = value[...].reshape(rows, half)


def join(make_place, own, other, rows):
    return call(
        lambda *refs: join_kernel(make_place, *refs),
        jax.ShapeDtypeStruct((rows, 2 * own.shape[-1]), own.dtype),
        [VMEM, VMEM],
        VMEM,
        "join_halves",
        8,
    )(own, other)


def hidden_kernel(make_place, reverse, own, other, wg, wu, after, hid, xs):
    n_z, rows, width = own.shape[1:]
    place = make_place()
    for s, pieces in enumerate((own, other)):
        for z in range(n_z):
            at = (place.behind(z) * 2 + (place.side ^ s)) * width
            at = pl.ds(pl.multiple_of(at, width), width)
            for r, to in enumerate(reverse):
                to = to if s else r
                xs[to * rows : (to + 1) * rows, at] = pieces[r, z]
    ff = wg.shape[1]
    tile = min(ff, 1024)

    def one(i, carry):
        at = pl.ds(pl.multiple_of(i * tile, tile), tile)
        g = jnp.dot(xs[...], wg[:, at], preferred_element_type=jnp.float32)
        u = jnp.dot(xs[...], wu[:, at], preferred_element_type=jnp.float32)
        hid[:, at] = (g / (1.0 + jnp.exp(-g)) * u).astype(jnp.bfloat16)
        return carry

    lax.fori_loop(0, ff // tile, one, 0)


def hidden_units(make_place, reverse, own, other, w_gate, w_up, after):
    n_row = own.shape[0] * own.shape[2]
    model_width, ff = w_gate.shape
    return call(
        lambda *refs: hidden_kernel(make_place, reverse, *refs),
        jax.ShapeDtypeStruct((n_row, ff), jnp.bfloat16),
        [VMEM] * 4 + [ANY],
        VMEM,
        "expert_hidden",
        12,
        scratch_shapes=[pltpu.VMEM((n_row, model_width), jnp.bfloat16)],
    )(own, other, w_gate, w_up, after)


def down_kernel(make_place, layout, order, s, counts, hid, wd, values, after, *outs):
    n = len(order)
    n_z, rows, width = outs[0].shape
    place = make_place()
    count = counts[place.expert]
    n_row = values.shape[1]
    row_of = lax.broadcasted_iota(jnp.int32, (rows, n_row), 0)
    at_of = lax.broadcasted_iota(jnp.int32, (rows, n_row), 1)
    scale = []
    for r in range(n):
        row = layout.first_row(place, r)
        chosen = (at_of == row_of + row) & (lax.div(row, BLK) < count)
        scale.append(jnp.sum(jnp.where(chosen, values[...], 0.0), axis=1, keepdims=True))
    for z in range(n_z):
        at = (place.ahead(z) * 2 + (place.side ^ s)) * width
        at = pl.ds(pl.multiple_of(at, width), width)
        part = jnp.dot(hid[...], wd[:, at], preferred_element_type=jnp.float32)
        for r in range(n):
            value = part[r * rows : (r + 1) * rows] * scale[r]
            outs[order[r]][z] = value.astype(jnp.bfloat16)


def down(make_place, layout, order, s, n_z, width, counts, hid, w_down, values, after):
    n = len(order)
    return call(
        lambda *refs: down_kernel(make_place, layout, order, s, *refs),
        [jax.ShapeDtypeStruct((n_z, layout.share, width), jnp.bfloat16)] * n,
        [SMEM] + [VMEM] * 3 + [ANY],
        [VMEM] * n,
        "expert_down",
        8,
    )(counts, hid, w_down, values, after)


def group_steps(layout, scope, tables, grains):
    make_place, n_dp, n_bits, n_expert, half, reverse, to_partner = scope
    chosen, counts, values, w_gate, w_up, w_down = tables
    n_chip = 1 << n_bits
    plain = list(range(n_chip))
    after = yield
    modes, hop_wait = DIRECT[layout.group], HOP_WAIT[layout.group]
    terms = [[p] for p in pick(make_place, layout, n_chip, n_expert, chosen, grains, after)]
    if not PICK_WAIT[layout.group]:
        after = yield terms[0][0], None
    mine, after = yield from scatter(
        terms, n_dp, n_bits, modes[0], hop_wait[0], PICK_WAIT[layout.group], after
    )
    crossed = swap_planes(mine, n_expert, after)
    own_half = gather(crossed, n_dp, n_bits, modes[1])
    after = yield crossed, None
    own = stack(own_half, after)
    other = to_partner(own)
    after = yield own, None
    hid = hidden_units(make_place, reverse, own, other, w_gate, w_up, after)
    after = yield hid, None

    def downs(order, s):
        return down(
            make_place, layout, order, s, n_expert, half, counts, hid, w_down, values, after
        )

    theirs = downs(reverse, 1)
    after = yield theirs[0], None
    mine = downs(plain, 0)
    after = yield mine[0], None
    terms = [[m, to_partner(t)] for m, t in zip(mine, theirs)]
    mine, after = yield from scatter(terms, n_dp, n_bits, modes[2], hop_wait[1], 0, after)
    crossed = swap_planes(mine, n_expert, after)
    yield crossed, gather(crossed, n_dp, n_bits, modes[3])


def body(
    context,
    out_weight,
    residual,
    gate_weight,
    up_weight,
    down_weight,
    gate_values,
    chosen_blocks,
    block_counts,
):
    n_expert = lax.axis_size("expert")
    n_dp = lax.axis_size("dp")
    n_bits = n_dp.bit_length() - 2
    n_chip = 1 << n_bits
    local_tokens, model_width = context.shape
    local_width = residual.shape[1]
    half = local_width // 2
    depth = out_weight.shape[0]
    local_blocks = local_tokens // BLK
    place = Place(n_bits, n_expert)
    side = place.side
    reverse = bit_reversed(n_bits)
    pair = pair_pairs(n_dp)

    def to_partner(value):
        return lax.ppermute(value, "dp", pair)

    def split_sides(value):
        own = lax.dynamic_slice_in_dim(value, side * half, half, axis=1)
        other = lax.dynamic_slice_in_dim(value, (1 - side) * half, half, axis=1)
        return own, to_partner(other)

    w_own, w_other = split_sides(out_weight)
    pieces = [(w_own, w_other)]
    for step in range(n_bits):
        pieces = pieces + [tuple(exchange(w, n_dp, step) for w in p) for p in pieces]
    pieces = [w for p in pieces for w in p]
    context_other = to_partner(context)
    residual_own, residual_other = split_sides(residual)
    w_gate, w_up, w_down = gate_weight[0], up_weight[0], down_weight[0]
    plain = list(range(n_chip))
    top = n_chip // 2
    share = CAP * BLK // GROUPS // n_chip

    def make_place():
        return Place(n_bits, n_expert)

    bounds = [0, top, n_chip - 1, n_chip]
    total = ()
    for lo, hi in zip(bounds[:-1], bounds[1:]):
        if hi == n_chip:
            total = total + (residual_own, residual_other)
        part = pieces[2 * lo : 2 * hi]
        total = (project(make_place, plain[lo:hi], context, context_other, part, total),)
    attended = total[0]

    layouts = [Layout(group, n_chip, local_blocks) for group in range(GROUPS)]
    grains = attended.reshape(-1, share, half)
    values = gate_values

    scope = (make_place, n_dp, n_bits, n_expert, half, reverse, to_partner)
    tables = (chosen_blocks, block_counts, values, w_gate, w_up, w_down)
    groups = [group_steps(layout, scope, tables, grains) for layout in layouts]
    for group in groups:
        next(group)
    after, received = None, [None] * GROUPS
    turn = 0
    while any(done is None for done in received):
        g = int(ORDER[turn]) if turn < len(ORDER) else turn % GROUPS
        turn += 1
        if received[g] is None:
            after, received[g] = groups[g].send(after)

    total, n = grains, grains.shape[0]
    for layout, got in zip(layouts[:-1], received[:-1]):
        total = finish(make_place, layout, n_chip, chosen_blocks, total, got, 0, n, False)
    last = (make_place, layouts[-1], n_chip, chosen_blocks, total, received[-1])
    other = finish(*last, n // 2, n, True)
    own = finish(*last, 0, n // 2, True)
    return join(make_place, own, to_partner(other), local_tokens)


def solution(mesh):
    in_specs = (
        P("dp", None),
        P("dp", "expert"),
        P("dp", "expert"),
        P("expert", None, "dp"),
        P("expert", None, "dp"),
        P("expert", "dp", None),
        P("expert", None),
        P(),
        P(),
    )
    out_specs = P("dp", "expert")
    return jax.shard_map(body, mesh=mesh, in_specs=in_specs, out_specs=out_specs, check_vma=False)
```

```python
import jax
import jax.numpy as jnp
from jax import lax
from jax.experimental import pallas as pl
from jax.experimental.pallas import tpu as pltpu
from jax.sharding import PartitionSpec as P

BLK = 128
CAP = 4
GROUPS = 2
DIRECT = ((0, 0, 0, 0), (0, 1, 1, 0))
PICK_WAIT = (0, 0)
HOP_WAIT = ((0, 1), (1, 0))
ORDER = '001010110001001101101011'


def bit_orders(n_bits):
    forward = list(range(1, n_bits + 1))
    return forward, forward[::-1]


def step_pairs(n_dp, step):
    orders = bit_orders(n_dp.bit_length() - 2)
    return [(i, i ^ (1 << orders[i & 1][step])) for i in range(n_dp)]


def pair_pairs(n_dp):
    return [(i, i ^ 1) for i in range(n_dp)]


def masks_of(n_bits, side):
    order = bit_orders(n_bits)[side]
    return [
        sum(1 << (order[t] - 1) for t in range(n_bits) if (r >> t) & 1) for r in range(1 << n_bits)
    ]


def bit_reversed(n_bits):
    return [
        sum(1 << (n_bits - 1 - t) for t in range(n_bits) if (r >> t) & 1)
        for r in range(1 << n_bits)
    ]


SMEM = pl.BlockSpec(memory_space=pltpu.SMEM)
VMEM = pl.BlockSpec(memory_space=pltpu.VMEM)
ANY = pl.BlockSpec(memory_space=pl.ANY)
MIB = 1024 * 1024


def exchange(value, n_dp, step):
    return lax.ppermute(value, "dp", step_pairs(n_dp, step))


def gather_steps(piece, n_dp, n_bits):
    pieces = [piece]
    for step in range(n_bits):
        pieces = pieces + [exchange(p, n_dp, step) for p in pieces]
    return pieces


def gather(piece, n_dp, n_bits, at_once):
    if at_once:
        return direct([piece] * (1 << n_bits), n_dp, n_bits)
    return gather_steps(piece, n_dp, n_bits)


def scatter(terms, n_dp, n_bits, at_once, hop_wait, wait, after):
    if at_once:
        if len(terms[0]) > 1:
            terms = [[t] for t in add_terms(terms, [after])]
            after = yield terms[0][0], None
        got = direct([t[0] for t in terms], n_dp, n_bits)
        if wait:
            after = yield got[1], None
        mine = add_terms([got], [after])[0]
        after = yield mine, None
        return mine, after
    for step in range(n_bits - 1, -1, -1):
        half_way = 1 << step
        send = [t[0] for t in terms[half_way:]]
        if len(terms[half_way]) > 1:
            others = [t[-1] for t in terms[:half_way]] if hop_wait else []
            send = add_terms(terms[half_way:], [after] + others)
            after = yield send[0], None
        terms = [t + [exchange(s, n_dp, step)] for t, s in zip(terms, send)]
        if wait and step == n_bits - 1:
            after = yield terms[half_way - 1][-1], None
    mine = add_terms(terms, [after])[0]
    after = yield mine, None
    return mine, after


def direct(values, n_dp, n_bits):
    masks = [masks_of(n_bits, side) for side in (0, 1)]
    out = []
    for r, value in enumerate(values):
        pairs = [(i, i ^ (masks[i & 1][r] << 1)) for i in range(n_dp)]
        out.append(lax.ppermute(value, "dp", pairs) if r else value)
    return out


def swap_planes(parts, n_expert, after=None):
    out = [parts[0]]
    for k in range(1, n_expert):
        pairs = [(i, (i + k) % n_expert) for i in range(n_expert)]
        out.append(lax.ppermute(parts[k], "expert", pairs))
    return stack(out, after)


def call(kernel, out_shape, in_specs, out_specs, name, limit, **more):
    return pl.pallas_call(
        kernel,
        out_shape=out_shape,
        in_specs=in_specs,
        out_specs=out_specs,
        compiler_params=pltpu.CompilerParams(vmem_limit_bytes=limit * MIB),
        name=name,
        **more,
    )


def add_kernel(counts, *refs):
    at, outs = sum(counts), refs[-len(counts) :]
    terms = iter(refs[:at])
    for n, out in zip(counts, outs):
        total = next(terms)[...].astype(jnp.float32)
        for _ in range(n - 1):
            total = total + next(terms)[...].astype(jnp.float32)
        out[...] = total.astype(out.dtype)


def add_terms(terms, unread):
    counts = [len(t) for t in terms]
    shapes = [jax.ShapeDtypeStruct(t[0].shape, t[0].dtype) for t in terms]
    return call(
        lambda *refs: add_kernel(counts, *refs),
        shapes,
        [VMEM] * sum(counts) + [ANY] * len(unread),
        [VMEM] * len(counts),
        "add_terms",
        8,
    )(*[x for t in terms for x in t], *unread)


def stack_kernel(n, *refs):
    for i in range(n):
        refs[-1][i] = refs[i][...]


def stack(parts, after):
    extra = [] if after is None else [after]
    return call(
        lambda *refs: stack_kernel(len(parts), *refs),
        jax.ShapeDtypeStruct((len(parts),) + parts[0].shape, parts[0].dtype),
        [VMEM] * len(parts) + [ANY] * len(extra),
        VMEM,
        "stack_planes",
        8,
    )(*parts, *extra)


class Place:
    def __init__(self, n_bits, n_expert):
        data = lax.axis_index("dp")
        self.chip, self.side = lax.div(data, 2), lax.rem(data, 2)
        self.expert = lax.axis_index("expert")
        self.n_expert = n_expert
        self.n_bits = n_bits

    def chip_at(self, r):
        first, second = (masks_of(self.n_bits, s)[r] for s in (0, 1))
        return self.chip ^ jnp.where(self.side == 0, first, second)

    def ahead(self, k):
        return lax.rem(self.expert + k, self.n_expert)

    def behind(self, k):
        return lax.rem(self.expert + (self.n_expert - k), self.n_expert)


class Layout:
    def __init__(self, group, n_chip, local_blocks):
        self.rows = CAP * BLK // GROUPS
        self.share = self.rows // n_chip
        self.group, self.local_blocks = group, local_blocks

    def first_row(self, place, r):
        return self.group * self.rows + place.chip_at(r) * self.share

    def grain(self, place, chosen, r, expert):
        row = self.first_row(place, r)
        block = chosen[expert, lax.div(row, BLK)]
        owner = lax.div(block, self.local_blocks)
        base = jnp.where(lax.rem(owner, 2) == place.side, 0, self.local_blocks)
        base = base + lax.rem(block, self.local_blocks)
        index = base * (BLK // self.share) + lax.div(lax.rem(row, BLK), self.share)
        return index, lax.div(owner, 2) == place.chip


def project_kernel(make_place, parts, ahead, n_w, n_res, *refs):
    context, other = refs[:2]
    weights = refs[2 : 2 + n_w]
    extra = refs[2 + n_w : 2 + n_w + n_res]
    outs, (w_all, c_own, c_other, sems) = refs[2 + n_w + n_res : -4], refs[-4:]
    depth = weights[0].shape[0]
    place = make_place()

    def fetch(r, src, dst, at, sem):
        copies = []
        for s in range(2):
            column = (place.chip_at(r) * 2 + (place.side ^ s)) * depth
            column = pl.ds(pl.multiple_of(column, depth), depth)
            n = at + s
            copy = pltpu.make_async_copy(
                src.at[:, column], dst.at[:, n * depth : (n + 1) * depth], sem.at[n]
            )
            copy.start()
            copies.append(copy)
        return copies

    copies = []
    for i, (src, dst) in enumerate(((context, c_own), (other, c_other))):
        for j, r in enumerate(parts):
            copies += fetch(r, src, dst, 2 * j, sems.at[i])
    later = []
    if ahead is not None:
        for i, src in enumerate((context, other)):
            later += fetch(ahead, src, outs[1].at[i], 0, sems.at[2 + i])
    for i, w in enumerate(weights):
        w_all[i * depth : (i + 1) * depth, :] = w[...]
    for i, c in enumerate((c_own, c_other)):
        for copy in copies[i * n_w : (i + 1) * n_w]:
            copy.wait()
        value = jnp.dot(c[...], w_all[...], preferred_element_type=jnp.float32)
        if n_res > 0:
            value = value + extra[0][i]
        outs[0][i] = value
    for copy in later:
        copy.wait()


def project(make_place, parts, ahead, own, other, weights, extra):
    rows = own.shape[0]
    depth, half = weights[0].shape
    k = depth * len(weights)
    shapes = [jax.ShapeDtypeStruct((2, rows, half), jnp.float32)]
    if ahead is not None:
        shapes.append(jax.ShapeDtypeStruct((2, rows, 2 * depth), own.dtype))
    return call(
        lambda *refs: project_kernel(make_place, parts, ahead, len(weights), len(extra), *refs),
        shapes,
        [ANY, ANY] + [VMEM] * (len(weights) + len(extra)),
        [VMEM] * len(shapes),
        "project",
        12,
        scratch_shapes=[
            pltpu.VMEM((k, half), jnp.bfloat16),
            pltpu.VMEM((rows, k), jnp.bfloat16),
            pltpu.VMEM((rows, k), jnp.bfloat16),
            pltpu.SemaphoreType.DMA((4, len(weights))),
        ],
    )(own, other, *weights, *extra)


def project_last_kernel(columns, total, own, other, *refs):
    weights, out, w_all = refs[:-2], refs[-2], refs[-1]
    depth = weights[0].shape[0]
    for i, w in enumerate(weights):
        w_all[i * depth : (i + 1) * depth, :] = w[...]
    for i, res in enumerate((own, other)):
        value = jnp.dot(columns[i], w_all[...], preferred_element_type=jnp.float32)
        out[i] = (value + total[i] + res[...].astype(jnp.float32)).astype(out.dtype)


def project_last(columns, total, own, other, weights):
    depth, half = weights[0].shape
    return call(
        project_last_kernel,
        jax.ShapeDtypeStruct(total.shape, jnp.bfloat16),
        [VMEM] * (4 + len(weights)),
        VMEM,
        "project_last",
        12,
        scratch_shapes=[pltpu.VMEM((depth * len(weights), half), jnp.bfloat16)],
    )(columns, total, own, other, *weights)


def pick_kernel(make_place, layout, n_chip, chosen, att_ref, *refs):
    place = make_place()
    outs = refs[-n_chip:]
    for r in range(n_chip):
        for k in range(place.n_expert):
            index, mine = layout.grain(place, chosen, r, place.ahead(k))
            value = att_ref[jnp.where(mine, index, 0)]
            outs[r][k] = jnp.where(mine, value, jnp.zeros_like(value))


def pick(make_place, layout, n_chip, n_expert, chosen, grains, after):
    shape = jax.ShapeDtypeStruct((n_expert,) + grains.shape[1:], grains.dtype)
    extra = [] if after is None else [after]
    return call(
        lambda *refs: pick_kernel(make_place, layout, n_chip, *refs),
        [shape] * n_chip,
        [SMEM, VMEM] + [ANY] * len(extra),
        [VMEM] * n_chip,
        "pick_blocks",
        8,
    )(chosen, grains, *extra)


def finish_kernel(make_place, layout, n_chip, lo, hi, chosen, *refs):
    pieces, old, out = refs[:n_chip], refs[n_chip], refs[n_chip + 1]
    acc = refs[-1]
    place = make_place()
    acc[...] = old[lo:hi].astype(jnp.float32)
    for r in range(n_chip):
        for k in range(place.n_expert):
            index, mine = layout.grain(place, chosen, r, place.behind(k))

            @pl.when(mine & (index >= lo) & (index < hi))
            def _():
                acc[index - lo] = acc[index - lo] + pieces[r][k].astype(jnp.float32)

    if acc is not out:
        out[...] = acc[...].astype(out.dtype)


def finish(make_place, layout, n_chip, chosen, old, pieces, lo, hi, last):
    dtype = jnp.bfloat16 if last else jnp.float32
    shape = (hi - lo,) + old.shape[1:]
    return call(
        lambda *refs: finish_kernel(make_place, layout, n_chip, lo, hi, *refs),
        jax.ShapeDtypeStruct(shape, dtype),
        [SMEM] + [VMEM] * (len(pieces) + 1),
        VMEM,
        "add_expert_rows",
        8,
        scratch_shapes=[pltpu.VMEM(shape, jnp.float32)] if last else (),
    )(chosen, *pieces, old)


def join_kernel(make_place, own, other, out):
    side = make_place().side
    rows, half = out.shape[0], out.shape[1] // 2
    for s, value in enumerate((own, other)):
        at = pl.ds(pl.multiple_of((side ^ s) * half, half), half)
        out[:, at] = value[...].reshape(rows, half)


def join(make_place, own, other, rows):
    return call(
        lambda *refs: join_kernel(make_place, *refs),
        jax.ShapeDtypeStruct((rows, 2 * own.shape[-1]), own.dtype),
        [VMEM, VMEM],
        VMEM,
        "join_halves",
        8,
    )(own, other)


def hidden_kernel(make_place, reverse, own, other, wg, wu, after, hid, xs):
    n_z, rows, width = own.shape[1:]
    place = make_place()
    for s, pieces in enumerate((own, other)):
        for z in range(n_z):
            at = (place.behind(z) * 2 + (place.side ^ s)) * width
            at = pl.ds(pl.multiple_of(at, width), width)
            for r, to in enumerate(reverse):
                to = to if s else r
                xs[to * rows : (to + 1) * rows, at] = pieces[r, z]
    ff = wg.shape[1]
    tile = min(ff, 1024)

    def one(i, carry):
        at = pl.ds(pl.multiple_of(i * tile, tile), tile)
        g = jnp.dot(xs[...], wg[:, at], preferred_element_type=jnp.float32)
        u = jnp.dot(xs[...], wu[:, at], preferred_element_type=jnp.float32)
        hid[:, at] = (g / (1.0 + jnp.exp(-g)) * u).astype(jnp.bfloat16)
        return carry

    lax.fori_loop(0, ff // tile, one, 0)


def hidden_units(make_place, reverse, own, other, w_gate, w_up, after):
    n_row = own.shape[0] * own.shape[2]
    model_width, ff = w_gate.shape
    return call(
        lambda *refs: hidden_kernel(make_place, reverse, *refs),
        jax.ShapeDtypeStruct((n_row, ff), jnp.bfloat16),
        [VMEM] * 4 + [ANY],
        VMEM,
        "expert_hidden",
        12,
        scratch_shapes=[pltpu.VMEM((n_row, model_width), jnp.bfloat16)],
    )(own, other, w_gate, w_up, after)


def down_kernel(make_place, layout, order, s, counts, hid, wd, values, after, *outs):
    n = len(order)
    n_z, rows, width = outs[0].shape
    place = make_place()
    count = counts[place.expert]
    n_row = values.shape[1]
    row_of = lax.broadcasted_iota(jnp.int32, (rows, n_row), 0)
    at_of = lax.broadcasted_iota(jnp.int32, (rows, n_row), 1)
    scale = []
    for r in range(n):
        row = layout.first_row(place, r)
        chosen = (at_of == row_of + row) & (lax.div(row, BLK) < count)
        scale.append(jnp.sum(jnp.where(chosen, values[...], 0.0), axis=1, keepdims=True))
    for z in range(n_z):
        at = (place.ahead(z) * 2 + (place.side ^ s)) * width
        at = pl.ds(pl.multiple_of(at, width), width)
        part = jnp.dot(hid[...], wd[:, at], preferred_element_type=jnp.float32)
        for r in range(n):
            value = part[r * rows : (r + 1) * rows] * scale[r]
            outs[order[r]][z] = value.astype(jnp.bfloat16)


def down(make_place, layout, order, s, n_z, width, counts, hid, w_down, values, after):
    n = len(order)
    return call(
        lambda *refs: down_kernel(make_place, layout, order, s, *refs),
        [jax.ShapeDtypeStruct((n_z, layout.share, width), jnp.bfloat16)] * n,
        [SMEM] + [VMEM] * 3 + [ANY],
        [VMEM] * n,
        "expert_down",
        8,
    )(counts, hid, w_down, values, after)


def group_steps(layout, scope, tables, grains):
    make_place, n_dp, n_bits, n_expert, half, reverse, to_partner = scope
    chosen, counts, values, w_gate, w_up, w_down = tables
    n_chip = 1 << n_bits
    plain = list(range(n_chip))
    after = yield
    modes, hop_wait = DIRECT[layout.group], HOP_WAIT[layout.group]
    terms = [[p] for p in pick(make_place, layout, n_chip, n_expert, chosen, grains, after)]
    if not PICK_WAIT[layout.group]:
        after = yield terms[0][0], None
    mine, after = yield from scatter(
        terms, n_dp, n_bits, modes[0], hop_wait[0], PICK_WAIT[layout.group], after
    )
    crossed = swap_planes(mine, n_expert, after)
    own_half = gather(crossed, n_dp, n_bits, modes[1])
    after = yield crossed, None
    own = stack(own_half, after)
    other = to_partner(own)
    after = yield own, None
    hid = hidden_units(make_place, reverse, own, other, w_gate, w_up, after)
    after = yield hid, None

    def downs(order, s):
        return down(
            make_place, layout, order, s, n_expert, half, counts, hid, w_down, values, after
        )

    theirs = downs(reverse, 1)
    after = yield theirs[0], None
    mine = downs(plain, 0)
    after = yield mine[0], None
    terms = [[m, to_partner(t)] for m, t in zip(mine, theirs)]
    mine, after = yield from scatter(terms, n_dp, n_bits, modes[2], hop_wait[1], 0, after)
    crossed = swap_planes(mine, n_expert, after)
    yield crossed, gather(crossed, n_dp, n_bits, modes[3])


def body(
    context,
    out_weight,
    residual,
    gate_weight,
    up_weight,
    down_weight,
    gate_values,
    chosen_blocks,
    block_counts,
):
    n_expert = lax.axis_size("expert")
    n_dp = lax.axis_size("dp")
    n_bits = n_dp.bit_length() - 2
    n_chip = 1 << n_bits
    local_tokens, model_width = context.shape
    local_width = residual.shape[1]
    half = local_width // 2
    depth = out_weight.shape[0]
    local_blocks = local_tokens // BLK
    place = Place(n_bits, n_expert)
    side = place.side
    reverse = bit_reversed(n_bits)
    pair = pair_pairs(n_dp)

    def to_partner(value):
        return lax.ppermute(value, "dp", pair)

    def split_sides(value):
        own = lax.dynamic_slice_in_dim(value, side * half, half, axis=1)
        other = lax.dynamic_slice_in_dim(value, (1 - side) * half, half, axis=1)
        return own, to_partner(other)

    w_own, w_other = split_sides(out_weight)
    pieces = [(w_own, w_other)]
    for step in range(n_bits):
        pieces = pieces + [tuple(exchange(w, n_dp, step) for w in p) for p in pieces]
    pieces = [w for p in pieces for w in p]
    context_other = to_partner(context)
    residual_own, residual_other = split_sides(residual)
    w_gate, w_up, w_down = gate_weight[0], up_weight[0], down_weight[0]
    plain = list(range(n_chip))
    top = n_chip // 2
    share = CAP * BLK // GROUPS // n_chip

    def make_place():
        return Place(n_bits, n_expert)

    last = n_chip - 1
    sides = (context, context_other)
    (total,) = project(make_place, plain[:top], None, *sides, pieces[: 2 * top], ())
    total, columns = project(
        make_place, plain[top:last], last, *sides, pieces[2 * top : 2 * last], (total,)
    )
    attended = project_last(columns, total, residual_own, residual_other, pieces[2 * last :])

    layouts = [Layout(group, n_chip, local_blocks) for group in range(GROUPS)]
    grains = attended.reshape(-1, share, half)
    values = gate_values

    scope = (make_place, n_dp, n_bits, n_expert, half, reverse, to_partner)
    tables = (chosen_blocks, block_counts, values, w_gate, w_up, w_down)
    groups = [group_steps(layout, scope, tables, grains) for layout in layouts]
    for group in groups:
        next(group)
    after, received = None, [None] * GROUPS
    turn = 0
    while any(done is None for done in received):
        g = int(ORDER[turn]) if turn < len(ORDER) else turn % GROUPS
        turn += 1
        if received[g] is None:
            after, received[g] = groups[g].send(after)

    total, n = grains, grains.shape[0]
    for layout, got in zip(layouts[:-1], received[:-1]):
        total = finish(make_place, layout, n_chip, chosen_blocks, total, got, 0, n, False)
    last = (make_place, layouts[-1], n_chip, chosen_blocks, total, received[-1])
    other = finish(*last, n // 2, n, True)
    own = finish(*last, 0, n // 2, True)
    return join(make_place, own, to_partner(other), local_tokens)


def solution(mesh):
    in_specs = (
        P("dp", None),
        P("dp", "expert"),
        P("dp", "expert"),
        P("expert", None, "dp"),
        P("expert", None, "dp"),
        P("expert", "dp", None),
        P("expert", None),
        P(),
        P(),
    )
    out_specs = P("dp", "expert")
    return jax.shard_map(body, mesh=mesh, in_specs=in_specs, out_specs=out_specs, check_vma=False)
```

```python
import jax
import jax.numpy as jnp
from jax import lax
from jax.experimental import pallas as pl
from jax.experimental.pallas import tpu as pltpu
from jax.sharding import PartitionSpec as P

BLK = 128
CAP = 4
GROUPS = 2
DIRECT = ((0, 0, 0, 0), (0, 1, 1, 0))
PICK_WAIT = (0, 0)
HOP_WAIT = ((0, 0), (0, 0))
ORDER = '001010110000101011011011'


def bit_orders(n_bits):
    forward = list(range(1, n_bits + 1))
    return forward, forward[::-1]


def step_pairs(n_dp, step):
    orders = bit_orders(n_dp.bit_length() - 2)
    return [(i, i ^ (1 << orders[i & 1][step])) for i in range(n_dp)]


def pair_pairs(n_dp):
    return [(i, i ^ 1) for i in range(n_dp)]


def masks_of(n_bits, side):
    order = bit_orders(n_bits)[side]
    return [
        sum(1 << (order[t] - 1) for t in range(n_bits) if (r >> t) & 1) for r in range(1 << n_bits)
    ]


def bit_reversed(n_bits):
    return [
        sum(1 << (n_bits - 1 - t) for t in range(n_bits) if (r >> t) & 1)
        for r in range(1 << n_bits)
    ]


SMEM = pl.BlockSpec(memory_space=pltpu.SMEM)
VMEM = pl.BlockSpec(memory_space=pltpu.VMEM)
ANY = pl.BlockSpec(memory_space=pl.ANY)
MIB = 1024 * 1024


def exchange(value, n_dp, step):
    return lax.ppermute(value, "dp", step_pairs(n_dp, step))


def gather_steps(piece, n_dp, n_bits):
    pieces = [piece]
    for step in range(n_bits):
        pieces = pieces + [exchange(p, n_dp, step) for p in pieces]
    return pieces


def gather(piece, n_dp, n_bits, at_once):
    if at_once:
        return direct([piece] * (1 << n_bits), n_dp, n_bits)
    return gather_steps(piece, n_dp, n_bits)


def scatter(terms, n_dp, n_bits, at_once, hop_wait, wait, after):
    if at_once:
        if len(terms[0]) > 1:
            terms = [[t] for t in add_terms(terms, [after])]
            after = yield terms[0][0], None
        got = direct([t[0] for t in terms], n_dp, n_bits)
        if wait:
            after = yield got[1], None
        mine = add_terms([got], [after])[0]
        after = yield mine, None
        return mine, after
    for step in range(n_bits - 1, -1, -1):
        half_way = 1 << step
        send = [t[0] for t in terms[half_way:]]
        if len(terms[half_way]) > 1:
            others = [t[-1] for t in terms[:half_way]] if hop_wait else []
            send = add_terms(terms[half_way:], [after] + others)
            after = yield send[0], None
        terms = [t + [exchange(s, n_dp, step)] for t, s in zip(terms, send)]
        if wait and step == n_bits - 1:
            after = yield terms[half_way - 1][-1], None
    mine = add_terms(terms, [after])[0]
    after = yield mine, None
    return mine, after


def direct(values, n_dp, n_bits):
    masks = [masks_of(n_bits, side) for side in (0, 1)]
    out = []
    for r, value in enumerate(values):
        pairs = [(i, i ^ (masks[i & 1][r] << 1)) for i in range(n_dp)]
        out.append(lax.ppermute(value, "dp", pairs) if r else value)
    return out


def swap_planes(parts, n_expert, after=None):
    out = [parts[0]]
    for k in range(1, n_expert):
        pairs = [(i, (i + k) % n_expert) for i in range(n_expert)]
        out.append(lax.ppermute(parts[k], "expert", pairs))
    return stack(out, after)


def call(kernel, out_shape, in_specs, out_specs, name, limit, **more):
    return pl.pallas_call(
        kernel,
        out_shape=out_shape,
        in_specs=in_specs,
        out_specs=out_specs,
        compiler_params=pltpu.CompilerParams(vmem_limit_bytes=limit * MIB),
        name=name,
        **more,
    )


def add_kernel(counts, *refs):
    at, outs = sum(counts), refs[-len(counts) :]
    terms = iter(refs[:at])
    for n, out in zip(counts, outs):
        total = next(terms)[...].astype(jnp.float32)
        for _ in range(n - 1):
            total = total + next(terms)[...].astype(jnp.float32)
        out[...] = total.astype(out.dtype)


def add_terms(terms, unread):
    counts = [len(t) for t in terms]
    shapes = [jax.ShapeDtypeStruct(t[0].shape, t[0].dtype) for t in terms]
    return call(
        lambda *refs: add_kernel(counts, *refs),
        shapes,
        [VMEM] * sum(counts) + [ANY] * len(unread),
        [VMEM] * len(counts),
        "add_terms",
        8,
    )(*[x for t in terms for x in t], *unread)


def stack_kernel(n, *refs):
    for i in range(n):
        refs[-1][i] = refs[i][...]


def stack(parts, after):
    extra = [] if after is None else [after]
    return call(
        lambda *refs: stack_kernel(len(parts), *refs),
        jax.ShapeDtypeStruct((len(parts),) + parts[0].shape, parts[0].dtype),
        [VMEM] * len(parts) + [ANY] * len(extra),
        VMEM,
        "stack_planes",
        8,
    )(*parts, *extra)


class Place:
    def __init__(self, n_bits, n_expert):
        data = lax.axis_index("dp")
        self.chip, self.side = lax.div(data, 2), lax.rem(data, 2)
        self.expert = lax.axis_index("expert")
        self.n_expert = n_expert
        self.n_bits = n_bits

    def chip_at(self, r):
        first, second = (masks_of(self.n_bits, s)[r] for s in (0, 1))
        return self.chip ^ jnp.where(self.side == 0, first, second)

    def ahead(self, k):
        return lax.rem(self.expert + k, self.n_expert)

    def behind(self, k):
        return lax.rem(self.expert + (self.n_expert - k), self.n_expert)


class Layout:
    def __init__(self, group, n_chip, local_blocks):
        self.rows = CAP * BLK // GROUPS
        self.share = self.rows // n_chip
        self.group, self.local_blocks = group, local_blocks

    def first_row(self, place, r):
        return self.group * self.rows + place.chip_at(r) * self.share

    def grain(self, place, chosen, r, expert):
        row = self.first_row(place, r)
        block = chosen[expert, lax.div(row, BLK)]
        owner = lax.div(block, self.local_blocks)
        base = jnp.where(lax.rem(owner, 2) == place.side, 0, self.local_blocks)
        base = base + lax.rem(block, self.local_blocks)
        index = base * (BLK // self.share) + lax.div(lax.rem(row, BLK), self.share)
        return index, lax.div(owner, 2) == place.chip


def project_kernel(make_place, parts, ahead, n_w, n_res, n_unread, *refs):
    context, other = refs[:2]
    weights = refs[2 : 2 + n_w]
    extra = refs[2 + n_w : 2 + n_w + n_res]
    outs, (w_all, c_own, c_other, sems) = refs[2 + n_w + n_res + n_unread : -4], refs[-4:]
    depth = weights[0].shape[0]
    place = make_place()

    def fetch(r, src, dst, at, sem):
        copies = []
        for s in range(2):
            column = (place.chip_at(r) * 2 + (place.side ^ s)) * depth
            column = pl.ds(pl.multiple_of(column, depth), depth)
            n = at + s
            copy = pltpu.make_async_copy(
                src.at[:, column], dst.at[:, n * depth : (n + 1) * depth], sem.at[n]
            )
            copy.start()
            copies.append(copy)
        return copies

    copies = []
    for i, (src, dst) in enumerate(((context, c_own), (other, c_other))):
        for j, r in enumerate(parts):
            copies += fetch(r, src, dst, 2 * j, sems.at[i])
    later = []
    if ahead is not None:
        for i, src in enumerate((context, other)):
            later += fetch(ahead, src, outs[1].at[i], 0, sems.at[2 + i])
    for i, w in enumerate(weights):
        w_all[i * depth : (i + 1) * depth, :] = w[...]
    for i, c in enumerate((c_own, c_other)):
        for copy in copies[i * n_w : (i + 1) * n_w]:
            copy.wait()
        value = jnp.dot(c[...], w_all[...], preferred_element_type=jnp.float32)
        if n_res > 0:
            value = value + extra[0][i]
        outs[0][i] = value
    for copy in later:
        copy.wait()


def project(make_place, parts, ahead, own, other, weights, extra, unread):
    rows = own.shape[0]
    depth, half = weights[0].shape
    k = depth * len(weights)
    shapes = [jax.ShapeDtypeStruct((2, rows, half), jnp.float32)]
    if ahead is not None:
        shapes.append(jax.ShapeDtypeStruct((2, rows, 2 * depth), own.dtype))
    return call(
        lambda *refs: project_kernel(
            make_place, parts, ahead, len(weights), len(extra), len(unread), *refs
        ),
        shapes,
        [ANY, ANY] + [VMEM] * (len(weights) + len(extra)) + [ANY] * len(unread),
        [VMEM] * len(shapes),
        "project",
        12,
        scratch_shapes=[
            pltpu.VMEM((k, half), jnp.bfloat16),
            pltpu.VMEM((rows, k), jnp.bfloat16),
            pltpu.VMEM((rows, k), jnp.bfloat16),
            pltpu.SemaphoreType.DMA((4, len(weights))),
        ],
    )(own, other, *weights, *extra, *unread)


def project_last_kernel(columns, total, own, other, *refs):
    weights, out, w_all = refs[:-2], refs[-2], refs[-1]
    depth = weights[0].shape[0]
    for i, w in enumerate(weights):
        w_all[i * depth : (i + 1) * depth, :] = w[...]
    for i, res in enumerate((own, other)):
        value = jnp.dot(columns[i], w_all[...], preferred_element_type=jnp.float32)
        out[i] = (value + total[i] + res[...].astype(jnp.float32)).astype(out.dtype)


def project_last(columns, total, own, other, weights):
    depth, half = weights[0].shape
    return call(
        project_last_kernel,
        jax.ShapeDtypeStruct(total.shape, jnp.bfloat16),
        [VMEM] * (4 + len(weights)),
        VMEM,
        "project_last",
        12,
        scratch_shapes=[pltpu.VMEM((depth * len(weights), half), jnp.bfloat16)],
    )(columns, total, own, other, *weights)


def pick_kernel(make_place, layout, n_chip, chosen, att_ref, *refs):
    place = make_place()
    outs = refs[-n_chip:]
    for r in range(n_chip):
        for k in range(place.n_expert):
            index, mine = layout.grain(place, chosen, r, place.ahead(k))
            value = att_ref[jnp.where(mine, index, 0)]
            outs[r][k] = jnp.where(mine, value, jnp.zeros_like(value))


def pick(make_place, layout, n_chip, n_expert, chosen, grains, after):
    shape = jax.ShapeDtypeStruct((n_expert,) + grains.shape[1:], grains.dtype)
    extra = [] if after is None else [after]
    return call(
        lambda *refs: pick_kernel(make_place, layout, n_chip, *refs),
        [shape] * n_chip,
        [SMEM, VMEM] + [ANY] * len(extra),
        [VMEM] * n_chip,
        "pick_blocks",
        8,
    )(chosen, grains, *extra)


def finish_kernel(make_place, layout, n_chip, lo, hi, chosen, *refs):
    pieces, old, out = refs[:n_chip], refs[n_chip], refs[n_chip + 1]
    acc = refs[-1]
    place = make_place()
    acc[...] = old[lo:hi].astype(jnp.float32)
    for r in range(n_chip):
        for k in range(place.n_expert):
            index, mine = layout.grain(place, chosen, r, place.behind(k))

            @pl.when(mine & (index >= lo) & (index < hi))
            def _():
                acc[index - lo] = acc[index - lo] + pieces[r][k].astype(jnp.float32)

    if acc is not out:
        out[...] = acc[...].astype(out.dtype)


def finish(make_place, layout, n_chip, chosen, old, pieces, lo, hi, last):
    dtype = jnp.bfloat16 if last else jnp.float32
    shape = (hi - lo,) + old.shape[1:]
    return call(
        lambda *refs: finish_kernel(make_place, layout, n_chip, lo, hi, *refs),
        jax.ShapeDtypeStruct(shape, dtype),
        [SMEM] + [VMEM] * (len(pieces) + 1),
        VMEM,
        "add_expert_rows",
        8,
        scratch_shapes=[pltpu.VMEM(shape, jnp.float32)] if last else (),
    )(chosen, *pieces, old)


def join_kernel(make_place, own, other, out):
    side = make_place().side
    rows, half = out.shape[0], out.shape[1] // 2
    for s, value in enumerate((own, other)):
        at = pl.ds(pl.multiple_of((side ^ s) * half, half), half)
        out[:, at] = value[...].reshape(rows, half)


def join(make_place, own, other, rows):
    return call(
        lambda *refs: join_kernel(make_place, *refs),
        jax.ShapeDtypeStruct((rows, 2 * own.shape[-1]), own.dtype),
        [VMEM, VMEM],
        VMEM,
        "join_halves",
        8,
    )(own, other)


def hidden_kernel(make_place, reverse, own, other, wg, wu, after, hid, xs):
    n_z, rows, width = own.shape[1:]
    place = make_place()
    for s, pieces in enumerate((own, other)):
        for z in range(n_z):
            at = (place.behind(z) * 2 + (place.side ^ s)) * width
            at = pl.ds(pl.multiple_of(at, width), width)
            for r, to in enumerate(reverse):
                to = to if s else r
                xs[to * rows : (to + 1) * rows, at] = pieces[r, z]
    ff = wg.shape[1]
    tile = min(ff, 1024)

    def one(i, carry):
        at = pl.ds(pl.multiple_of(i * tile, tile), tile)
        g = jnp.dot(xs[...], wg[:, at], preferred_element_type=jnp.float32)
        u = jnp.dot(xs[...], wu[:, at], preferred_element_type=jnp.float32)
        hid[:, at] = (g / (1.0 + jnp.exp(-g)) * u).astype(jnp.bfloat16)
        return carry

    lax.fori_loop(0, ff // tile, one, 0)


def hidden_units(make_place, reverse, own, other, w_gate, w_up, after):
    n_row = own.shape[0] * own.shape[2]
    model_width, ff = w_gate.shape
    return call(
        lambda *refs: hidden_kernel(make_place, reverse, *refs),
        jax.ShapeDtypeStruct((n_row, ff), jnp.bfloat16),
        [VMEM] * 4 + [ANY],
        VMEM,
        "expert_hidden",
        12,
        scratch_shapes=[pltpu.VMEM((n_row, model_width), jnp.bfloat16)],
    )(own, other, w_gate, w_up, after)


def scale_kernel(make_place, layouts, n_chip, counts, values, *outs):
    place = make_place()
    count = counts[place.expert]
    rows, n_row = layouts[0].share, values.shape[1]
    row_of = lax.broadcasted_iota(jnp.int32, (rows, n_row), 0)
    at_of = lax.broadcasted_iota(jnp.int32, (rows, n_row), 1)
    for layout, out in zip(layouts, outs):
        for r in range(n_chip):
            row = layout.first_row(place, r)
            chosen = (at_of == row_of + row) & (lax.div(row, BLK) < count)
            scale = jnp.sum(jnp.where(chosen, values[...], 0.0), axis=1, keepdims=True)
            out[r * rows : (r + 1) * rows, :] = scale


def scales(make_place, layouts, n_chip, counts, values):
    shape = jax.ShapeDtypeStruct((n_chip * layouts[0].share, 1), jnp.float32)
    return call(
        lambda *refs: scale_kernel(make_place, layouts, n_chip, *refs),
        [shape] * len(layouts),
        [SMEM, VMEM],
        [VMEM] * len(layouts),
        "row_scales",
        4,
    )(counts, values)


def down_kernel(make_place, layout, order, s, hid, wd, scale, after, *outs):
    n = len(order)
    n_z, rows, width = outs[0].shape
    place = make_place()
    for z in range(n_z):
        at = (place.ahead(z) * 2 + (place.side ^ s)) * width
        at = pl.ds(pl.multiple_of(at, width), width)
        part = jnp.dot(hid[...], wd[:, at], preferred_element_type=jnp.float32)
        for r in range(n):
            value = part[r * rows : (r + 1) * rows] * scale[r * rows : (r + 1) * rows]
            outs[order[r]][z] = value.astype(jnp.bfloat16)


def down(make_place, layout, order, s, n_z, width, hid, w_down, scale, after):
    n = len(order)
    return call(
        lambda *refs: down_kernel(make_place, layout, order, s, *refs),
        [jax.ShapeDtypeStruct((n_z, layout.share, width), jnp.bfloat16)] * n,
        [VMEM] * 3 + [ANY],
        [VMEM] * n,
        "expert_down",
        8,
    )(hid, w_down, scale, after)


def group_steps(layout, scope, tables, grains):
    make_place, n_dp, n_bits, n_expert, half, reverse, to_partner = scope
    chosen, scale, w_gate, w_up, w_down = tables
    n_chip = 1 << n_bits
    plain = list(range(n_chip))
    after = yield
    modes, hop_wait = DIRECT[layout.group], HOP_WAIT[layout.group]
    terms = [[p] for p in pick(make_place, layout, n_chip, n_expert, chosen, grains, after)]
    if not PICK_WAIT[layout.group]:
        after = yield terms[0][0], None
    mine, after = yield from scatter(
        terms, n_dp, n_bits, modes[0], hop_wait[0], PICK_WAIT[layout.group], after
    )
    crossed = swap_planes(mine, n_expert, after)
    own_half = gather(crossed, n_dp, n_bits, modes[1])
    after = yield crossed, None
    own = stack(own_half, after)
    other = to_partner(own)
    after = yield own, None
    hid = hidden_units(make_place, reverse, own, other, w_gate, w_up, after)
    after = yield hid, None

    def downs(order, s):
        return down(
            make_place, layout, order, s, n_expert, half, hid, w_down, scale[layout.group], after
        )

    theirs = downs(reverse, 1)
    after = yield theirs[0], None
    mine = downs(plain, 0)
    after = yield mine[0], None
    terms = [[m, to_partner(t)] for m, t in zip(mine, theirs)]
    mine, after = yield from scatter(terms, n_dp, n_bits, modes[2], hop_wait[1], 0, after)
    crossed = swap_planes(mine, n_expert, after)
    yield crossed, gather(crossed, n_dp, n_bits, modes[3])


def body(
    context,
    out_weight,
    residual,
    gate_weight,
    up_weight,
    down_weight,
    gate_values,
    chosen_blocks,
    block_counts,
):
    n_expert = lax.axis_size("expert")
    n_dp = lax.axis_size("dp")
    n_bits = n_dp.bit_length() - 2
    n_chip = 1 << n_bits
    local_tokens, model_width = context.shape
    local_width = residual.shape[1]
    half = local_width // 2
    depth = out_weight.shape[0]
    local_blocks = local_tokens // BLK
    place = Place(n_bits, n_expert)
    side = place.side
    reverse = bit_reversed(n_bits)
    pair = pair_pairs(n_dp)

    def to_partner(value):
        return lax.ppermute(value, "dp", pair)

    def split_sides(value):
        own = lax.dynamic_slice_in_dim(value, side * half, half, axis=1)
        other = lax.dynamic_slice_in_dim(value, (1 - side) * half, half, axis=1)
        return own, to_partner(other)

    w_own, w_other = split_sides(out_weight)
    pieces = [(w_own, w_other)]
    for step in range(n_bits):
        pieces = pieces + [tuple(exchange(w, n_dp, step) for w in p) for p in pieces]
    pieces = [w for p in pieces for w in p]
    context_other = to_partner(context)
    residual_own, residual_other = split_sides(residual)
    w_gate, w_up, w_down = gate_weight[0], up_weight[0], down_weight[0]
    plain = list(range(n_chip))
    top = n_chip // 2
    share = CAP * BLK // GROUPS // n_chip

    def make_place():
        return Place(n_bits, n_expert)

    layouts = [Layout(group, n_chip, local_blocks) for group in range(GROUPS)]
    factors = scales(make_place, layouts, n_chip, block_counts, gate_values)
    last = n_chip - 1
    sides = (context, context_other)
    (total,) = project(make_place, plain[:top], None, *sides, pieces[: 2 * top], (), factors)
    total, columns = project(
        make_place, plain[top:last], last, *sides, pieces[2 * top : 2 * last], (total,), ()
    )
    attended = project_last(columns, total, residual_own, residual_other, pieces[2 * last :])

    grains = attended.reshape(-1, share, half)

    scope = (make_place, n_dp, n_bits, n_expert, half, reverse, to_partner)
    tables = (chosen_blocks, factors, w_gate, w_up, w_down)
    groups = [group_steps(layout, scope, tables, grains) for layout in layouts]
    for group in groups:
        next(group)
    after, received = None, [None] * GROUPS
    turn = 0
    while any(done is None for done in received):
        g = int(ORDER[turn]) if turn < len(ORDER) else turn % GROUPS
        turn += 1
        if received[g] is None:
            after, received[g] = groups[g].send(after)

    total, n = grains, grains.shape[0]
    for layout, got in zip(layouts[:-1], received[:-1]):
        total = finish(make_place, layout, n_chip, chosen_blocks, total, got, 0, n, False)
    last = (make_place, layouts[-1], n_chip, chosen_blocks, total, received[-1])
    other = finish(*last, n // 2, n, True)
    own = finish(*last, 0, n // 2, True)
    return join(make_place, own, to_partner(other), local_tokens)


def solution(mesh):
    in_specs = (
        P("dp", None),
        P("dp", "expert"),
        P("dp", "expert"),
        P("expert", None, "dp"),
        P("expert", None, "dp"),
        P("expert", "dp", None),
        P("expert", None),
        P(),
        P(),
    )
    out_specs = P("dp", "expert")
    return jax.shard_map(body, mesh=mesh, in_specs=in_specs, out_specs=out_specs, check_vma=False)
```

```python
import jax
import jax.numpy as jnp
from jax import lax
from jax.experimental import pallas as pl
from jax.experimental.pallas import tpu as pltpu
from jax.sharding import PartitionSpec as P

BLK = 128
CAP = 4
GROUPS = 2
DIRECT = ((0, 0, 0, 0), (0, 1, 1, 1))
PICK_WAIT = (0, 0)
HOP_WAIT = ((0, 0), (0, 0))
ORDER = '001010110000101011011011'


def bit_orders(n_bits):
    forward = list(range(1, n_bits + 1))
    return forward, forward[::-1]


def step_pairs(n_dp, step):
    orders = bit_orders(n_dp.bit_length() - 2)
    return [(i, i ^ (1 << orders[i & 1][step])) for i in range(n_dp)]


def pair_pairs(n_dp):
    return [(i, i ^ 1) for i in range(n_dp)]


def masks_of(n_bits, side):
    order = bit_orders(n_bits)[side]
    return [
        sum(1 << (order[t] - 1) for t in range(n_bits) if (r >> t) & 1) for r in range(1 << n_bits)
    ]


def bit_reversed(n_bits):
    return [
        sum(1 << (n_bits - 1 - t) for t in range(n_bits) if (r >> t) & 1)
        for r in range(1 << n_bits)
    ]


SMEM = pl.BlockSpec(memory_space=pltpu.SMEM)
VMEM = pl.BlockSpec(memory_space=pltpu.VMEM)
ANY = pl.BlockSpec(memory_space=pl.ANY)
MIB = 1024 * 1024


def exchange(value, n_dp, step):
    return lax.ppermute(value, "dp", step_pairs(n_dp, step))


def gather_steps(piece, n_dp, n_bits):
    pieces = [piece]
    for step in range(n_bits):
        pieces = pieces + [exchange(p, n_dp, step) for p in pieces]
    return pieces


def gather(piece, n_dp, n_bits, at_once):
    if at_once:
        return direct([piece] * (1 << n_bits), n_dp, n_bits)
    return gather_steps(piece, n_dp, n_bits)


def scatter(terms, n_dp, n_bits, at_once, hop_wait, wait, after):
    if at_once:
        if len(terms[0]) > 1:
            terms = [[t] for t in add_terms(terms, [after])]
            after = yield terms[0][0], None
        got = direct([t[0] for t in terms], n_dp, n_bits)
        if wait:
            after = yield got[1], None
        mine = add_terms([got], [after])[0]
        after = yield mine, None
        return mine, after
    for step in range(n_bits - 1, -1, -1):
        half_way = 1 << step
        send = [t[0] for t in terms[half_way:]]
        if len(terms[half_way]) > 1:
            others = [t[-1] for t in terms[:half_way]] if hop_wait else []
            send = add_terms(terms[half_way:], [after] + others)
            after = yield send[0], None
        terms = [t + [exchange(s, n_dp, step)] for t, s in zip(terms, send)]
        if wait and step == n_bits - 1:
            after = yield terms[half_way - 1][-1], None
    mine = add_terms(terms, [after])[0]
    after = yield mine, None
    return mine, after


def direct(values, n_dp, n_bits):
    masks = [masks_of(n_bits, side) for side in (0, 1)]
    out = []
    for r, value in enumerate(values):
        pairs = [(i, i ^ (masks[i & 1][r] << 1)) for i in range(n_dp)]
        out.append(lax.ppermute(value, "dp", pairs) if r else value)
    return out


def swap_planes(parts, n_expert, after=None):
    out = [parts[0]]
    for k in range(1, n_expert):
        pairs = [(i, (i + k) % n_expert) for i in range(n_expert)]
        out.append(lax.ppermute(parts[k], "expert", pairs))
    return stack(out, after)


def call(kernel, out_shape, in_specs, out_specs, name, limit, **more):
    return pl.pallas_call(
        kernel,
        out_shape=out_shape,
        in_specs=in_specs,
        out_specs=out_specs,
        compiler_params=pltpu.CompilerParams(vmem_limit_bytes=limit * MIB),
        name=name,
        **more,
    )


def add_kernel(counts, *refs):
    at, outs = sum(counts), refs[-len(counts) :]
    terms = iter(refs[:at])
    for n, out in zip(counts, outs):
        total = next(terms)[...].astype(jnp.float32)
        for _ in range(n - 1):
            total = total + next(terms)[...].astype(jnp.float32)
        out[...] = total.astype(out.dtype)


def add_terms(terms, unread):
    counts = [len(t) for t in terms]
    shapes = [jax.ShapeDtypeStruct(t[0].shape, t[0].dtype) for t in terms]
    return call(
        lambda *refs: add_kernel(counts, *refs),
        shapes,
        [VMEM] * sum(counts) + [ANY] * len(unread),
        [VMEM] * len(counts),
        "add_terms",
        8,
    )(*[x for t in terms for x in t], *unread)


def stack_kernel(n, *refs):
    for i in range(n):
        refs[-1][i] = refs[i][...]


def stack(parts, after):
    extra = [] if after is None else [after]
    return call(
        lambda *refs: stack_kernel(len(parts), *refs),
        jax.ShapeDtypeStruct((len(parts),) + parts[0].shape, parts[0].dtype),
        [VMEM] * len(parts) + [ANY] * len(extra),
        VMEM,
        "stack_planes",
        8,
    )(*parts, *extra)


class Place:
    def __init__(self, n_bits, n_expert):
        data = lax.axis_index("dp")
        self.chip, self.side = lax.div(data, 2), lax.rem(data, 2)
        self.expert = lax.axis_index("expert")
        self.n_expert = n_expert
        self.n_bits = n_bits

    def chip_at(self, r):
        first, second = (masks_of(self.n_bits, s)[r] for s in (0, 1))
        return self.chip ^ jnp.where(self.side == 0, first, second)

    def ahead(self, k):
        return lax.rem(self.expert + k, self.n_expert)

    def behind(self, k):
        return lax.rem(self.expert + (self.n_expert - k), self.n_expert)


class Layout:
    def __init__(self, group, n_chip, local_blocks):
        self.rows = CAP * BLK // GROUPS
        self.share = self.rows // n_chip
        self.group, self.local_blocks = group, local_blocks

    def first_row(self, place, r):
        return self.group * self.rows + place.chip_at(r) * self.share

    def grain(self, place, chosen, r, expert):
        row = self.first_row(place, r)
        block = chosen[expert, lax.div(row, BLK)]
        owner = lax.div(block, self.local_blocks)
        base = jnp.where(lax.rem(owner, 2) == place.side, 0, self.local_blocks)
        base = base + lax.rem(block, self.local_blocks)
        index = base * (BLK // self.share) + lax.div(lax.rem(row, BLK), self.share)
        return index, lax.div(owner, 2) == place.chip


def project_kernel(make_place, parts, ahead, n_w, n_res, n_unread, *refs):
    context, other = refs[:2]
    weights = refs[2 : 2 + n_w]
    extra = refs[2 + n_w : 2 + n_w + n_res]
    outs, (w_all, c_own, c_other, sems) = refs[2 + n_w + n_res + n_unread : -4], refs[-4:]
    depth = weights[0].shape[0]
    place = make_place()

    def fetch(r, src, dst, at, sem):
        copies = []
        for s in range(2):
            column = (place.chip_at(r) * 2 + (place.side ^ s)) * depth
            column = pl.ds(pl.multiple_of(column, depth), depth)
            n = at + s
            copy = pltpu.make_async_copy(
                src.at[:, column], dst.at[:, n * depth : (n + 1) * depth], sem.at[n]
            )
            copy.start()
            copies.append(copy)
        return copies

    copies = []
    for i, (src, dst) in enumerate(((context, c_own), (other, c_other))):
        for j, r in enumerate(parts):
            copies += fetch(r, src, dst, 2 * j, sems.at[i])
    later = []
    if ahead is not None:
        for i, src in enumerate((context, other)):
            later += fetch(ahead, src, outs[1].at[i], 0, sems.at[2 + i])
    for i, w in enumerate(weights):
        w_all[i * depth : (i + 1) * depth, :] = w[...]
    for i, c in enumerate((c_own, c_other)):
        for copy in copies[i * n_w : (i + 1) * n_w]:
            copy.wait()
        value = jnp.dot(c[...], w_all[...], preferred_element_type=jnp.float32)
        if n_res > 0:
            value = value + extra[0][i]
        outs[0][i] = value
    for copy in later:
        copy.wait()


def project(make_place, parts, ahead, own, other, weights, extra, unread):
    rows = own.shape[0]
    depth, half = weights[0].shape
    k = depth * len(weights)
    shapes = [jax.ShapeDtypeStruct((2, rows, half), jnp.float32)]
    if ahead is not None:
        shapes.append(jax.ShapeDtypeStruct((2, rows, 2 * depth), own.dtype))
    return call(
        lambda *refs: project_kernel(
            make_place, parts, ahead, len(weights), len(extra), len(unread), *refs
        ),
        shapes,
        [ANY, ANY] + [VMEM] * (len(weights) + len(extra)) + [ANY] * len(unread),
        [VMEM] * len(shapes),
        "project",
        12,
        scratch_shapes=[
            pltpu.VMEM((k, half), jnp.bfloat16),
            pltpu.VMEM((rows, k), jnp.bfloat16),
            pltpu.VMEM((rows, k), jnp.bfloat16),
            pltpu.SemaphoreType.DMA((4, len(weights))),
        ],
    )(own, other, *weights, *extra, *unread)


def project_last_kernel(columns, total, own, other, *refs):
    weights, out, w_all = refs[:-2], refs[-2], refs[-1]
    depth = weights[0].shape[0]
    for i, w in enumerate(weights):
        w_all[i * depth : (i + 1) * depth, :] = w[...]
    for i, res in enumerate((own, other)):
        value = jnp.dot(columns[i], w_all[...], preferred_element_type=jnp.float32)
        out[i] = (value + total[i] + res[...].astype(jnp.float32)).astype(out.dtype)


def project_last(columns, total, own, other, weights):
    depth, half = weights[0].shape
    return call(
        project_last_kernel,
        jax.ShapeDtypeStruct(total.shape, jnp.bfloat16),
        [VMEM] * (4 + len(weights)),
        VMEM,
        "project_last",
        12,
        scratch_shapes=[pltpu.VMEM((depth * len(weights), half), jnp.bfloat16)],
    )(columns, total, own, other, *weights)


def pick_kernel(make_place, layout, n_chip, chosen, att_ref, *refs):
    place = make_place()
    outs = refs[-n_chip:]
    for r in range(n_chip):
        for k in range(place.n_expert):
            index, mine = layout.grain(place, chosen, r, place.ahead(k))
            value = att_ref[jnp.where(mine, index, 0)]
            outs[r][k] = jnp.where(mine, value, jnp.zeros_like(value))


def pick(make_place, layout, n_chip, n_expert, chosen, grains, after):
    shape = jax.ShapeDtypeStruct((n_expert,) + grains.shape[1:], grains.dtype)
    extra = [] if after is None else [after]
    return call(
        lambda *refs: pick_kernel(make_place, layout, n_chip, *refs),
        [shape] * n_chip,
        [SMEM, VMEM] + [ANY] * len(extra),
        [VMEM] * n_chip,
        "pick_blocks",
        8,
    )(chosen, grains, *extra)


def finish_kernel(make_place, layout, n_chip, lo, hi, chosen, *refs):
    pieces, old, out = refs[:n_chip], refs[n_chip], refs[n_chip + 1]
    acc = refs[-1]
    place = make_place()
    acc[...] = old[lo:hi].astype(jnp.float32)
    for r in range(n_chip):
        for k in range(place.n_expert):
            index, mine = layout.grain(place, chosen, r, place.behind(k))

            @pl.when(mine & (index >= lo) & (index < hi))
            def _():
                acc[index - lo] = acc[index - lo] + pieces[r][k].astype(jnp.float32)

    if acc is not out:
        out[...] = acc[...].astype(out.dtype)


def finish(make_place, layout, n_chip, chosen, old, pieces, lo, hi, last):
    dtype = jnp.bfloat16 if last else jnp.float32
    shape = (hi - lo,) + old.shape[1:]
    return call(
        lambda *refs: finish_kernel(make_place, layout, n_chip, lo, hi, *refs),
        jax.ShapeDtypeStruct(shape, dtype),
        [SMEM] + [VMEM] * (len(pieces) + 1),
        VMEM,
        "add_expert_rows",
        8,
        scratch_shapes=[pltpu.VMEM(shape, jnp.float32)] if last else (),
    )(chosen, *pieces, old)


def join_kernel(make_place, own, other, out):
    side = make_place().side
    rows, half = out.shape[0], out.shape[1] // 2
    for s, value in enumerate((own, other)):
        at = pl.ds(pl.multiple_of((side ^ s) * half, half), half)
        out[:, at] = value[...].reshape(rows, half)


def join(make_place, own, other, rows):
    return call(
        lambda *refs: join_kernel(make_place, *refs),
        jax.ShapeDtypeStruct((rows, 2 * own.shape[-1]), own.dtype),
        [VMEM, VMEM],
        VMEM,
        "join_halves",
        8,
    )(own, other)


def hidden_kernel(make_place, reverse, own, other, wg, wu, after, hid, xs):
    n_z, rows, width = own.shape[1:]
    place = make_place()
    for s, pieces in enumerate((own, other)):
        for z in range(n_z):
            at = (place.behind(z) * 2 + (place.side ^ s)) * width
            at = pl.ds(pl.multiple_of(at, width), width)
            for r, to in enumerate(reverse):
                to = to if s else r
                xs[to * rows : (to + 1) * rows, at] = pieces[r, z]
    ff = wg.shape[1]
    tile = min(ff, 1024)

    def one(i, carry):
        at = pl.ds(pl.multiple_of(i * tile, tile), tile)
        g = jnp.dot(xs[...], wg[:, at], preferred_element_type=jnp.float32)
        u = jnp.dot(xs[...], wu[:, at], preferred_element_type=jnp.float32)
        hid[:, at] = (g / (1.0 + jnp.exp(-g)) * u).astype(jnp.bfloat16)
        return carry

    lax.fori_loop(0, ff // tile, one, 0)


def hidden_units(make_place, reverse, own, other, w_gate, w_up, after):
    n_row = own.shape[0] * own.shape[2]
    model_width, ff = w_gate.shape
    return call(
        lambda *refs: hidden_kernel(make_place, reverse, *refs),
        jax.ShapeDtypeStruct((n_row, ff), jnp.bfloat16),
        [VMEM] * 4 + [ANY],
        VMEM,
        "expert_hidden",
        12,
        scratch_shapes=[pltpu.VMEM((n_row, model_width), jnp.bfloat16)],
    )(own, other, w_gate, w_up, after)


def scale_kernel(make_place, layouts, n_chip, counts, values, *outs):
    place = make_place()
    count = counts[place.expert]
    rows, n_row = layouts[0].share, values.shape[1]
    row_of = lax.broadcasted_iota(jnp.int32, (rows, n_row), 0)
    at_of = lax.broadcasted_iota(jnp.int32, (rows, n_row), 1)
    for layout, out in zip(layouts, outs):
        for r in range(n_chip):
            row = layout.first_row(place, r)
            chosen = (at_of == row_of + row) & (lax.div(row, BLK) < count)
            scale = jnp.sum(jnp.where(chosen, values[...], 0.0), axis=1, keepdims=True)
            out[r * rows : (r + 1) * rows, :] = scale


def scales(make_place, layouts, n_chip, counts, values):
    shape = jax.ShapeDtypeStruct((n_chip * layouts[0].share, 1), jnp.float32)
    return call(
        lambda *refs: scale_kernel(make_place, layouts, n_chip, *refs),
        [shape] * len(layouts),
        [SMEM, VMEM],
        [VMEM] * len(layouts),
        "row_scales",
        4,
    )(counts, values)


def down_kernel(make_place, layout, order, s, hid, wd, scale, after, *outs):
    n = len(order)
    n_z, rows, width = outs[0].shape
    place = make_place()
    for z in range(n_z):
        at = (place.ahead(z) * 2 + (place.side ^ s)) * width
        at = pl.ds(pl.multiple_of(at, width), width)
        part = jnp.dot(hid[...], wd[:, at], preferred_element_type=jnp.float32)
        for r in range(n):
            value = part[r * rows : (r + 1) * rows] * scale[r * rows : (r + 1) * rows]
            outs[order[r]][z] = value.astype(jnp.bfloat16)


def down(make_place, layout, order, s, n_z, width, hid, w_down, scale, after):
    n = len(order)
    return call(
        lambda *refs: down_kernel(make_place, layout, order, s, *refs),
        [jax.ShapeDtypeStruct((n_z, layout.share, width), jnp.bfloat16)] * n,
        [VMEM] * 3 + [ANY],
        [VMEM] * n,
        "expert_down",
        8,
    )(hid, w_down, scale, after)


def group_steps(layout, scope, tables, grains):
    make_place, n_dp, n_bits, n_expert, half, reverse, to_partner = scope
    chosen, scale, w_gate, w_up, w_down = tables
    n_chip = 1 << n_bits
    plain = list(range(n_chip))
    after = yield
    modes, hop_wait = DIRECT[layout.group], HOP_WAIT[layout.group]
    terms = [[p] for p in pick(make_place, layout, n_chip, n_expert, chosen, grains, after)]
    if not PICK_WAIT[layout.group]:
        after = yield terms[0][0], None
    mine, after = yield from scatter(
        terms, n_dp, n_bits, modes[0], hop_wait[0], PICK_WAIT[layout.group], after
    )
    crossed = swap_planes(mine, n_expert, after)
    own_half = gather(crossed, n_dp, n_bits, modes[1])
    after = yield crossed, None
    own = stack(own_half, after)
    other = to_partner(own)
    after = yield own, None
    hid = hidden_units(make_place, reverse, own, other, w_gate, w_up, after)
    after = yield hid, None

    def downs(order, s):
        return down(
            make_place, layout, order, s, n_expert, half, hid, w_down, scale[layout.group], after
        )

    theirs = downs(reverse, 1)
    after = yield theirs[0], None
    mine = downs(plain, 0)
    after = yield mine[0], None
    terms = [[m, to_partner(t)] for m, t in zip(mine, theirs)]
    mine, after = yield from scatter(terms, n_dp, n_bits, modes[2], hop_wait[1], 0, after)
    crossed = swap_planes(mine, n_expert, after)
    yield crossed, gather(crossed, n_dp, n_bits, modes[3])


def body(
    context,
    out_weight,
    residual,
    gate_weight,
    up_weight,
    down_weight,
    gate_values,
    chosen_blocks,
    block_counts,
):
    n_expert = lax.axis_size("expert")
    n_dp = lax.axis_size("dp")
    n_bits = n_dp.bit_length() - 2
    n_chip = 1 << n_bits
    local_tokens, model_width = context.shape
    local_width = residual.shape[1]
    half = local_width // 2
    depth = out_weight.shape[0]
    local_blocks = local_tokens // BLK
    place = Place(n_bits, n_expert)
    side = place.side
    reverse = bit_reversed(n_bits)
    pair = pair_pairs(n_dp)

    def to_partner(value):
        return lax.ppermute(value, "dp", pair)

    def split_sides(value):
        own = lax.dynamic_slice_in_dim(value, side * half, half, axis=1)
        other = lax.dynamic_slice_in_dim(value, (1 - side) * half, half, axis=1)
        return own, to_partner(other)

    w_own, w_other = split_sides(out_weight)
    pieces = [(w_own, w_other)]
    for step in range(n_bits):
        pieces = pieces + [tuple(exchange(w, n_dp, step) for w in p) for p in pieces]
    pieces = [w for p in pieces for w in p]
    context_other = to_partner(context)
    residual_own, residual_other = split_sides(residual)
    w_gate, w_up, w_down = gate_weight[0], up_weight[0], down_weight[0]
    plain = list(range(n_chip))
    top = n_chip // 2
    share = CAP * BLK // GROUPS // n_chip

    def make_place():
        return Place(n_bits, n_expert)

    layouts = [Layout(group, n_chip, local_blocks) for group in range(GROUPS)]
    factors = scales(make_place, layouts, n_chip, block_counts, gate_values)
    last = n_chip - 1
    sides = (context, context_other)
    (total,) = project(make_place, plain[:top], None, *sides, pieces[: 2 * top], (), factors)
    total, columns = project(
        make_place, plain[top:last], last, *sides, pieces[2 * top : 2 * last], (total,), ()
    )
    attended = project_last(columns, total, residual_own, residual_other, pieces[2 * last :])

    grains = attended.reshape(-1, share, half)

    scope = (make_place, n_dp, n_bits, n_expert, half, reverse, to_partner)
    tables = (chosen_blocks, factors, w_gate, w_up, w_down)
    groups = [group_steps(layout, scope, tables, grains) for layout in layouts]
    for group in groups:
        next(group)
    after, received = None, [None] * GROUPS
    turn = 0
    while any(done is None for done in received):
        g = int(ORDER[turn]) if turn < len(ORDER) else turn % GROUPS
        turn += 1
        if received[g] is None:
            after, received[g] = groups[g].send(after)

    total, n = grains, grains.shape[0]
    for layout, got in zip(layouts[:-1], received[:-1]):
        total = finish(make_place, layout, n_chip, chosen_blocks, total, got, 0, n, False)
    last = (make_place, layouts[-1], n_chip, chosen_blocks, total, received[-1])
    other = finish(*last, n // 2, n, True)
    own = finish(*last, 0, n // 2, True)
    return join(make_place, own, to_partner(other), local_tokens)


def solution(mesh):
    in_specs = (
        P("dp", None),
        P("dp", "expert"),
        P("dp", "expert"),
        P("expert", None, "dp"),
        P("expert", None, "dp"),
        P("expert", "dp", None),
        P("expert", None),
        P(),
        P(),
    )
    out_specs = P("dp", "expert")
    return jax.shard_map(body, mesh=mesh, in_specs=in_specs, out_specs=out_specs, check_vma=False)
```
